32 devices in a mesh: ctx: 8 (over z, y), wt: 4 (over x, core).
Axes of the slice: x: 2, y: 2, z: 4, core: 2. Of those that a mesh axis runs over, the one named last changes fastest.
Arguments:
- tokens: bfloat16 [1024, 768], P('ctx'), may hold values from -6 to 6
- first_gain: float32 [768], replicated, may hold values from 0.1 to 1.9
- qkv_weight: bfloat16 [768, 3, 768], P(None, None, 'wt'), may hold values from -0.21875 to 0.21875
- attn_weight: bfloat16 [768, 768], P('wt'), as said below
- second_gain: float32 [768], replicated, may hold values from 0.1 to 1.9
- in_weight: bfloat16 [768, 2, 1152], P(None, None, 'wt'), may hold values from -0.21875 to 0.21875
- mlp_weight: bfloat16 [1152, 768], P('wt'), may hold values from -0.1875 to 0.1875
- cotangent: bfloat16 [1024, 768], P('ctx'), as said below
Outputs:
- output: bfloat16 [1024, 768], P('ctx')
- tokens_grad: bfloat16 [1024, 768], P('ctx')
- first_gain_grad: float32 [768], replicated
- qkv_weight_grad: float32 [768, 3, 768], P(None, None, 'wt')
- attn_weight_grad: float32 [768, 768], P('wt')
- second_gain_grad: float32 [768], replicated
- in_weight_grad: float32 [768, 2, 1152], P(None, None, 'wt')
- mlp_weight_grad: float32 [1152, 768], P('wt')
The draws below stay inside these ranges and needn't reach their ends.
Inputs may be any that keep to these rules, and one draw needn't show every extreme that they name: `attn_weight`: dense real entries, independent from element to element. `cotangent`: dense real entries of order one in every row.
All inputs are finite; a program needn't handle non-finite values.
Results may differ from the reference program's by a relative error of at most 0.025.
Values may be sent and summed in bfloat16 or wider, within the bound.
No kernel may reach another device: no remote copies, remote signals or barrier semaphores. Data moves between devices by JAX's collectives and lax.ppermute only.
A program may use at most 128 MiB of HBM per device.

```python
import jax
import jax.numpy as jnp
from jax import lax

D = 768
HEADS = 12
HEAD = 64
FF = 1152
TOKENS = 1024


def draw_attn_weight(key, part):
    key = jax.random.fold_in(key, 5)
    spread = (TOKENS / (3.0 * D)) ** 0.5
    values = jax.random.normal(key, (D, D), jnp.float32) * spread
    return values.astype(jnp.bfloat16)


def draw_cotangent(key, part):
    key = jax.random.fold_in(key, 9)
    ladder = jnp.arange(TOKENS).astype(jnp.float32) / TOKENS
    row_scale = 0.5 + ladder
    values = jnp.clip(jax.random.normal(key, (TOKENS, D), jnp.float32), -6.0, 6.0)
    return (values * row_scale[:, None]).astype(jnp.bfloat16)


def levels(stream_key, dims, pieces, smallest, largest):
    gain, own = 1.0, jax.random.fold_in(stream_key, 6)
    for position, shards_of in pieces:
        draws = jnp.exp(jax.random.uniform(jax.random.fold_in(own, position), (shards_of,), jnp.float32, smallest / len(pieces), largest / len(pieces)))
        gain = gain * jnp.repeat(draws, dims[position] // shards_of).reshape([-1 if axis == position else 1 for axis in range(len(dims))])
    return gain


def gaussian(key, extent, deviation, limit, pieces=(), held_as=jnp.bfloat16):
    values = deviation * jax.random.normal(key, extent, jnp.float32)
    if pieces:
        values = values * levels(key, extent, pieces, -0.22, 0.18)
    return jnp.clip(values, -limit, limit).astype(held_as)


def setup_inputs(seed: int = 0) -> dict:
    key_list = jax.random.split(jax.random.key(seed), 9)
    tokens = gaussian(key_list[0], (TOKENS, D), 1.0, 6.0, ((0, 8),))
    first_gain = jnp.clip(1.0 + 0.18 * jax.random.normal(key_list[1], (D,), jnp.float32), 0.1, 1.9)
    qkv_weight = gaussian(key_list[2], (D, 3, D), D ** -0.5, 0.21875, ((2, 4),))
    attn_weight = draw_attn_weight(jax.random.fold_in(key_list[8], 71), 0)
    second_gain = jnp.clip(1.0 + 0.18 * jax.random.normal(key_list[4], (D,), jnp.float32), 0.1, 1.9)
    in_weight = gaussian(key_list[5], (D, 2, FF), D ** -0.5, 0.21875, ((2, 4),))
    mlp_weight = gaussian(key_list[6], (FF, D), FF ** -0.5, 0.1875, ((0, 4),))
    cotangent = draw_cotangent(jax.random.fold_in(key_list[8], 71), 0)
    return {"tokens": tokens, "first_gain": first_gain, "qkv_weight": qkv_weight, "attn_weight": attn_weight, "second_gain": second_gain, "in_weight": in_weight, "mlp_weight": mlp_weight, "cotangent": cotangent}


rope_base = 160000.0
norm_epsilon = 1e-05
highest = lax.Precision.HIGHEST

@jax.custom_vjp
def low(v):
    return lax.optimization_barrier(v.astype(jnp.bfloat16)).astype(jnp.float32)

@jax.custom_vjp
def low_back(v):
    return v

def low_keep(v):
    return (low(v), None)

def low_pass(kept, grad):
    return (grad,)

def back_keep(v):
    return (v, None)

def back_low(kept, grad):
    return (low(grad),)
low.defvjp(low_keep, low_pass)
low_back.defvjp(back_keep, back_low)

def layer_norm(values):
    center = values - lax.optimization_barrier(jnp.mean(values, axis=-1, keepdims=True))
    return center * lax.rsqrt(lax.optimization_barrier(jnp.mean(center * center, axis=-1, keepdims=True)) + norm_epsilon)

def rotate(values, positions, direction):
    half_width = values.shape[-1] // 2
    frequency = rope_base ** (-(jnp.arange(half_width).astype(jnp.float32) * 2.0 / values.shape[-1]))
    angles = positions[:, None] * frequency[None, :]
    cosine_part = jnp.cos(angles)[:, None, :]
    sine_part = jnp.sin(angles)[:, None, :]
    lower_half = values[..., :half_width]
    upper_half = values[..., half_width:]
    return jnp.concatenate([lower_half * cosine_part - direction * upper_half * sine_part, upper_half * cosine_part + direction * lower_half * sine_part], axis=-1)

def attention(query_rows, key_rows, value_rows):
    block_size = min(512, TOKENS)
    score_scale = HEAD ** (-0.5)

    def one_block(query_block):
        scores = low_back(jnp.einsum('thd,shd->ths', query_block, key_rows, precision=highest) * score_scale)
        chances = jax.nn.softmax(scores, axis=-1)
        return jnp.einsum('ths,shd->thd', low(chances), value_rows, precision=highest)
    result = lax.map(jax.checkpoint(one_block), query_rows.reshape(TOKENS // block_size, block_size, HEADS, HEAD))
    return result.reshape(TOKENS, D)

def forward(inputs, first_gain, qkv_weight, attn_weight, second_gain, in_weight, mlp_weight):
    first_input = low(layer_norm(inputs) * first_gain)
    projected = jnp.einsum('td,dsh->tsh', first_input, qkv_weight, precision=highest)
    positions = jnp.arange(TOKENS).astype(jnp.float32)
    query_raw = low_back(projected[:, 0]).reshape(TOKENS, HEADS, HEAD)
    key_raw = low_back(projected[:, 1]).reshape(TOKENS, HEADS, HEAD)
    value_rows = low_back(low(projected[:, 2])).reshape(TOKENS, HEADS, HEAD)
    query_rows = low(rotate(query_raw, positions, 1.0))
    key_rows = low(rotate(key_raw, positions, 1.0))
    attended = low_back(low(attention(query_rows, key_rows, value_rows)))
    middle = inputs + low_back(jnp.dot(attended, attn_weight, precision=highest))
    second_input = low(layer_norm(middle) * second_gain)
    gate_up = low_back(jnp.einsum('td,dsf->tsf', second_input, in_weight, precision=highest))
    hidden = low(jax.nn.gelu(gate_up[:, 0], approximate=False) * gate_up[:, 1])
    return middle + low_back(jnp.dot(hidden, mlp_weight, precision=highest))

def reference(tokens, first_gain, qkv_weight, attn_weight, second_gain, in_weight, mlp_weight, cotangent):
    output, pull = jax.vjp(forward, tokens.astype(jnp.float32), first_gain, qkv_weight.astype(jnp.float32), attn_weight.astype(jnp.float32), second_gain, in_weight.astype(jnp.float32), mlp_weight.astype(jnp.float32))
    grads = pull(cotangent.astype(jnp.float32))
    return (output.astype(jnp.bfloat16), grads[0].astype(jnp.bfloat16), grads[1], grads[2], grads[3], grads[4], grads[5], grads[6])
```

```python
import functools

import jax
import jax.numpy as jnp
from jax import lax
from jax.experimental import pallas as pl
from jax.experimental.pallas import tpu as pltpu
from jax.sharding import PartitionSpec as P

HEAD = 64


rope_base = 160000.0
norm_epsilon = 1e-05


def layer_norm(values):
    center = values - jnp.mean(values, axis=-1, keepdims=True)
    return center * lax.rsqrt(jnp.mean(center * center, axis=-1, keepdims=True) + norm_epsilon)


def rotate(values, positions, direction):
    half_width = values.shape[-1] // 2
    frequency = rope_base ** (
        -(jnp.arange(half_width).astype(jnp.float32) * 2.0 / values.shape[-1])
    )
    angles = positions[:, None] * frequency[None, :]
    cosine_part = jnp.cos(angles)[:, None, :]
    sine_part = jnp.sin(angles)[:, None, :]
    lower_half = values[..., :half_width]
    upper_half = values[..., half_width:]
    return jnp.concatenate(
        [
            lower_half * cosine_part - direction * upper_half * sine_part,
            upper_half * cosine_part + direction * lower_half * sine_part,
        ],
        axis=-1,
    )


def block_size_for(shard_rows):
    candidate = shard_rows * max(1, 1024 // shard_rows)
    return candidate


def score_terms(
    query_block, grad_block, logsum_block, delta_block, key_block, value_block, score_scale
):
    scores = (
        jnp.einsum("thd,shd->ths", query_block, key_block, preferred_element_type=jnp.float32)
        * score_scale
    )
    chances = jnp.exp(scores - logsum_block[..., None])
    chance_grad = jnp.einsum(
        "thd,shd->ths", grad_block, value_block, preferred_element_type=jnp.float32
    )
    score_grad = (chances * (chance_grad - delta_block[..., None])).astype(jnp.bfloat16)
    return (chances.astype(jnp.bfloat16), score_grad)


def split_body(
    tokens, first_gain, qkv_weight, attn_weight, second_gain, in_weight, mlp_weight, cotangent
):
    row_count = tokens.shape[0]
    local_width = qkv_weight.shape[2]
    heads_here = local_width // HEAD
    score_scale = HEAD ** (-0.5)
    positions = (lax.axis_index("ctx") * row_count + jnp.arange(row_count, dtype=jnp.int32)).astype(
        jnp.float32
    )
    inputs = tokens.astype(jnp.float32)
    normed_first, first_pull = jax.vjp(layer_norm, inputs)
    first_input = (normed_first * first_gain).astype(jnp.bfloat16)
    projected = jnp.einsum(
        "td,dsh->tsh", first_input, qkv_weight, preferred_element_type=jnp.float32
    )
    shaped = projected.reshape(row_count, 3, heads_here, HEAD)
    query_rows = rotate(shaped[:, 0], positions, 1.0).astype(jnp.bfloat16)
    key_rows = rotate(shaped[:, 1], positions, 1.0).astype(jnp.bfloat16)
    value_rows = shaped[:, 2].astype(jnp.bfloat16)
    key_flat = key_rows.reshape(row_count, local_width)
    value_flat = value_rows.reshape(row_count, local_width)
    start_state = (
        jnp.full((row_count, heads_here), -1e30, jnp.float32),
        jnp.zeros((row_count, heads_here), jnp.float32),
        jnp.zeros((row_count, heads_here, HEAD), jnp.float32),
    )
    key_piece = lax.all_gather(key_flat, "ctx", axis=0, tiled=True)
    value_piece = lax.all_gather(value_flat, "ctx", axis=0, tiled=True)
    piece_rows = key_piece.shape[0]
    block_size = block_size_for(row_count)
    key_blocks = key_piece.reshape(piece_rows // block_size, block_size, heads_here, HEAD)
    value_blocks = value_piece.reshape(piece_rows // block_size, block_size, heads_here, HEAD)

    def forward_visit(state, block_item):
        running_max, running_sum, weighted = state
        key_block, value_block = block_item
        scores = (
            jnp.einsum("thd,shd->ths", query_rows, key_block, preferred_element_type=jnp.float32)
            * score_scale
        )
        new_max = jnp.maximum(running_max, jnp.max(scores, axis=-1))
        factor = jnp.exp(running_max - new_max)
        exponent = jnp.exp(scores - new_max[..., None])
        running_sum = running_sum * factor + jnp.sum(exponent, axis=-1)
        weighted = weighted * factor[..., None] + jnp.einsum(
            "ths,shd->thd",
            exponent.astype(jnp.bfloat16),
            value_block,
            preferred_element_type=jnp.float32,
        )
        return ((new_max, running_sum, weighted), None)

    result = lax.scan(forward_visit, start_state, (key_blocks, value_blocks))
    running_max, running_sum, weighted = result[0]
    attended_exact = weighted / running_sum[..., None]
    logsum = running_max + jnp.log(running_sum)
    attended = attended_exact.astype(jnp.bfloat16).reshape(row_count, local_width)
    branch = lax.psum(
        jnp.dot(attended, attn_weight, preferred_element_type=jnp.float32).astype(jnp.bfloat16),
        "wt",
    ).astype(jnp.float32)
    middle = inputs + branch
    normed_second, second_pull = jax.vjp(layer_norm, middle)
    second_input = (normed_second * second_gain).astype(jnp.bfloat16)
    gate_up = jnp.einsum("td,dsf->tsf", second_input, in_weight, preferred_element_type=jnp.float32)

    def activate(pair):
        return jax.nn.gelu(pair[:, 0], approximate=False) * pair[:, 1]

    hidden_exact, activate_back = jax.vjp(activate, gate_up)
    hidden = hidden_exact.astype(jnp.bfloat16)
    mlp_branch = lax.psum(
        jnp.dot(hidden, mlp_weight, preferred_element_type=jnp.float32).astype(jnp.bfloat16), "wt"
    ).astype(jnp.float32)
    output = (middle + mlp_branch).astype(jnp.bfloat16)
    hidden_grad = jnp.einsum("td,fd->tf", cotangent, mlp_weight, preferred_element_type=jnp.float32)
    mlp_weight_grad = jnp.einsum("tf,td->fd", hidden, cotangent, preferred_element_type=jnp.float32)
    gate_up_grad = activate_back(hidden_grad)[0].astype(jnp.bfloat16)
    second_part = jnp.einsum(
        "tsf,dsf->td", gate_up_grad, in_weight, preferred_element_type=jnp.float32
    )
    in_weight_grad = jnp.einsum(
        "td,tsf->dsf", second_input, gate_up_grad, preferred_element_type=jnp.float32
    )
    second_grad = lax.psum(second_part.astype(jnp.bfloat16), "wt").astype(jnp.float32)
    second_gain_grad = jnp.sum(second_grad * normed_second, axis=0)
    middle_grad = cotangent.astype(jnp.float32) + second_pull(second_grad * second_gain)[0]
    branch_grad = middle_grad.astype(jnp.bfloat16)
    attended_grad = jnp.einsum(
        "td,hd->th", branch_grad, attn_weight, preferred_element_type=jnp.float32
    )
    attn_weight_grad = jnp.einsum(
        "th,td->hd", attended, branch_grad, preferred_element_type=jnp.float32
    )
    grad_rows = attended_grad.astype(jnp.bfloat16).reshape(row_count, heads_here, HEAD)
    row_delta = jnp.sum(grad_rows.astype(jnp.float32) * attended_exact, axis=-1)
    zero_rows = jnp.zeros((row_count, heads_here, HEAD), jnp.float32)
    query_acc = zero_rows
    key_piece = lax.all_gather(key_flat, "ctx", axis=0, tiled=True)
    value_piece = lax.all_gather(value_flat, "ctx", axis=0, tiled=True)
    piece_rows = key_piece.shape[0]
    block_size = block_size_for(row_count)
    key_blocks = key_piece.reshape(piece_rows // block_size, block_size, heads_here, HEAD)
    value_blocks = value_piece.reshape(piece_rows // block_size, block_size, heads_here, HEAD)

    def backward_visit(partial_value, block_item):
        key_block, value_block = block_item
        chance_low, score_grad = score_terms(
            query_rows, grad_rows, logsum, row_delta, key_block, value_block, score_scale
        )
        partial_value = (
            partial_value
            + jnp.einsum("ths,shd->thd", score_grad, key_block, preferred_element_type=jnp.float32)
            * score_scale
        )
        key_term = (
            jnp.einsum("ths,thd->shd", score_grad, query_rows, preferred_element_type=jnp.float32)
            * score_scale
        )
        value_term = jnp.einsum(
            "ths,thd->shd", chance_low, grad_rows, preferred_element_type=jnp.float32
        )
        return (partial_value, (key_term, value_term))

    query_acc, terms = lax.scan(backward_visit, query_acc, (key_blocks, value_blocks))
    key_total = terms[0].reshape(piece_rows, local_width)
    value_total = terms[1].reshape(piece_rows, local_width)
    key_sum, value_sum = (
        lax.psum_scatter(key_total, "ctx", scatter_dimension=0, tiled=True),
        lax.psum_scatter(value_total, "ctx", scatter_dimension=0, tiled=True),
    )
    key_grad = key_sum.reshape(row_count, heads_here, HEAD)
    value_grad = value_sum.reshape(row_count, heads_here, HEAD)
    query_back = rotate(query_acc, positions, -1.0)
    key_back = rotate(key_grad, positions, -1.0)
    projected_grad = (
        jnp.stack([query_back, key_back, value_grad], axis=1)
        .reshape(row_count, 3, local_width)
        .astype(jnp.bfloat16)
    )
    first_part = jnp.einsum(
        "tsh,dsh->td", projected_grad, qkv_weight, preferred_element_type=jnp.float32
    )
    qkv_weight_grad = jnp.einsum(
        "td,tsh->dsh", first_input, projected_grad, preferred_element_type=jnp.float32
    )
    first_grad = lax.psum(first_part.astype(jnp.bfloat16), "wt").astype(jnp.float32)
    first_gain_grad = jnp.sum(first_grad * normed_first, axis=0)
    tokens_grad = (middle_grad + first_pull(first_grad * first_gain)[0]).astype(jnp.bfloat16)
    summed = lax.psum(
        (
            first_gain_grad,
            qkv_weight_grad,
            attn_weight_grad,
            second_gain_grad,
            in_weight_grad,
            mlp_weight_grad,
        ),
        "ctx",
    )
    return (output, tokens_grad, summed[0], summed[1], summed[2], summed[3], summed[4], summed[5])


F32 = jnp.float32
BF16 = jnp.bfloat16
NT = (((1,), (1,)), ((), ()))
TN = (((0,), (0,)), ((), ()))
REPLICATED_TOKENS = 2048


def mm(a, b, dims=(((1,), (0,)), ((), ()))):
    return lax.dot_general(a, b, dims, preferred_element_type=F32)


def norm_parts(values):
    center = values - jnp.mean(values, axis=-1, keepdims=True)
    scale = lax.rsqrt(jnp.mean(center * center, axis=-1, keepdims=True) + norm_epsilon)
    return center * scale, scale


def norm_back(grad, normed, scale):
    mean_grad = jnp.mean(grad, axis=-1, keepdims=True)
    mean_both = jnp.mean(grad * normed, axis=-1, keepdims=True)
    return scale * (grad - mean_grad - normed * mean_both)


def call(kernel, outs, args, scratch=(), flops=0, cells=0):
    in_specs = [
        pl.BlockSpec(memory_space=pltpu.SMEM if a.dtype == jnp.int32 else pltpu.VMEM) for a in args
    ]
    moved = sum(a.size * a.dtype.itemsize for a in args) + sum(
        o.size * o.dtype.itemsize for o in outs
    )
    return pl.pallas_call(
        kernel,
        out_shape=outs,
        in_specs=in_specs,
        out_specs=[pl.BlockSpec(memory_space=pltpu.VMEM)] * len(outs),
        scratch_shapes=list(scratch),
        compiler_params=pltpu.CompilerParams(vmem_limit_bytes=40 * 1024 * 1024),
        cost_estimate=pl.CostEstimate(flops=flops, bytes_accessed=moved, transcendentals=cells),
    )(*args)


def attention_kernel(
    heads,
    place,
    mine,
    other,
    gain,
    weight,
    cosine,
    sine,
    tok_ref,
    first_ref,
    qkv_ref,
    att_ref,
    lse_ref,
):
    here, core = place[0], place[1]
    blocks, half, width = mine.shape
    rows = 2 * half
    tokens = blocks * rows
    local = heads * HEAD

    def norm_block(b, carry):
        source = jnp.bitwise_xor(b, here)
        own, far = mine[source], other[source]
        low = core == 0
        block = jnp.concatenate(
            [jnp.where(low, own, far), jnp.where(low, far, own)], axis=0
        )
        at = pl.ds(pl.multiple_of(b * rows, rows), rows)
        tok_ref[at, :] = block
        normed, _ = norm_parts(block.astype(F32))
        first_ref[at, :] = (normed * gain[...]).astype(BF16)
        return carry

    lax.fori_loop(0, blocks, norm_block, 0)
    chunk = 256
    for start in range(0, tokens, chunk):
        at = slice(start, start + chunk)
        raw = mm(weight[...], first_ref[at, :], NT)
        cos, sin = cosine[:, at], sine[:, at]
        for part in range(2):
            for head in range(heads):
                base = part * local + head * HEAD
                lower = raw[base : base + HEAD // 2]
                upper = raw[base + HEAD // 2 : base + HEAD]
                turned = jnp.concatenate(
                    [lower * cos - upper * sin, upper * cos + lower * sin], axis=0
                ).astype(BF16)
                if part == 0:
                    turned = turned * jnp.asarray(HEAD ** (-0.5), BF16)
                qkv_ref[base : base + HEAD, at] = turned
        qkv_ref[2 * local :, at] = raw[2 * local :].astype(BF16)
    lse_ref[...] = jnp.zeros_like(lse_ref)
    for head in range(heads):
        base = head * HEAD
        keys = qkv_ref[local + base : local + base + HEAD, :].T
        values = qkv_ref[2 * local + base : 2 * local + base + HEAD, :]
        for start in range(0, tokens, chunk):
            at = slice(start, start + chunk)
            scores = mm(keys, qkv_ref[base : base + HEAD, at])
            top = jnp.max(scores, axis=0, keepdims=True)
            exponent = jnp.exp(scores - top)
            total = jnp.sum(exponent, axis=0, keepdims=True)
            weighted = mm(values, exponent.astype(BF16))
            att_ref[base : base + HEAD, at] = (weighted / total).astype(BF16)
            lse_ref[head : head + 1, at] = top + jnp.log(total)


def cdf_terms(gate):
    half = 0.5 * (1.0 + lax.erf(gate * (0.5**0.5)))
    slope = half + gate * (jnp.exp(-0.5 * gate * gate) * 0.3989422804014327)
    return half, slope


def mlp_kernel(
    place,
    tok,
    att,
    attn_weight,
    gain,
    in_weight,
    mlp_weight,
    cot,
    middle_ref,
    second_ref,
    part_ref,
    hidden_ref,
    gate_ref,
    out_ref,
    all_hidden,
    all_att,
):
    here, quarter, side = place[0], place[2], place[3]
    tokens, width = tok.shape
    parts, local, _ = att.shape
    sides, units, _ = mlp_weight.shape
    for p in range(parts):
        all_att[p * local : (p + 1) * local, :] = att[jnp.bitwise_xor(quarter, p)]
    chunk = 256
    for start in range(0, tokens, chunk):
        at = slice(start, start + chunk)
        attended = all_att[:, at].T
        middle = tok[at, :].astype(F32)
        branch = mm(attended[:, :local], attn_weight[quarter])
        for p in range(1, parts):
            branch += mm(
                attended[:, p * local : (p + 1) * local], attn_weight[jnp.bitwise_xor(quarter, p)]
            )
        middle = middle + branch
        middle_ref[at, :] = middle
        normed, _ = norm_parts(middle)
        second = (normed * gain[...]).astype(BF16)
        second_ref[at, :] = second
        cot_rows = cot[at, :]
        total = None
        for p in range(sides):
            r = jnp.bitwise_xor(side, p)
            gate_up = mm(in_weight[r], second, NT)
            gate, up = gate_up[:units], gate_up[units:]
            half, slope = cdf_terms(gate)
            active = gate * half
            all_hidden[r, :, at] = (active * up).astype(BF16)
            back = mm(mlp_weight[r], cot_rows, NT)
            grads = jnp.concatenate([slope * up * back, active * back], axis=0).astype(BF16)
            gate_ref[r, :, at] = grads
            piece = mm(grads.T, in_weight[r])
            total = piece if total is None else total + piece
        part_ref[at, :] = total.astype(BF16)
    rows = out_ref.shape[0]
    own = pl.ds(pl.multiple_of(here * rows, rows), rows)
    total = None
    for p in range(sides):
        r = jnp.bitwise_xor(side, p)
        piece = mm(all_hidden[r, :, own].T, mlp_weight[r])
        total = piece if total is None else total + piece
    out_ref[...] = total.astype(BF16)
    hidden_ref[...] = all_hidden[0]


def back_kernel(
    heads,
    place,
    middle,
    part_a,
    part_b,
    cot,
    gain,
    attn_weight,
    qkv,
    lse,
    weight,
    cosine,
    sine,
    gain_ref,
    branch_ref,
    own_ref,
    grad_ref,
    first_ref,
    back_rows,
):
    here = place[0]
    tokens, width = middle.shape
    rows = own_ref.shape[0]
    local = heads * HEAD
    gain_ref[...] = jnp.zeros_like(gain_ref)

    def norm_block(b, carry):
        at = pl.ds(pl.multiple_of(b * rows, rows), rows)
        second = part_a[at, :].astype(F32) + part_b[at, :].astype(F32)
        normed, scale = norm_parts(middle[at, :])
        gain_ref[...] += jnp.sum(second * normed, axis=0, keepdims=True)
        grad = cot[at, :].astype(F32) + norm_back(second * gain[...], normed, scale)
        branch_ref[at, :] = grad.astype(BF16)

        @pl.when(b == here)
        def _():
            own_ref[...] = grad

        return carry

    lax.fori_loop(0, tokens // rows, norm_block, 0)
    chunk = 256
    for start in range(0, tokens, chunk):
        at = slice(start, start + chunk)
        back_rows[:, at] = mm(attn_weight[...], branch_ref[at, :], NT).astype(BF16)
    scale = HEAD ** (-0.5)
    for head in range(heads):
        base = head * HEAD
        keys_t = qkv[local + base : local + base + HEAD, :]
        keys = keys_t.T
        values = qkv[2 * local + base : 2 * local + base + HEAD, :].T
        key_grad = jnp.zeros((tokens, HEAD), F32)
        value_grad = jnp.zeros((tokens, HEAD), F32)
        for start in range(0, tokens, chunk):
            at = slice(start, start + chunk)
            query = qkv[base : base + HEAD, at]
            out_grad = back_rows[base : base + HEAD, at]
            chances = jnp.exp(mm(keys, query) - lse[head : head + 1, at])
            chance_grad = mm(values, out_grad)
            delta = jnp.sum(chances * chance_grad, axis=0, keepdims=True)
            score_grad = (chances * (chance_grad - delta)).astype(BF16)
            query_grad = mm(keys_t, score_grad) * scale
            key_grad += mm(score_grad, query.T)
            value_grad += mm(chances.astype(BF16), out_grad.T)
            cos, sin = cosine[:, at], sine[:, at]
            lower, upper = query_grad[: HEAD // 2], query_grad[HEAD // 2 :]
            grad_ref[base : base + HEAD, at] = jnp.concatenate(
                [lower * cos + upper * sin, upper * cos - lower * sin], axis=0
            ).astype(BF16)
        turned = key_grad.T
        lower, upper = turned[: HEAD // 2], turned[HEAD // 2 :]
        cos, sin = cosine[...], sine[...]
        grad_ref[local + base : local + base + HEAD, :] = jnp.concatenate(
            [lower * cos + upper * sin, upper * cos - lower * sin], axis=0
        ).astype(BF16)
        grad_ref[2 * local + base : 2 * local + base + HEAD, :] = value_grad.T.astype(BF16)
    own = pl.ds(pl.multiple_of(here * rows, rows), rows)
    first_ref[...] = mm(grad_ref[:, own].T, weight[...]).astype(BF16)


def gather_halves(rows_here, core, spots):
    rows, width = rows_here.shape
    half = lax.dynamic_slice_in_dim(rows_here, core * (rows // 2), rows // 2, axis=0)
    pieces = [half]
    for step in range(1, spots):
        pieces.append(
            lax.ppermute(half, "ctx", [(spot, spot ^ step) for spot in range(spots)])
        )
    mine = jnp.stack(pieces)
    return mine, swap(mine, 1)


def swap(value, mask):
    return lax.ppermute(value, "wt", [(spot, spot ^ mask) for spot in range(4)])


def replicated_body(
    spots,
    tokens,
    first_gain,
    qkv_weight,
    attn_weight,
    second_gain,
    in_weight,
    mlp_weight,
    cotangent,
):
    rows, width = tokens.shape
    total_rows = rows * spots
    local = qkv_weight.shape[2]
    heads = local // HEAD
    units = mlp_weight.shape[0]
    here, quarter = lax.axis_index("ctx"), lax.axis_index("wt")
    core, side = quarter % 2, quarter // 2
    place = jnp.stack([here, core, quarter, side]).astype(jnp.int32)
    frequency = rope_base ** (-(jnp.arange(HEAD // 2).astype(F32) * 2.0 / HEAD))
    angles = frequency[:, None] * jnp.arange(total_rows).astype(F32)[None, :]
    cosine, sine = jnp.cos(angles), jnp.sin(angles)
    qkv_t = jnp.transpose(qkv_weight, (1, 2, 0)).reshape(3 * local, width)
    in_t = jnp.transpose(in_weight, (1, 2, 0)).reshape(2 * units, width)

    mine, other = gather_halves(tokens, core, spots)
    attn_pair = jnp.stack([attn_weight, swap(attn_weight, 2)])
    in_pair = jnp.stack([in_t, swap(in_t, 2)])
    mlp_pair = jnp.stack([mlp_weight, swap(mlp_weight, 2)])
    attn_far = swap(attn_pair, 1)
    attn_all = jnp.stack([attn_pair[0], attn_far[0], attn_pair[1], attn_far[1]])

    tok_all, first_input, qkv, att, lse = call(
        functools.partial(attention_kernel, heads),
        [
            jax.ShapeDtypeStruct((total_rows, width), BF16),
            jax.ShapeDtypeStruct((total_rows, width), BF16),
            jax.ShapeDtypeStruct((3 * local, total_rows), BF16),
            jax.ShapeDtypeStruct((local, total_rows), BF16),
            jax.ShapeDtypeStruct((8, total_rows), F32),
        ],
        [place, mine, other, first_gain[None, :], qkv_t, cosine, sine],
        flops=2 * total_rows * local * (3 * width + 8 * total_rows),
        cells=heads * total_rows * total_rows,
    )
    cotangent, _ = lax.optimization_barrier((cotangent, mine))
    cot_mine, cot_other = gather_halves(cotangent, core, spots)
    cot_low = jnp.where(core == 0, cot_mine, cot_other)
    cot_high = jnp.where(core == 0, cot_other, cot_mine)
    cot_xor = jnp.stack([cot_low, cot_high], axis=1).reshape(spots, rows, width)
    cot_all = jnp.concatenate(
        [lax.dynamic_index_in_dim(cot_xor, here ^ b, 0, keepdims=False) for b in range(spots)], 0
    )

    att_pair = jnp.stack([att, swap(att, 2)])
    att_far = swap(att_pair, 1)
    att_all = jnp.stack([att_pair[0], att_far[0], att_pair[1], att_far[1]])
    middle, second_input, second_part, hidden, gate_grad, out_part = call(
        mlp_kernel,
        [
            jax.ShapeDtypeStruct((total_rows, width), F32),
            jax.ShapeDtypeStruct((total_rows, width), BF16),
            jax.ShapeDtypeStruct((total_rows, width), BF16),
            jax.ShapeDtypeStruct((units, total_rows), BF16),
            jax.ShapeDtypeStruct((2, 2 * units, total_rows), BF16),
            jax.ShapeDtypeStruct((rows, width), BF16),
        ],
        [place, tok_all, att_all, attn_all, second_gain[None, :], in_pair, mlp_pair, cot_all],
        scratch=[
            pltpu.VMEM((2, units, total_rows), BF16),
            pltpu.VMEM((4 * local, total_rows), BF16),
        ],
        flops=2 * total_rows * width * (4 * local + 10 * units),
        cells=4 * units * total_rows,
    )
    second_far = swap(second_part, 1)
    out_far = swap(out_part, 1)

    second_gain_grad, branch_grad, middle_grad, grad_t, first_part = call(
        functools.partial(back_kernel, heads),
        [
            jax.ShapeDtypeStruct((1, width), F32),
            jax.ShapeDtypeStruct((total_rows, width), BF16),
            jax.ShapeDtypeStruct((rows, width), F32),
            jax.ShapeDtypeStruct((3 * local, total_rows), BF16),
            jax.ShapeDtypeStruct((rows, width), BF16),
        ],
        [
            place,
            middle,
            second_part,
            second_far,
            cot_all,
            second_gain[None, :],
            attn_weight,
            qkv,
            lse,
            qkv_t,
            cosine,
            sine,
        ],
        scratch=[pltpu.VMEM((local, total_rows), BF16)],
        flops=2 * total_rows * local * (width + 20 * total_rows),
        cells=heads * total_rows * total_rows,
    )
    qkv_grad = mm(grad_t, first_input)
    gain_part = jnp.sum(qkv_t.astype(F32) * qkv_grad, axis=0) / first_gain
    gain_high = gain_part.astype(BF16)
    gain_low = (gain_part - gain_high.astype(F32)).astype(BF16)
    gain_rows = jnp.concatenate([gain_high[None], gain_low[None], jnp.zeros((14, width), BF16)], 0)
    message = jnp.concatenate([first_part, gain_rows], 0)
    pair = message.astype(F32) + swap(message, 1).astype(F32)
    pair_low = pair.astype(BF16)
    gain_pair = pair[rows] + pair[rows + 1]
    gain_top = gain_pair.astype(BF16)
    gain_rest = (gain_pair - gain_top.astype(F32)).astype(BF16)
    across = jnp.concatenate([pair_low[:rows], gain_top[None], gain_rest[None], pair_low[rows + 2 :]], 0)
    far = swap(across, 2)
    first_sum = across.astype(F32) + far.astype(F32)
    first_gain_grad = first_sum[rows] + first_sum[rows + 1]
    first_grad = first_sum[:rows]

    attn_grad = mm(att, branch_grad)
    in_grad = mm(gate_grad[0], second_input)
    mlp_grad = mm(hidden, cot_all)
    own_middle = lax.dynamic_slice_in_dim(middle, here * rows, rows, axis=0)
    output = (own_middle + (out_part.astype(F32) + out_far.astype(F32))).astype(BF16)
    normed, scale = norm_parts(tokens.astype(F32))
    tokens_grad = (middle_grad + norm_back(first_grad * first_gain, normed, scale)).astype(BF16)
    return (
        output,
        tokens_grad,
        first_gain_grad,
        jnp.transpose(qkv_grad.reshape(3, local, width), (2, 0, 1)),
        attn_grad,
        second_gain_grad[0],
        jnp.transpose(in_grad.reshape(2, units, width), (2, 0, 1)),
        mlp_grad,
    )


def body(sizes, tokens, *rest):
    spots, lanes = sizes["ctx"], sizes["wt"]
    rows = tokens.shape[0]
    small = spots * rows <= REPLICATED_TOKENS and rows % 128 == 0 and (spots * rows) % 256 == 0
    if small and lanes == 4 and spots & (spots - 1) == 0:
        return replicated_body(spots, tokens, *rest)
    return split_body(tokens, *rest)


def solution(mesh):
    return jax.shard_map(
        functools.partial(body, dict(mesh.shape)),
        mesh=mesh,
        in_specs=(
            P("ctx", None),
            P(),
            P(None, None, "wt"),
            P("wt", None),
            P(),
            P(None, None, "wt"),
            P("wt", None),
            P("ctx", None),
        ),
        out_specs=(
            P("ctx", None),
            P("ctx", None),
            P(),
            P(None, None, "wt"),
            P("wt", None),
            P(),
            P(None, None, "wt"),
            P("wt", None),
        ),
        check_vma=False,
    )
```

```python
import functools

import jax
import jax.numpy as jnp
from jax import lax
from jax.experimental import pallas as pl
from jax.experimental.pallas import tpu as pltpu
from jax.sharding import PartitionSpec as P

HEAD = 64


rope_base = 160000.0
norm_epsilon = 1e-05


def layer_norm(values):
    center = values - jnp.mean(values, axis=-1, keepdims=True)
    return center * lax.rsqrt(jnp.mean(center * center, axis=-1, keepdims=True) + norm_epsilon)


def rotate(values, positions, direction):
    half_width = values.shape[-1] // 2
    frequency = rope_base ** (
        -(jnp.arange(half_width).astype(jnp.float32) * 2.0 / values.shape[-1])
    )
    angles = positions[:, None] * frequency[None, :]
    cosine_part = jnp.cos(angles)[:, None, :]
    sine_part = jnp.sin(angles)[:, None, :]
    lower_half = values[..., :half_width]
    upper_half = values[..., half_width:]
    return jnp.concatenate(
        [
            lower_half * cosine_part - direction * upper_half * sine_part,
            upper_half * cosine_part + direction * lower_half * sine_part,
        ],
        axis=-1,
    )


def block_size_for(shard_rows):
    candidate = shard_rows * max(1, 1024 // shard_rows)
    return candidate


def score_terms(
    query_block, grad_block, logsum_block, delta_block, key_block, value_block, score_scale
):
    scores = (
        jnp.einsum("thd,shd->ths", query_block, key_block, preferred_element_type=jnp.float32)
        * score_scale
    )
    chances = jnp.exp(scores - logsum_block[..., None])
    chance_grad = jnp.einsum(
        "thd,shd->ths", grad_block, value_block, preferred_element_type=jnp.float32
    )
    score_grad = (chances * (chance_grad - delta_block[..., None])).astype(jnp.bfloat16)
    return (chances.astype(jnp.bfloat16), score_grad)


def split_body(
    tokens, first_gain, qkv_weight, attn_weight, second_gain, in_weight, mlp_weight, cotangent
):
    row_count = tokens.shape[0]
    local_width = qkv_weight.shape[2]
    heads_here = local_width // HEAD
    score_scale = HEAD ** (-0.5)
    positions = (lax.axis_index("ctx") * row_count + jnp.arange(row_count, dtype=jnp.int32)).astype(
        jnp.float32
    )
    inputs = tokens.astype(jnp.float32)
    normed_first, first_pull = jax.vjp(layer_norm, inputs)
    first_input = (normed_first * first_gain).astype(jnp.bfloat16)
    projected = jnp.einsum(
        "td,dsh->tsh", first_input, qkv_weight, preferred_element_type=jnp.float32
    )
    shaped = projected.reshape(row_count, 3, heads_here, HEAD)
    query_rows = rotate(shaped[:, 0], positions, 1.0).astype(jnp.bfloat16)
    key_rows = rotate(shaped[:, 1], positions, 1.0).astype(jnp.bfloat16)
    value_rows = shaped[:, 2].astype(jnp.bfloat16)
    key_flat = key_rows.reshape(row_count, local_width)
    value_flat = value_rows.reshape(row_count, local_width)
    start_state = (
        jnp.full((row_count, heads_here), -1e30, jnp.float32),
        jnp.zeros((row_count, heads_here), jnp.float32),
        jnp.zeros((row_count, heads_here, HEAD), jnp.float32),
    )
    key_piece = lax.all_gather(key_flat, "ctx", axis=0, tiled=True)
    value_piece = lax.all_gather(value_flat, "ctx", axis=0, tiled=True)
    piece_rows = key_piece.shape[0]
    block_size = block_size_for(row_count)
    key_blocks = key_piece.reshape(piece_rows // block_size, block_size, heads_here, HEAD)
    value_blocks = value_piece.reshape(piece_rows // block_size, block_size, heads_here, HEAD)

    def forward_visit(state, block_item):
        running_max, running_sum, weighted = state
        key_block, value_block = block_item
        scores = (
            jnp.einsum("thd,shd->ths", query_rows, key_block, preferred_element_type=jnp.float32)
            * score_scale
        )
        new_max = jnp.maximum(running_max, jnp.max(scores, axis=-1))
        factor = jnp.exp(running_max - new_max)
        exponent = jnp.exp(scores - new_max[..., None])
        running_sum = running_sum * factor + jnp.sum(exponent, axis=-1)
        weighted = weighted * factor[..., None] + jnp.einsum(
            "ths,shd->thd",
            exponent.astype(jnp.bfloat16),
            value_block,
            preferred_element_type=jnp.float32,
        )
        return ((new_max, running_sum, weighted), None)

    result = lax.scan(forward_visit, start_state, (key_blocks, value_blocks))
    running_max, running_sum, weighted = result[0]
    attended_exact = weighted / running_sum[..., None]
    logsum = running_max + jnp.log(running_sum)
    attended = attended_exact.astype(jnp.bfloat16).reshape(row_count, local_width)
    branch = lax.psum(
        jnp.dot(attended, attn_weight, preferred_element_type=jnp.float32).astype(jnp.bfloat16),
        "wt",
    ).astype(jnp.float32)
    middle = inputs + branch
    normed_second, second_pull = jax.vjp(layer_norm, middle)
    second_input = (normed_second * second_gain).astype(jnp.bfloat16)
    gate_up = jnp.einsum("td,dsf->tsf", second_input, in_weight, preferred_element_type=jnp.float32)

    def activate(pair):
        return jax.nn.gelu(pair[:, 0], approximate=False) * pair[:, 1]

    hidden_exact, activate_back = jax.vjp(activate, gate_up)
    hidden = hidden_exact.astype(jnp.bfloat16)
    mlp_branch = lax.psum(
        jnp.dot(hidden, mlp_weight, preferred_element_type=jnp.float32).astype(jnp.bfloat16), "wt"
    ).astype(jnp.float32)
    output = (middle + mlp_branch).astype(jnp.bfloat16)
    hidden_grad = jnp.einsum("td,fd->tf", cotangent, mlp_weight, preferred_element_type=jnp.float32)
    mlp_weight_grad = jnp.einsum("tf,td->fd", hidden, cotangent, preferred_element_type=jnp.float32)
    gate_up_grad = activate_back(hidden_grad)[0].astype(jnp.bfloat16)
    second_part = jnp.einsum(
        "tsf,dsf->td", gate_up_grad, in_weight, preferred_element_type=jnp.float32
    )
    in_weight_grad = jnp.einsum(
        "td,tsf->dsf", second_input, gate_up_grad, preferred_element_type=jnp.float32
    )
    second_grad = lax.psum(second_part.astype(jnp.bfloat16), "wt").astype(jnp.float32)
    second_gain_grad = jnp.sum(second_grad * normed_second, axis=0)
    middle_grad = cotangent.astype(jnp.float32) + second_pull(second_grad * second_gain)[0]
    branch_grad = middle_grad.astype(jnp.bfloat16)
    attended_grad = jnp.einsum(
        "td,hd->th", branch_grad, attn_weight, preferred_element_type=jnp.float32
    )
    attn_weight_grad = jnp.einsum(
        "th,td->hd", attended, branch_grad, preferred_element_type=jnp.float32
    )
    grad_rows = attended_grad.astype(jnp.bfloat16).reshape(row_count, heads_here, HEAD)
    row_delta = jnp.sum(grad_rows.astype(jnp.float32) * attended_exact, axis=-1)
    zero_rows = jnp.zeros((row_count, heads_here, HEAD), jnp.float32)
    query_acc = zero_rows
    key_piece = lax.all_gather(key_flat, "ctx", axis=0, tiled=True)
    value_piece = lax.all_gather(value_flat, "ctx", axis=0, tiled=True)
    piece_rows = key_piece.shape[0]
    block_size = block_size_for(row_count)
    key_blocks = key_piece.reshape(piece_rows // block_size, block_size, heads_here, HEAD)
    value_blocks = value_piece.reshape(piece_rows // block_size, block_size, heads_here, HEAD)

    def backward_visit(partial_value, block_item):
        key_block, value_block = block_item
        chance_low, score_grad = score_terms(
            query_rows, grad_rows, logsum, row_delta, key_block, value_block, score_scale
        )
        partial_value = (
            partial_value
            + jnp.einsum("ths,shd->thd", score_grad, key_block, preferred_element_type=jnp.float32)
            * score_scale
        )
        key_term = (
            jnp.einsum("ths,thd->shd", score_grad, query_rows, preferred_element_type=jnp.float32)
            * score_scale
        )
        value_term = jnp.einsum(
            "ths,thd->shd", chance_low, grad_rows, preferred_element_type=jnp.float32
        )
        return (partial_value, (key_term, value_term))

    query_acc, terms = lax.scan(backward_visit, query_acc, (key_blocks, value_blocks))
    key_total = terms[0].reshape(piece_rows, local_width)
    value_total = terms[1].reshape(piece_rows, local_width)
    key_sum, value_sum = (
        lax.psum_scatter(key_total, "ctx", scatter_dimension=0, tiled=True),
        lax.psum_scatter(value_total, "ctx", scatter_dimension=0, tiled=True),
    )
    key_grad = key_sum.reshape(row_count, heads_here, HEAD)
    value_grad = value_sum.reshape(row_count, heads_here, HEAD)
    query_back = rotate(query_acc, positions, -1.0)
    key_back = rotate(key_grad, positions, -1.0)
    projected_grad = (
        jnp.stack([query_back, key_back, value_grad], axis=1)
        .reshape(row_count, 3, local_width)
        .astype(jnp.bfloat16)
    )
    first_part = jnp.einsum(
        "tsh,dsh->td", projected_grad, qkv_weight, preferred_element_type=jnp.float32
    )
    qkv_weight_grad = jnp.einsum(
        "td,tsh->dsh", first_input, projected_grad, preferred_element_type=jnp.float32
    )
    first_grad = lax.psum(first_part.astype(jnp.bfloat16), "wt").astype(jnp.float32)
    first_gain_grad = jnp.sum(first_grad * normed_first, axis=0)
    tokens_grad = (middle_grad + first_pull(first_grad * first_gain)[0]).astype(jnp.bfloat16)
    summed = lax.psum(
        (
            first_gain_grad,
            qkv_weight_grad,
            attn_weight_grad,
            second_gain_grad,
            in_weight_grad,
            mlp_weight_grad,
        ),
        "ctx",
    )
    return (output, tokens_grad, summed[0], summed[1], summed[2], summed[3], summed[4], summed[5])


F32 = jnp.float32
BF16 = jnp.bfloat16
NT = (((1,), (1,)), ((), ()))
TN = (((0,), (0,)), ((), ()))
REPLICATED_TOKENS = 2048


def mm(a, b, dims=(((1,), (0,)), ((), ()))):
    return lax.dot_general(a, b, dims, preferred_element_type=F32)


def norm_parts(values):
    center = values - jnp.mean(values, axis=-1, keepdims=True)
    scale = lax.rsqrt(jnp.mean(center * center, axis=-1, keepdims=True) + norm_epsilon)
    return center * scale, scale


def norm_back(grad, normed, scale):
    mean_grad = jnp.mean(grad, axis=-1, keepdims=True)
    mean_both = jnp.mean(grad * normed, axis=-1, keepdims=True)
    return scale * (grad - mean_grad - normed * mean_both)


def fast(shape, dtype):
    return pltpu.VMEM(shape, dtype)


class Away:
    def __init__(self, value):
        self.value = value


def call(kernel, outs, args, scratch=(), copies=0, flops=0, cells=0, room=16):
    in_specs, values = [], []
    for arg in args:
        value = arg.value if isinstance(arg, Away) else arg
        if value.dtype == jnp.int32:
            in_specs.append(pl.BlockSpec(memory_space=pltpu.SMEM))
            values.append(value)
            continue
        space = pltpu.HBM if isinstance(arg, Away) else pltpu.VMEM
        in_specs.append(pl.BlockSpec(memory_space=space))
        values.append(pltpu.with_memory_space_constraint(value, space))
    out_specs = [
        pl.BlockSpec(memory_space=pltpu.HBM if isinstance(o, Away) else pltpu.VMEM) for o in outs
    ]
    moved = sum(a.size * a.dtype.itemsize for a in values)
    return pl.pallas_call(
        kernel,
        out_shape=[o.value if isinstance(o, Away) else o for o in outs],
        in_specs=in_specs,
        out_specs=out_specs,
        scratch_shapes=[pltpu.VMEM(shape, dtype) for shape, dtype in scratch]
        + ([pltpu.SemaphoreType.DMA((copies,))] if copies else []),
        compiler_params=pltpu.CompilerParams(vmem_limit_bytes=room * 1024 * 1024),
        cost_estimate=pl.CostEstimate(
            flops=flops, bytes_accessed=moved if flops else 0, transcendentals=cells
        ),
    )(*values)


class Mover:
    def __init__(self, sems):
        self.sems, self.count, self.results = sems, 0, []

    def load(self, source, target):
        copy = pltpu.make_async_copy(source, target, self.sems.at[self.count])
        self.count += 1
        copy.start()
        return copy

    def store(self, source, target):
        self.results.append(self.load(source, target))

    def finish(self):
        for copy in self.results:
            copy.wait()


def wait_all(copies):
    for copy in copies:
        copy.wait()


def load_pieces(move, place, target, own, near, far, ids):
    here, core = place[0], place[1]
    rows = own.shape[0]
    half = rows // 2
    copies = [move.load(own, target.at[pl.ds(pl.multiple_of(here * rows, rows), rows), :])]
    for pieces, side in ((near, core), (far, 1 - core)):
        for ref, steps in zip(pieces, ids):
            for i, step in enumerate(steps):
                if step:
                    spot = jnp.bitwise_xor(here, step) * rows + side * half
                    copies.append(
                        move.load(ref.at[i], target.at[pl.ds(pl.multiple_of(spot, half), half), :])
                    )
    return copies


def loop(count, step, unroll=1):
    def some(i, carry):
        for j in range(unroll):
            step(i * unroll + j)
        return carry

    if unroll == count:
        some(0, 0)
    else:
        lax.fori_loop(0, count // unroll, some, 0)


def part_of(i, size):
    if isinstance(i, int):
        return slice(i * size, (i + 1) * size)
    return pl.ds(pl.multiple_of(i * size, size), size)


def attend(heads, first, qkv, att, lse, keys, chunk=256):
    def one_head(head):
        keys[...] = qkv[part_of(heads + head, HEAD), :].T
        rows = part_of(head, HEAD)

        def one_chunk(i):
            at = part_of(i, chunk)
            scores = mm(keys[...], qkv[rows, part_of(i + first // chunk, chunk)])
            top = jnp.max(scores, axis=0, keepdims=True)
            exponent = jnp.exp(scores - top)
            total = jnp.sum(exponent, axis=0, keepdims=True)
            weighted = mm(qkv[part_of(2 * heads + head, HEAD), :], exponent.astype(BF16))
            att[rows, at] = (weighted / total).astype(BF16)
            lse[pl.ds(head, 1), at] = top + jnp.log(total)

        loop(att.shape[1] // chunk, one_chunk, att.shape[1] // chunk)

    lse[...] = jnp.zeros_like(lse)
    loop(heads, one_head)


def project_kernel(heads, ids, place, own, *refs):
    count = len(ids)
    near, far, refs = refs[:count], refs[count : 2 * count], refs[2 * count :]
    gain, weight_in, cosine, sine, tok_out, first, qkv, att, lse, tok, weight, keys, sems = refs
    move = Mover(sems)
    local = heads * HEAD
    tokens = tok.shape[0]
    pieces = load_pieces(move, place, tok, own, near, far, ids)
    weight_load = move.load(weight_in, weight)
    wait_all(pieces)
    move.store(tok, tok_out)
    weight_load.wait()
    chunk = 256

    def one_chunk(i):
        at = part_of(i, chunk)
        normed, _ = norm_parts(tok[at, :].astype(F32))
        rounded = (normed * gain[...]).astype(BF16)
        first[at, :] = rounded
        raw = mm(weight[...], rounded, NT)
        cos, sin = cosine[:, at], sine[:, at]
        for part in range(2):
            for head in range(heads):
                base = part * local + head * HEAD
                lower = raw[base : base + HEAD // 2]
                upper = raw[base + HEAD // 2 : base + HEAD]
                turned = jnp.concatenate(
                    [lower * cos - upper * sin, upper * cos + lower * sin], axis=0
                ).astype(BF16)
                if part == 0:
                    turned = turned * jnp.asarray(HEAD ** (-0.5), BF16)
                qkv[base : base + HEAD, at] = turned
        qkv[2 * local :, at] = raw[2 * local :].astype(BF16)

    loop(tokens // chunk, one_chunk, 2)
    attend(heads, 0, qkv, att, lse, keys)
    move.finish()


def queries_kernel(heads, qkv, att, lse, keys):
    attend(heads, qkv.shape[1] - att.shape[1], qkv, att, lse, keys)


def cdf_terms(gate):
    half = 0.5 * (1.0 + lax.erf(gate * (0.5**0.5)))
    slope = half + gate * (jnp.exp(-0.5 * gate * gate) * 0.3989422804014327)
    return half, slope


def mlp_kernel(turn, ids, place, tok_in, *refs):
    count = len(ids)
    if turn == 0:
        cot_own, near, far = refs[0], refs[1 : 1 + count], refs[1 + count : 1 + 2 * count]
        refs = refs[1 + 2 * count :]
        atts, attns, mlp_own, mlp_far = refs[:4], refs[4:8], refs[8], refs[9]
        gain, cot, attn, w_in, w_mlp, tok_next = refs[10:16]
        refs = refs[16:]
    else:
        cot, atts, (gain, attn, w_in, w_mlp), refs = refs[0], refs[1:5], refs[5:9], refs[9:]
    middle_ref, second_ref, hidden_ref, gate_ref, part_ref, out_ref = refs[:6]
    tokens = middle_ref.shape[0]
    sems = refs[-1]
    move = Mover(sems)
    here, quarter, side = place[0], place[2], place[3]
    local = atts[0].shape[0]
    units = hidden_ref.shape[0]
    begin = turn * tokens
    first_loads = []
    if turn == 0:
        tok, refs = refs[6], refs[:6] + refs[7:]
        first_loads.append(move.load(tok_in.at[:tokens, :], tok))
    else:
        tok = tok_in
    att, hidden_v, gate_v = refs[6:9]
    for p in range(4):
        spot = pl.ds(pl.multiple_of(jnp.bitwise_xor(quarter, p) * local, local), local)
        first_loads.append(move.load(atts[p], att.at[spot, :]))
        if turn == 0:
            first_loads.append(move.load(attns[p], attn.at[spot, :]))
    in_loads, mlp_loads = [], []
    if turn == 0:
        for source, r in ((mlp_own, side), (mlp_far, 1 - side)):
            for part, target in ((0, w_in), (1, w_in), (2, w_mlp)):
                spot = pl.ds(pl.multiple_of((r + 2 * (part % 2)) * units, units), units)
                rows = source.at[part * units : (part + 1) * units, :]
                (mlp_loads if part == 2 else in_loads).append(move.load(rows, target.at[spot, :]))
        mlp_loads += load_pieces(move, place, cot, cot_own, near, far, ids)
        mlp_loads.append(move.load(tok_in.at[tokens:, :], tok_next))
    wait_all(first_loads)
    chunk = 256

    def one_chunk(i):
        at = part_of(i, chunk)
        middle = tok[at, :].astype(F32) + mm(att[:, at].T, attn[...])
        middle_ref[at, :] = middle
        normed, _ = norm_parts(middle)
        second = (normed * gain[...]).astype(BF16)
        second_ref[at, :] = second

        if i == 0:
            wait_all(in_loads)

        gate_up = mm(w_in[...], second, NT)
        gate, up = gate_up[: 2 * units], gate_up[2 * units :]
        half, slope = cdf_terms(gate)
        active = gate * half
        hidden_v[:, at] = (active * up).astype(BF16)

        if i == 0:
            wait_all(mlp_loads)

        back = mm(w_mlp[...], cot[part_of(i + begin // chunk, chunk), :], NT)
        grads = jnp.concatenate([slope * up * back, active * back], axis=0).astype(BF16)
        gate_v[:, at] = grads
        part_ref[at, :] = mm(grads.T, w_in[...]).astype(BF16)

    loop(tokens // chunk, one_chunk, tokens // chunk)
    mine = pl.ds(pl.multiple_of(side * units, units), units)
    mine_up = pl.ds(pl.multiple_of(side * units + 2 * units, units), units)
    hidden_ref[...] = hidden_v[mine, :]
    gate_ref[:units, :] = gate_v[mine, :]
    gate_ref[units:, :] = gate_v[mine_up, :]
    rows = out_ref.shape[0]
    spots = tokens // rows
    out_ref[...] = jnp.zeros_like(out_ref)

    @pl.when(here // spots == turn)
    def _():
        own = pl.ds(pl.multiple_of((here - turn * spots) * rows, rows), rows)
        out_ref[...] = mm(hidden_v[:, own].T, w_mlp[...]).astype(BF16)


def back_kernel(heads, place, *refs):
    middles, parts, fars, refs = refs[:2], refs[2:4], refs[4:6], refs[6:]
    cot, gain, attn, qkv, refs = refs[0], refs[1], refs[2], refs[3], refs[4:]
    lses, weight, cosine, sine, refs = refs[:2], refs[2], refs[3], refs[4], refs[5:]
    gain_v, branch, own_v, grad_v, first_v, back_rows, lse, keys, values, key_grad, value_grad = refs
    here = place[0]
    turns = middles[0].shape[0]
    tokens = 2 * turns
    rows = own_v.shape[0]
    local = heads * HEAD
    spots = turns // rows
    gain_v[...] = jnp.zeros_like(gain_v)

    def norm_block(turn, b, carry):
        here_at = pl.ds(pl.multiple_of(b * rows, rows), rows)
        at = pl.ds(pl.multiple_of((b + turn * spots) * rows, rows), rows)
        second = parts[turn][here_at, :].astype(F32) + fars[turn][here_at, :].astype(F32)
        normed, scale = norm_parts(middles[turn][here_at, :])
        gain_v[...] += jnp.sum(second * normed, axis=0, keepdims=True)
        grad = cot[at, :].astype(F32) + norm_back(second * gain[...], normed, scale)
        branch[at, :] = grad.astype(BF16)

        @pl.when(b + turn * spots == here)
        def _():
            own_v[...] = grad

        return carry

    for turn in range(2):
        lax.fori_loop(0, spots, functools.partial(norm_block, turn), 0)
    chunk = 256

    def grad_chunk(i):
        at = part_of(i, chunk)
        back_rows[:, at] = mm(attn[...], branch[at, :], NT).astype(BF16)

    loop(tokens // chunk, grad_chunk, 2)
    for turn in range(2):
        lse[:, turn * turns : (turn + 1) * turns] = lses[turn][...]
    scale = HEAD ** (-0.5)

    def turn_back(grad, cos, sin):
        lower, upper = grad[: HEAD // 2], grad[HEAD // 2 :]
        return jnp.concatenate(
            [lower * cos + upper * sin, upper * cos - lower * sin], axis=0
        ).astype(BF16)

    def one_head(head):
        rows_q, rows_k, rows_v = [part_of(p * heads + head, HEAD) for p in range(3)]
        keys[...] = qkv[rows_k, :].T
        values[...] = qkv[rows_v, :].T
        key_grad[...] = jnp.zeros_like(key_grad)
        value_grad[...] = jnp.zeros_like(value_grad)

        def one_chunk(i):
            at = part_of(i, chunk)
            query = qkv[rows_q, at]
            out_grad = back_rows[rows_q, at]
            chances = jnp.exp(mm(keys[...], query) - lse[pl.ds(head, 1), at])
            chance_grad = mm(values[...], out_grad)
            delta = jnp.sum(chances * chance_grad, axis=0, keepdims=True)
            score_grad = (chances * (chance_grad - delta)).astype(BF16)
            query_grad = mm(qkv[rows_k, :], score_grad) * scale
            key_grad[...] += mm(score_grad, query.T)
            value_grad[...] += mm(chances.astype(BF16), out_grad.T)
            grad_v[rows_q, at] = turn_back(query_grad, cosine[:, at], sine[:, at])

        loop(tokens // chunk, one_chunk, tokens // chunk)
        grad_v[rows_k, :] = turn_back(key_grad[...].T, cosine[...], sine[...])
        grad_v[rows_v, :] = value_grad[...].T.astype(BF16)

    loop(heads, one_head)
    own = pl.ds(pl.multiple_of(here * rows, rows), rows)
    first_v[...] = mm(grad_v[:, own].T, weight[...]).astype(BF16)


def over_ctx(value, step, spots):
    return lax.ppermute(value, "ctx", [(spot, spot ^ step) for spot in range(spots)])


def swap(value, mask):
    return lax.ppermute(value, "wt", [(spot, spot ^ mask) for spot in range(4)])


def half_of(block, core):
    half = block.shape[0] // 2
    return lax.dynamic_slice_in_dim(block, core * half, half, axis=0)


def gather_tokens(block, core, spots):
    half = half_of(block, core)
    steps = [over_ctx(half, step, spots) for step in range(2, spots, 2)]
    first = jnp.stack([half, steps[0]])
    rest = jnp.stack(steps[1:])
    first_y = over_ctx(first, 1, spots)
    rest_y = over_ctx(rest, 1, spots)
    near = [first, first_y, rest, rest_y]
    later = list(range(4, spots, 2))
    ids = ((0, 2), (1, 3), tuple(later), tuple(step + 1 for step in later))
    return near, [swap(piece, 1) for piece in near], ids, steps


def gather_cotangent(block, core, spots, after, gate):
    half = half_of(block, core)
    pair = jnp.stack([half, over_ctx(half, 1, spots)])
    pair, _ = lax.optimization_barrier((pair, after))
    near = [pair] + [over_ctx(pair, step, spots) for step in range(2, spots, 2)]
    ids = tuple((step, step + 1) for step in range(0, spots, 2))
    near, _ = lax.optimization_barrier((near, gate))
    return near, [swap(piece, 1) for piece in near], ids


def two_rows(row):
    high = row.astype(BF16)
    low = (row - high.astype(F32)).astype(BF16)
    return jnp.concatenate([high[None], low[None], jnp.zeros((14, row.shape[0]), BF16)], 0)


def sum_rows(pair):
    return pair[0].astype(F32) + pair[1].astype(F32)


def replicated_body(
    spots,
    tokens,
    first_gain,
    qkv_weight,
    attn_weight,
    second_gain,
    in_weight,
    mlp_weight,
    cotangent,
):
    rows, width = tokens.shape
    total_rows = rows * spots
    local = qkv_weight.shape[2]
    heads = local // HEAD
    units = mlp_weight.shape[0]
    here, quarter = lax.axis_index("ctx"), lax.axis_index("wt")
    core, side = quarter % 2, quarter // 2
    place = jnp.stack([here, core, quarter, side]).astype(jnp.int32)
    frequency = rope_base ** (-(jnp.arange(HEAD // 2).astype(F32) * 2.0 / HEAD))
    angles = frequency[:, None] * jnp.arange(total_rows).astype(F32)[None, :]
    cosine, sine = jnp.cos(angles), jnp.sin(angles)
    qkv_t = jnp.transpose(qkv_weight, (1, 2, 0)).reshape(3 * local, width)
    in_t = jnp.transpose(in_weight, (1, 2, 0)).reshape(2 * units, width)

    near, far, ids, steps = gather_tokens(tokens, core, spots)
    attn_core = swap(attn_weight, 1)
    attn_side = swap(attn_weight, 2)
    attn_both = swap(attn_side, 1)
    mlp_weights = jnp.concatenate([in_t, mlp_weight], axis=0)
    mlp_weights, _ = lax.optimization_barrier((mlp_weights, attn_side))
    mlp_side = swap(mlp_weights, 2)
    half_rows = total_rows // 2
    tall, wide = (total_rows, width), (half_rows, width)
    cells = heads * total_rows * half_rows
    tok_all, first_input, qkv, att_a, lse_a = call(
        functools.partial(project_kernel, heads, ids),
        [
            Away(pltpu.HBM(tall, BF16)),
            fast(tall, BF16),
            fast((3 * local, total_rows), BF16),
            fast((local, half_rows), BF16),
            fast((8, half_rows), F32),
        ],
        [
            place,
            Away(tokens),
            *map(Away, near),
            *map(Away, far),
            first_gain[None, :],
            Away(qkv_t),
            cosine,
            sine,
        ],
        scratch=[(tall, BF16), ((3 * local, width), BF16), ((total_rows, HEAD), BF16)],
        copies=20,
    )
    side_a = swap(att_a, 2)
    att_b, lse_b = call(
        functools.partial(queries_kernel, heads),
        [fast((local, half_rows), BF16), fast((8, half_rows), F32)],
        [qkv],
        scratch=[((total_rows, HEAD), BF16)],
    )
    cot_near, cot_far, cot_ids = gather_cotangent(cotangent, core, spots, steps[-1], att_b)
    side_a, _ = lax.optimization_barrier((side_a, att_b))
    atts_a = [att_a, swap(att_a, 1), side_a, swap(side_a, 1)]
    halves = [
        fast(wide, F32),
        fast(wide, BF16),
        fast((units, half_rows), BF16),
        fast((2 * units, half_rows), BF16),
        fast(wide, BF16),
        fast((rows, width), BF16),
    ]
    room = [
        ((4 * local, half_rows), BF16),
        ((2 * units, half_rows), BF16),
        ((4 * units, half_rows), BF16),
    ]
    second_row = second_gain[None, :]
    cot_all, attn_all, in_all, mlp_all, tok_b, *results_a = call(
        functools.partial(mlp_kernel, 0, cot_ids),
        [
            fast(tall, BF16),
            fast((4 * local, width), BF16),
            fast((4 * units, width), BF16),
            fast((2 * units, width), BF16),
            fast(wide, BF16),
            *halves,
        ],
        [
            place,
            *map(Away, [tok_all, cotangent, *cot_near, *cot_far]),
            att_a,
            *map(Away, atts_a[1:]),
            *map(Away, [attn_weight, attn_core, attn_side, attn_both]),
            *map(Away, [mlp_weights, mlp_side]),
            second_row,
        ],
        scratch=[(wide, BF16), *room],
        copies=32,
        flops=2 * half_rows * width * (4 * local + 10 * units),
        cells=4 * units * half_rows,
        room=20,
    )
    side_b, _ = lax.optimization_barrier((swap(att_b, 2), cot_all))
    atts_b = [att_b, swap(att_b, 1), side_b, swap(side_b, 1)]
    results_b = call(
        functools.partial(mlp_kernel, 1, ()),
        halves,
        [
            place,
            tok_b,
            cot_all,
            att_b,
            *map(Away, atts_b[1:]),
            second_row,
            attn_all,
            in_all,
            mlp_all,
        ],
        scratch=room,
        copies=8,
        flops=2 * half_rows * width * (4 * local + 10 * units),
        cells=4 * units * half_rows,
        room=20,
    )
    middles, seconds, hiddens, gates, parts, out_parts = zip(results_a, results_b)
    fars = [swap(part, 1) for part in parts]
    out_part = jnp.where(here < spots // 2, *out_parts)
    out_far = swap(out_part, 1)

    second_gain_grad, branch_grad, middle_grad, grad_t, first_part = call(
        functools.partial(back_kernel, heads),
        [
            fast((1, width), F32),
            fast(tall, BF16),
            fast((rows, width), F32),
            fast((3 * local, total_rows), BF16),
            fast((rows, width), BF16),
        ],
        [
            place,
            *middles,
            *parts,
            *fars,
            cot_all,
            second_row,
            attn_weight,
            qkv,
            lse_a,
            lse_b,
            qkv_t,
            cosine,
            sine,
        ],
        scratch=[
            ((local, total_rows), BF16),
            ((8, total_rows), F32),
            ((total_rows, HEAD), BF16),
            ((total_rows, HEAD), BF16),
            ((total_rows, HEAD), F32),
            ((total_rows, HEAD), F32),
        ],
        flops=2 * total_rows * local * (width + 20 * total_rows),
        cells=heads * total_rows * total_rows,
    )
    pair = (first_part.astype(F32) + swap(first_part, 1).astype(F32)).astype(BF16)
    qkv_grad = mm(grad_t, first_input)
    gain_rows = two_rows(jnp.sum(qkv_t.astype(F32) * qkv_grad, axis=0) / first_gain)
    across = jnp.concatenate([pair, gain_rows], 0)
    far_rows = swap(across, 2)
    first_grad = pair.astype(F32) + far_rows[:rows].astype(F32)
    gain_rows = two_rows(sum_rows(gain_rows) + sum_rows(far_rows[rows:]))
    first_gain_grad = sum_rows(gain_rows) + sum_rows(swap(gain_rows, 1))

    hiddens, out_far, _ = lax.optimization_barrier((hiddens, out_far, pair))
    attn_grad = mm(jnp.concatenate([att_a, att_b], 1), branch_grad)
    in_grad = mm(gates[0], seconds[0]) + mm(gates[1], seconds[1])
    mlp_grad = mm(hiddens[0], cot_all[:half_rows]) + mm(hiddens[1], cot_all[half_rows:])
    own_row = (here % (spots // 2)) * rows
    own_middle = jnp.where(
        here < spots // 2,
        *[lax.dynamic_slice_in_dim(middle, own_row, rows, axis=0) for middle in middles],
    )
    output = (own_middle + (out_part.astype(F32) + out_far.astype(F32))).astype(BF16)
    normed, scale = norm_parts(tokens.astype(F32))
    tokens_grad = (middle_grad + norm_back(first_grad * first_gain, normed, scale)).astype(BF16)
    return (
        output,
        tokens_grad,
        first_gain_grad,
        jnp.transpose(qkv_grad.reshape(3, local, width), (2, 0, 1)),
        attn_grad,
        second_gain_grad[0],
        jnp.transpose(in_grad.reshape(2, units, width), (2, 0, 1)),
        mlp_grad,
    )


def body(sizes, tokens, *rest):
    spots, lanes = sizes["ctx"], sizes["wt"]
    rows = tokens.shape[0]
    small = spots * rows <= REPLICATED_TOKENS and rows % 128 == 0 and (spots * rows) % 256 == 0
    if small and lanes == 4 and spots == 8:
        return replicated_body(spots, tokens, *rest)
    return split_body(tokens, *rest)


def solution(mesh):
    return jax.shard_map(
        functools.partial(body, dict(mesh.shape)),
        mesh=mesh,
        in_specs=(
            P("ctx", None),
            P(),
            P(None, None, "wt"),
            P("wt", None),
            P(),
            P(None, None, "wt"),
            P("wt", None),
            P("ctx", None),
        ),
        out_specs=(
            P("ctx", None),
            P("ctx", None),
            P(),
            P(None, None, "wt"),
            P("wt", None),
            P(),
            P(None, None, "wt"),
            P("wt", None),
        ),
        check_vma=False,
    )
```

```python
import functools

import jax
import jax.numpy as jnp
from jax import lax
from jax.experimental import pallas as pl
from jax.experimental.pallas import tpu as pltpu
from jax.sharding import PartitionSpec as P

HEAD = 64


rope_base = 160000.0
norm_epsilon = 1e-05


def layer_norm(values):
    center = values - jnp.mean(values, axis=-1, keepdims=True)
    return center * lax.rsqrt(jnp.mean(center * center, axis=-1, keepdims=True) + norm_epsilon)


def rotate(values, positions, direction):
    half_width = values.shape[-1] // 2
    frequency = rope_base ** (
        -(jnp.arange(half_width).astype(jnp.float32) * 2.0 / values.shape[-1])
    )
    angles = positions[:, None] * frequency[None, :]
    cosine_part = jnp.cos(angles)[:, None, :]
    sine_part = jnp.sin(angles)[:, None, :]
    lower_half = values[..., :half_width]
    upper_half = values[..., half_width:]
    return jnp.concatenate(
        [
            lower_half * cosine_part - direction * upper_half * sine_part,
            upper_half * cosine_part + direction * lower_half * sine_part,
        ],
        axis=-1,
    )


def block_size_for(shard_rows):
    candidate = shard_rows * max(1, 1024 // shard_rows)
    return candidate


def score_terms(
    query_block, grad_block, logsum_block, delta_block, key_block, value_block, score_scale
):
    scores = (
        jnp.einsum("thd,shd->ths", query_block, key_block, preferred_element_type=jnp.float32)
        * score_scale
    )
    chances = jnp.exp(scores - logsum_block[..., None])
    chance_grad = jnp.einsum(
        "thd,shd->ths", grad_block, value_block, preferred_element_type=jnp.float32
    )
    score_grad = (chances * (chance_grad - delta_block[..., None])).astype(jnp.bfloat16)
    return (chances.astype(jnp.bfloat16), score_grad)


def split_body(
    tokens, first_gain, qkv_weight, attn_weight, second_gain, in_weight, mlp_weight, cotangent
):
    row_count = tokens.shape[0]
    local_width = qkv_weight.shape[2]
    heads_here = local_width // HEAD
    score_scale = HEAD ** (-0.5)
    positions = (lax.axis_index("ctx") * row_count + jnp.arange(row_count, dtype=jnp.int32)).astype(
        jnp.float32
    )
    inputs = tokens.astype(jnp.float32)
    normed_first, first_pull = jax.vjp(layer_norm, inputs)
    first_input = (normed_first * first_gain).astype(jnp.bfloat16)
    projected = jnp.einsum(
        "td,dsh->tsh", first_input, qkv_weight, preferred_element_type=jnp.float32
    )
    shaped = projected.reshape(row_count, 3, heads_here, HEAD)
    query_rows = rotate(shaped[:, 0], positions, 1.0).astype(jnp.bfloat16)
    key_rows = rotate(shaped[:, 1], positions, 1.0).astype(jnp.bfloat16)
    value_rows = shaped[:, 2].astype(jnp.bfloat16)
    key_flat = key_rows.reshape(row_count, local_width)
    value_flat = value_rows.reshape(row_count, local_width)
    start_state = (
        jnp.full((row_count, heads_here), -1e30, jnp.float32),
        jnp.zeros((row_count, heads_here), jnp.float32),
        jnp.zeros((row_count, heads_here, HEAD), jnp.float32),
    )
    key_piece = lax.all_gather(key_flat, "ctx", axis=0, tiled=True)
    value_piece = lax.all_gather(value_flat, "ctx", axis=0, tiled=True)
    piece_rows = key_piece.shape[0]
    block_size = block_size_for(row_count)
    key_blocks = key_piece.reshape(piece_rows // block_size, block_size, heads_here, HEAD)
    value_blocks = value_piece.reshape(piece_rows // block_size, block_size, heads_here, HEAD)

    def forward_visit(state, block_item):
        running_max, running_sum, weighted = state
        key_block, value_block = block_item
        scores = (
            jnp.einsum("thd,shd->ths", query_rows, key_block, preferred_element_type=jnp.float32)
            * score_scale
        )
        new_max = jnp.maximum(running_max, jnp.max(scores, axis=-1))
        factor = jnp.exp(running_max - new_max)
        exponent = jnp.exp(scores - new_max[..., None])
        running_sum = running_sum * factor + jnp.sum(exponent, axis=-1)
        weighted = weighted * factor[..., None] + jnp.einsum(
            "ths,shd->thd",
            exponent.astype(jnp.bfloat16),
            value_block,
            preferred_element_type=jnp.float32,
        )
        return ((new_max, running_sum, weighted), None)

    result = lax.scan(forward_visit, start_state, (key_blocks, value_blocks))
    running_max, running_sum, weighted = result[0]
    attended_exact = weighted / running_sum[..., None]
    logsum = running_max + jnp.log(running_sum)
    attended = attended_exact.astype(jnp.bfloat16).reshape(row_count, local_width)
    branch = lax.psum(
        jnp.dot(attended, attn_weight, preferred_element_type=jnp.float32).astype(jnp.bfloat16),
        "wt",
    ).astype(jnp.float32)
    middle = inputs + branch
    normed_second, second_pull = jax.vjp(layer_norm, middle)
    second_input = (normed_second * second_gain).astype(jnp.bfloat16)
    gate_up = jnp.einsum("td,dsf->tsf", second_input, in_weight, preferred_element_type=jnp.float32)

    def activate(pair):
        return jax.nn.gelu(pair[:, 0], approximate=False) * pair[:, 1]

    hidden_exact, activate_back = jax.vjp(activate, gate_up)
    hidden = hidden_exact.astype(jnp.bfloat16)
    mlp_branch = lax.psum(
        jnp.dot(hidden, mlp_weight, preferred_element_type=jnp.float32).astype(jnp.bfloat16), "wt"
    ).astype(jnp.float32)
    output = (middle + mlp_branch).astype(jnp.bfloat16)
    hidden_grad = jnp.einsum("td,fd->tf", cotangent, mlp_weight, preferred_element_type=jnp.float32)
    mlp_weight_grad = jnp.einsum("tf,td->fd", hidden, cotangent, preferred_element_type=jnp.float32)
    gate_up_grad = activate_back(hidden_grad)[0].astype(jnp.bfloat16)
    second_part = jnp.einsum(
        "tsf,dsf->td", gate_up_grad, in_weight, preferred_element_type=jnp.float32
    )
    in_weight_grad = jnp.einsum(
        "td,tsf->dsf", second_input, gate_up_grad, preferred_element_type=jnp.float32
    )
    second_grad = lax.psum(second_part.astype(jnp.bfloat16), "wt").astype(jnp.float32)
    second_gain_grad = jnp.sum(second_grad * normed_second, axis=0)
    middle_grad = cotangent.astype(jnp.float32) + second_pull(second_grad * second_gain)[0]
    branch_grad = middle_grad.astype(jnp.bfloat16)
    attended_grad = jnp.einsum(
        "td,hd->th", branch_grad, attn_weight, preferred_element_type=jnp.float32
    )
    attn_weight_grad = jnp.einsum(
        "th,td->hd", attended, branch_grad, preferred_element_type=jnp.float32
    )
    grad_rows = attended_grad.astype(jnp.bfloat16).reshape(row_count, heads_here, HEAD)
    row_delta = jnp.sum(grad_rows.astype(jnp.float32) * attended_exact, axis=-1)
    zero_rows = jnp.zeros((row_count, heads_here, HEAD), jnp.float32)
    query_acc = zero_rows
    key_piece = lax.all_gather(key_flat, "ctx", axis=0, tiled=True)
    value_piece = lax.all_gather(value_flat, "ctx", axis=0, tiled=True)
    piece_rows = key_piece.shape[0]
    block_size = block_size_for(row_count)
    key_blocks = key_piece.reshape(piece_rows // block_size, block_size, heads_here, HEAD)
    value_blocks = value_piece.reshape(piece_rows // block_size, block_size, heads_here, HEAD)

    def backward_visit(partial_value, block_item):
        key_block, value_block = block_item
        chance_low, score_grad = score_terms(
            query_rows, grad_rows, logsum, row_delta, key_block, value_block, score_scale
        )
        partial_value = (
            partial_value
            + jnp.einsum("ths,shd->thd", score_grad, key_block, preferred_element_type=jnp.float32)
            * score_scale
        )
        key_term = (
            jnp.einsum("ths,thd->shd", score_grad, query_rows, preferred_element_type=jnp.float32)
            * score_scale
        )
        value_term = jnp.einsum(
            "ths,thd->shd", chance_low, grad_rows, preferred_element_type=jnp.float32
        )
        return (partial_value, (key_term, value_term))

    query_acc, terms = lax.scan(backward_visit, query_acc, (key_blocks, value_blocks))
    key_total = terms[0].reshape(piece_rows, local_width)
    value_total = terms[1].reshape(piece_rows, local_width)
    key_sum, value_sum = (
        lax.psum_scatter(key_total, "ctx", scatter_dimension=0, tiled=True),
        lax.psum_scatter(value_total, "ctx", scatter_dimension=0, tiled=True),
    )
    key_grad = key_sum.reshape(row_count, heads_here, HEAD)
    value_grad = value_sum.reshape(row_count, heads_here, HEAD)
    query_back = rotate(query_acc, positions, -1.0)
    key_back = rotate(key_grad, positions, -1.0)
    projected_grad = (
        jnp.stack([query_back, key_back, value_grad], axis=1)
        .reshape(row_count, 3, local_width)
        .astype(jnp.bfloat16)
    )
    first_part = jnp.einsum(
        "tsh,dsh->td", projected_grad, qkv_weight, preferred_element_type=jnp.float32
    )
    qkv_weight_grad = jnp.einsum(
        "td,tsh->dsh", first_input, projected_grad, preferred_element_type=jnp.float32
    )
    first_grad = lax.psum(first_part.astype(jnp.bfloat16), "wt").astype(jnp.float32)
    first_gain_grad = jnp.sum(first_grad * normed_first, axis=0)
    tokens_grad = (middle_grad + first_pull(first_grad * first_gain)[0]).astype(jnp.bfloat16)
    summed = lax.psum(
        (
            first_gain_grad,
            qkv_weight_grad,
            attn_weight_grad,
            second_gain_grad,
            in_weight_grad,
            mlp_weight_grad,
        ),
        "ctx",
    )
    return (output, tokens_grad, summed[0], summed[1], summed[2], summed[3], summed[4], summed[5])


F32 = jnp.float32
BF16 = jnp.bfloat16
NT = (((1,), (1,)), ((), ()))
TN = (((0,), (0,)), ((), ()))
REPLICATED_TOKENS = 2048


def mm(a, b, dims=(((1,), (0,)), ((), ()))):
    return lax.dot_general(a, b, dims, preferred_element_type=F32)


def norm_parts(values):
    return norm_stats(values)[:2]


def norm_stats(values):
    mean = jnp.mean(values, axis=-1, keepdims=True)
    center = values - mean
    scale = lax.rsqrt(jnp.mean(center * center, axis=-1, keepdims=True) + norm_epsilon)
    return center * scale, scale, mean


def norm_back(grad, normed, scale):
    mean_grad = jnp.mean(grad, axis=-1, keepdims=True)
    mean_both = jnp.mean(grad * normed, axis=-1, keepdims=True)
    return scale * (grad - mean_grad - normed * mean_both)


def fast(shape, dtype):
    return pltpu.VMEM(shape, dtype)


class Away:
    def __init__(self, value):
        self.value = value


def call(kernel, outs, args, scratch=(), copies=0, flops=0, cells=0, room=16):
    in_specs, values = [], []
    for arg in args:
        value = arg.value if isinstance(arg, Away) else arg
        if value.dtype == jnp.int32:
            in_specs.append(pl.BlockSpec(memory_space=pltpu.SMEM))
            values.append(value)
            continue
        space = pltpu.HBM if isinstance(arg, Away) else pltpu.VMEM
        in_specs.append(pl.BlockSpec(memory_space=space))
        values.append(pltpu.with_memory_space_constraint(value, space))
    out_specs = [
        pl.BlockSpec(memory_space=pltpu.HBM if isinstance(o, Away) else pltpu.VMEM) for o in outs
    ]
    moved = sum(a.size * a.dtype.itemsize for a in values)
    return pl.pallas_call(
        kernel,
        out_shape=[o.value if isinstance(o, Away) else o for o in outs],
        in_specs=in_specs,
        out_specs=out_specs,
        scratch_shapes=[pltpu.VMEM(shape, dtype) for shape, dtype in scratch]
        + ([pltpu.SemaphoreType.DMA((copies,))] if copies else []),
        compiler_params=pltpu.CompilerParams(vmem_limit_bytes=room * 1024 * 1024),
        cost_estimate=pl.CostEstimate(
            flops=flops, bytes_accessed=moved if flops else 0, transcendentals=cells
        ),
    )(*values)


class Mover:
    def __init__(self, sems):
        self.sems, self.count, self.results = sems, 0, []

    def load(self, source, target):
        copy = pltpu.make_async_copy(source, target, self.sems.at[self.count])
        self.count += 1
        copy.start()
        return copy

    def store(self, source, target):
        self.results.append(self.load(source, target))

    def finish(self):
        for copy in self.results:
            copy.wait()


def wait_all(copies):
    for copy in copies:
        copy.wait()


def load_pieces(move, place, target, own, near, far, ids):
    here, core = place[0], place[1]
    rows = own.shape[0]
    half = rows // 2
    copies = [move.load(own, target.at[pl.ds(pl.multiple_of(here * rows, rows), rows), :])]
    for pieces, side in ((near, core), (far, 1 - core)):
        for ref, steps in zip(pieces, ids):
            for i, step in enumerate(steps):
                if step:
                    spot = jnp.bitwise_xor(here, step) * rows + side * half
                    copies.append(
                        move.load(ref.at[i], target.at[pl.ds(pl.multiple_of(spot, half), half), :])
                    )
    return copies


def loop(count, step, unroll=1):
    def some(i, carry):
        for j in range(unroll):
            step(i * unroll + j)
        return carry

    if unroll == count:
        some(0, 0)
    else:
        lax.fori_loop(0, count // unroll, some, 0)


def part_of(i, size):
    if isinstance(i, int):
        return slice(i * size, (i + 1) * size)
    return pl.ds(pl.multiple_of(i * size, size), size)


def attend(heads, first, qkv, att, exact, lse, keys, chunk=256):
    def one_head(head):
        keys[...] = qkv[part_of(heads + head, HEAD), :].T
        rows = part_of(head, HEAD)

        def one_chunk(i):
            at = part_of(i, chunk)
            scores = mm(keys[...], qkv[rows, part_of(i + first // chunk, chunk)])
            top = jnp.max(scores, axis=0, keepdims=True)
            exponent = jnp.exp(scores - top)
            total = jnp.sum(exponent, axis=0, keepdims=True)
            weighted = mm(qkv[part_of(2 * heads + head, HEAD), :], exponent.astype(BF16))
            weighted = weighted / total
            exact[rows, at] = weighted
            att[rows, at] = weighted.astype(BF16)
            lse[pl.ds(head, 1), at] = top + jnp.log(total)

        loop(att.shape[1] // chunk, one_chunk, att.shape[1] // chunk)

    lse[...] = jnp.zeros_like(lse)
    loop(heads, one_head)


def project_kernel(heads, ids, place, own, *refs):
    count = len(ids)
    near, far, refs = refs[:count], refs[count : 2 * count], refs[2 * count :]
    gain, weight_in, cosine, sine, tok_out, first, qkv, att, exact, lse, tok, weight, keys, sems = refs
    move = Mover(sems)
    local = heads * HEAD
    tokens = tok.shape[0]
    pieces = load_pieces(move, place, tok, own, near, far, ids)
    weight_load = move.load(weight_in, weight)
    wait_all(pieces)
    move.store(tok, tok_out)
    weight_load.wait()
    chunk = 256

    def one_chunk(i):
        at = part_of(i, chunk)
        normed, _ = norm_parts(tok[at, :].astype(F32))
        rounded = (normed * gain[...]).astype(BF16)
        first[at, :] = rounded
        raw = mm(weight[...], rounded, NT)
        cos, sin = cosine[:, at], sine[:, at]
        for part in range(2):
            for head in range(heads):
                base = part * local + head * HEAD
                lower = raw[base : base + HEAD // 2]
                upper = raw[base + HEAD // 2 : base + HEAD]
                turned = jnp.concatenate(
                    [lower * cos - upper * sin, upper * cos + lower * sin], axis=0
                ).astype(BF16)
                if part == 0:
                    turned = turned * jnp.asarray(HEAD ** (-0.5), BF16)
                qkv[base : base + HEAD, at] = turned
        qkv[2 * local :, at] = raw[2 * local :].astype(BF16)

    loop(tokens // chunk, one_chunk, 2)
    attend(heads, 0, qkv, att, exact, lse, keys)
    move.finish()


def queries_kernel(heads, qkv, att, exact, lse, keys):
    attend(heads, qkv.shape[1] - att.shape[1], qkv, att, exact, lse, keys)


def cdf_terms(gate):
    half = 0.5 * (1.0 + lax.erf(gate * (0.5**0.5)))
    slope = half + gate * (jnp.exp(-0.5 * gate * gate) * 0.3989422804014327)
    return half, slope


def mlp_kernel(turn, ids, place, tok_in, *refs):
    count = len(ids)
    if turn == 0:
        cot_own, near, far = refs[0], refs[1 : 1 + count], refs[1 + count : 1 + 2 * count]
        refs = refs[1 + 2 * count :]
        atts, attns, (in_own, in_far, mlp_own, rest_far) = refs[:4], refs[4:7], refs[7:11]
        attns = [*attns[:2], rest_far.at[mlp_own.shape[0] :, :], attns[2]]
        gain, cot, attn, w_in, w_mlp, tok_next = refs[11:17]
        refs = refs[17:]
    else:
        cot, atts, (gain, attn, w_in, w_mlp), refs = refs[0], refs[1:5], refs[5:9], refs[9:]
        (mid_before, out_before), refs = refs[:2], refs[2:]
    middle_ref, second_ref, hidden_ref, gate_ref, part_ref, mean_ref, scale_ref = refs[:7]
    mid_ref, out_ref, refs = refs[7], refs[8], refs[9:]
    tokens = middle_ref.shape[0]
    sems = refs[-1]
    move = Mover(sems)
    here, quarter, side = place[0], place[2], place[3]
    local = atts[0].shape[0]
    units = hidden_ref.shape[0]
    begin = turn * tokens
    first_loads = []
    if turn == 0:
        tok, refs = refs[0], refs[1:]
        first_loads.append(move.load(tok_in.at[:tokens, :], tok))
    else:
        tok = tok_in
    att, hidden_v, gate_v = refs[:3]
    for p in range(4):
        spot = pl.ds(pl.multiple_of(jnp.bitwise_xor(quarter, p) * local, local), local)
        first_loads.append(move.load(atts[p], att.at[spot, :]))
        if turn == 0:
            first_loads.append(move.load(attns[p], attn.at[spot, :]))
    in_loads, mlp_loads = [], []
    if turn == 0:
        for source, r in ((in_own, side), (in_far, 1 - side)):
            for part in range(2):
                spot = pl.ds(pl.multiple_of((r + 2 * part) * units, units), units)
                rows = source.at[part * units : (part + 1) * units, :]
                in_loads.append(move.load(rows, w_in.at[spot, :]))
        for source, r in ((mlp_own, side), (rest_far, 1 - side)):
            spot = pl.ds(pl.multiple_of(r * units, units), units)
            mlp_loads.append(move.load(source.at[:units, :], w_mlp.at[spot, :]))
        mlp_loads += load_pieces(move, place, cot, cot_own, near, far, ids)
        mlp_loads.append(move.load(tok_in.at[tokens:, :], tok_next))
    wait_all(first_loads)
    chunk = 256

    def one_chunk(i):
        at = part_of(i, chunk)
        middle = tok[at, :].astype(F32) + mm(att[:, at].T, attn[...])
        middle_ref[at, :] = middle
        normed, scale_ref[at, :], mean_ref[at, :] = norm_stats(middle)
        second = (normed * gain[...]).astype(BF16)
        second_ref[at, :] = second

        if i == 0:
            wait_all(in_loads)

        gate_up = mm(w_in[...], second, NT)
        gate, up = gate_up[: 2 * units], gate_up[2 * units :]
        half, slope = cdf_terms(gate)
        active = gate * half
        hidden_v[:, at] = (active * up).astype(BF16)

        if i == 0:
            wait_all(mlp_loads)

        back = mm(w_mlp[...], cot[part_of(i + begin // chunk, chunk), :], NT)
        grads = jnp.concatenate([slope * up * back, active * back], axis=0).astype(BF16)
        gate_v[:, at] = grads
        part_ref[at, :] = mm(grads.T, w_in[...]).astype(BF16)

    loop(tokens // chunk, one_chunk, tokens // chunk)
    mine = pl.ds(pl.multiple_of(side * units, units), units)
    mine_up = pl.ds(pl.multiple_of(side * units + 2 * units, units), units)
    hidden_ref[...] = hidden_v[mine, :]
    gate_ref[:units, :] = gate_v[mine, :]
    gate_ref[units:, :] = gate_v[mine_up, :]
    rows = out_ref.shape[0]
    spots = tokens // rows
    mid_ref[...] = mid_before[...] if turn else jnp.zeros_like(mid_ref)
    out_ref[...] = out_before[...] if turn else jnp.zeros_like(out_ref)

    @pl.when(here // spots == turn)
    def _():
        own = pl.ds(pl.multiple_of((here - turn * spots) * rows, rows), rows)
        mid_ref[...] = middle_ref[own, :]
        out_ref[...] = mm(hidden_v[:, own].T, w_mlp[...]).astype(BF16)


def two_rows(row):
    high = row.astype(BF16).astype(F32)
    spots = lax.broadcasted_iota(jnp.int32, (16, row.shape[1]), 0)
    rows = jnp.where(spots == 0, high, jnp.where(spots == 1, row - high, 0.0))
    return rows.astype(BF16)


def sum_rows(rows):
    return jnp.sum(rows.astype(F32), axis=0, keepdims=True)


def back_kernel(heads, place, *refs):
    middles, means, scales, refs = refs[:2], refs[2:4], refs[4:6], refs[6:]
    parts, fars, refs = refs[:2], refs[2:4], refs[4:]
    cot, gain, attn, qkv, refs = refs[0], refs[1], refs[2], refs[3], refs[4:]
    exacts, lses, refs = refs[:2], refs[2:4], refs[4:]
    weight, cosine, sine, refs = refs[0], refs[1], refs[2], refs[3:]
    first_in, first_gain, gain_v, branch, own_v, message, qkv_out, refs = *refs[:7], refs[7:]
    grad_v, back_rows, lse, keys, values, key_grad, value_grad, qkv_grad, sems = refs
    move = Mover(sems)
    here = place[0]
    turns = middles[0].shape[0]
    tokens = 2 * turns
    rows = own_v.shape[0]
    local = heads * HEAD
    spots = turns // rows
    gain_v[...] = jnp.zeros_like(gain_v)

    def norm_block(turn, b, carry):
        here_at = pl.ds(pl.multiple_of(b * rows, rows), rows)
        at = pl.ds(pl.multiple_of((b + turn * spots) * rows, rows), rows)
        second = parts[turn][here_at, :].astype(F32) + fars[turn][here_at, :].astype(F32)
        scale = scales[turn][here_at, :]
        normed = (middles[turn][here_at, :] - means[turn][here_at, :]) * scale
        gain_v[...] += jnp.sum(second * normed, axis=0, keepdims=True)
        grad = cot[at, :].astype(F32) + norm_back(second * gain[...], normed, scale)
        branch[at, :] = grad.astype(BF16)

        @pl.when(b + turn * spots == here)
        def _():
            own_v[...] = grad

        return carry

    for turn in range(2):
        lax.fori_loop(0, spots, functools.partial(norm_block, turn), 0)
    chunk = 256

    def grad_chunk(i):
        at = part_of(i, chunk)
        back_rows[:, at] = mm(attn[...], branch[at, :], NT).astype(BF16)

    loop(tokens // chunk, grad_chunk, 2)
    for turn in range(2):
        lse[:, turn * turns : (turn + 1) * turns] = lses[turn][...]
    scale = HEAD ** (-0.5)

    def turn_back(grad, cos, sin):
        lower, upper = grad[: HEAD // 2], grad[HEAD // 2 :]
        return jnp.concatenate(
            [lower * cos + upper * sin, upper * cos - lower * sin], axis=0
        ).astype(BF16)

    def one_head(head):
        rows_q, rows_k, rows_v = [part_of(p * heads + head, HEAD) for p in range(3)]
        keys[...] = qkv[rows_k, :].T
        values[...] = qkv[rows_v, :].T
        key_grad[...] = jnp.zeros_like(key_grad)
        value_grad[...] = jnp.zeros_like(value_grad)

        def one_chunk(i):
            at = part_of(i, chunk)
            query = qkv[rows_q, at]
            out_grad = back_rows[rows_q, at]
            chances = jnp.exp(mm(keys[...], query) - lse[pl.ds(head, 1), at])
            chance_grad = mm(values[...], out_grad)
            exact = exacts[i * chunk // turns][rows_q, part_of(i % (turns // chunk), chunk)]
            delta = jnp.sum(out_grad.astype(F32) * exact, axis=0, keepdims=True)
            score_grad = (chances * (chance_grad - delta)).astype(BF16)
            query_grad = mm(qkv[rows_k, :], score_grad) * scale
            key_grad[...] += mm(score_grad, query.T)
            value_grad[...] += mm(chances.astype(BF16), out_grad.T)
            grad_v[rows_q, at] = turn_back(query_grad, cosine[:, at], sine[:, at])

        loop(tokens // chunk, one_chunk, tokens // chunk)
        grad_v[rows_k, :] = turn_back(key_grad[...].T, cosine[...], sine[...])
        grad_v[rows_v, :] = value_grad[...].T.astype(BF16)

    loop(heads, one_head)
    own = pl.ds(pl.multiple_of(here * rows, rows), rows)
    message[:rows, :] = mm(grad_v[:, own].T, weight[...]).astype(BF16)
    gain_row = jnp.zeros_like(gain_v)
    for part in range(3):
        at = part_of(part, local)
        product = mm(grad_v[at, :], first_in[...])
        qkv_grad[at, :] = product
        move.store(qkv_grad.at[at, :], qkv_out.at[at, :])
        gain_row += jnp.sum(weight[at, :].astype(F32) * product, axis=0, keepdims=True)
    message[rows:, :] = two_rows(gain_row / first_gain[...])
    move.finish()


def sum_kernel(message, far, out):
    rows = out.shape[0] - 16
    out[:rows, :] = (message[:rows, :].astype(F32) + far[:rows, :].astype(F32)).astype(BF16)
    out[rows:, :] = two_rows(sum_rows(message[rows:, :]) + sum_rows(far[rows:, :]))


def last_kernel(mine, far, tokens, gain, middle_grad, tokens_grad, gain_grad):
    rows = tokens.shape[0]
    gain_grad[...] = sum_rows(mine[rows:, :]) + sum_rows(far[rows:, :])
    first_grad = mine[:rows, :].astype(F32) + far[:rows, :].astype(F32)
    normed, scale = norm_parts(tokens[...].astype(F32))
    back = norm_back(first_grad * gain[...], normed, scale)
    tokens_grad[...] = (middle_grad[...] + back).astype(BF16)


def products_kernel(gate_a, gate_b, hidden_a, hidden_b, second_a, second_b, cot, *refs):
    in_out, mlp_out, in_grad, mlp_grad, sems = refs
    move = Mover(sems)
    tokens = second_a.shape[0]
    units = hidden_a.shape[0]
    for part in range(2):
        at = part_of(part, units)
        in_grad[at, :] = mm(gate_a[at, :], second_a[...]) + mm(gate_b[at, :], second_b[...])
        move.store(in_grad.at[at, :], in_out.at[at, :])
    mlp_grad[...] = mm(hidden_a[...], cot[:tokens, :]) + mm(hidden_b[...], cot[tokens:, :])
    move.store(mlp_grad, mlp_out)
    move.finish()


def output_kernel(att_a, att_b, branch, middle, part, far, attn_out, output, attn_grad, sems):
    move = Mover(sems)
    tokens = att_a.shape[1]
    attn_grad[...] = mm(att_a[...], branch[:tokens, :]) + mm(att_b[...], branch[tokens:, :])
    move.store(attn_grad, attn_out)
    branch_sum = part[...].astype(F32) + far[...].astype(F32)
    output[...] = (middle[...] + branch_sum).astype(BF16)
    move.finish()


def over_ctx(value, step, spots):
    return lax.ppermute(value, "ctx", [(spot, spot ^ step) for spot in range(spots)])


def swap(value, mask):
    return lax.ppermute(value, "wt", [(spot, spot ^ mask) for spot in range(4)])


def half_of(block, core):
    half = block.shape[0] // 2
    return lax.dynamic_slice_in_dim(block, core * half, half, axis=0)


def gather_tokens(block, core, spots):
    half = half_of(block, core)
    steps = [over_ctx(half, step, spots) for step in range(2, spots, 2)]
    first = jnp.stack([half, steps[0]])
    rest = jnp.stack(steps[1:])
    first_y = over_ctx(first, 1, spots)
    rest_y = over_ctx(rest, 1, spots)
    near = [first, first_y, rest, rest_y]
    later = list(range(4, spots, 2))
    ids = ((0, 2), (1, 3), tuple(later), tuple(step + 1 for step in later))
    return near, [swap(piece, 1) for piece in near], ids, steps


def gather_cotangent(block, core, spots, after, gate):
    half = half_of(block, core)
    pair = jnp.stack([half, over_ctx(half, 1, spots)])
    pair, _ = lax.optimization_barrier((pair, after))
    near = [pair] + [over_ctx(pair, step, spots) for step in range(2, spots, 2)]
    ids = tuple((step, step + 1) for step in range(0, spots, 2))
    near, _ = lax.optimization_barrier((near, gate))
    return near, [swap(piece, 1) for piece in near], ids


def replicated_body(
    spots,
    tokens,
    first_gain,
    qkv_weight,
    attn_weight,
    second_gain,
    in_weight,
    mlp_weight,
    cotangent,
):
    rows, width = tokens.shape
    total_rows = rows * spots
    local = qkv_weight.shape[2]
    heads = local // HEAD
    units = mlp_weight.shape[0]
    here, quarter = lax.axis_index("ctx"), lax.axis_index("wt")
    core, side = quarter % 2, quarter // 2
    place = jnp.stack([here, core, quarter, side]).astype(jnp.int32)
    frequency = rope_base ** (-(jnp.arange(HEAD // 2).astype(F32) * 2.0 / HEAD))
    angles = frequency[:, None] * jnp.arange(total_rows).astype(F32)[None, :]
    cosine, sine = jnp.cos(angles), jnp.sin(angles)
    qkv_t = jnp.transpose(qkv_weight, (1, 2, 0)).reshape(3 * local, width)
    in_t = jnp.transpose(in_weight, (1, 2, 0)).reshape(2 * units, width)

    near, far, ids, steps = gather_tokens(tokens, core, spots)
    attn_core = swap(attn_weight, 1)
    in_side = swap(in_t, 2)
    rest = jnp.concatenate([mlp_weight, attn_weight], axis=0)
    rest_side = swap(rest, 2)
    attn_both = swap(rest_side[units:], 1)
    half_rows = total_rows // 2
    tall, wide = (total_rows, width), (half_rows, width)
    cells = heads * total_rows * half_rows
    tok_all, first_input, qkv, att_a, exact_a, lse_a = call(
        functools.partial(project_kernel, heads, ids),
        [
            Away(pltpu.HBM(tall, BF16)),
            fast(tall, BF16),
            fast((3 * local, total_rows), BF16),
            fast((local, half_rows), BF16),
            fast((local, half_rows), F32),
            fast((8, half_rows), F32),
        ],
        [
            place,
            Away(tokens),
            *map(Away, near),
            *map(Away, far),
            first_gain[None, :],
            Away(qkv_t),
            cosine,
            sine,
        ],
        scratch=[(tall, BF16), ((3 * local, width), BF16), ((total_rows, HEAD), BF16)],
        copies=20,
    )
    side_a = swap(att_a, 2)
    att_b, exact_b, lse_b = call(
        functools.partial(queries_kernel, heads),
        [
            fast((local, half_rows), BF16),
            fast((local, half_rows), F32),
            fast((8, half_rows), F32),
        ],
        [qkv],
        scratch=[((total_rows, HEAD), BF16)],
    )
    cot_near, cot_far, cot_ids = gather_cotangent(cotangent, core, spots, steps[-1], att_b)
    side_a, _ = lax.optimization_barrier((side_a, att_b))
    atts_a = [att_a, swap(att_a, 1), side_a, swap(side_a, 1)]
    halves = [
        fast(wide, F32),
        fast(wide, BF16),
        fast((units, half_rows), BF16),
        fast((2 * units, half_rows), BF16),
        fast(wide, BF16),
        fast((half_rows, 1), F32),
        fast((half_rows, 1), F32),
        fast((rows, width), F32),
        fast((rows, width), BF16),
    ]
    room = [
        ((4 * local, half_rows), BF16),
        ((2 * units, half_rows), BF16),
        ((4 * units, half_rows), BF16),
    ]
    second_row = second_gain[None, :]
    cot_all, attn_all, in_all, mlp_all, tok_b, *results_a = call(
        functools.partial(mlp_kernel, 0, cot_ids),
        [
            fast(tall, BF16),
            fast((4 * local, width), BF16),
            fast((4 * units, width), BF16),
            fast((2 * units, width), BF16),
            fast(wide, BF16),
            *halves,
        ],
        [
            place,
            *map(Away, [tok_all, cotangent, *cot_near, *cot_far]),
            att_a,
            *map(Away, atts_a[1:]),
            *map(Away, [attn_weight, attn_core, attn_both]),
            *map(Away, [in_t, in_side, mlp_weight, rest_side]),
            second_row,
        ],
        scratch=[(wide, BF16), *room],
        copies=32,
        flops=2 * half_rows * width * (4 * local + 10 * units),
        cells=4 * units * half_rows,
        room=20,
    )
    atts_b = [att_b, *[swap(att_b, mask) for mask in (1, 2, 3)]]
    atts_b, _ = lax.optimization_barrier((atts_b, cot_all))
    results_b = call(
        functools.partial(mlp_kernel, 1, ()),
        halves,
        [
            place,
            tok_b,
            cot_all,
            att_b,
            *map(Away, atts_b[1:]),
            second_row,
            attn_all,
            in_all,
            mlp_all,
            *results_a[7:],
        ],
        scratch=room,
        copies=8,
        flops=2 * half_rows * width * (4 * local + 10 * units),
        cells=4 * units * half_rows,
        room=20,
    )
    middles, seconds, hiddens, gates, parts, means, scales = zip(results_a[:7], results_b[:7])
    own_middle, out_part = results_b[7:]
    fars = [swap(part, 1) for part in parts]
    out_far = swap(out_part, 1)
    in_grad, mlp_grad = call(
        products_kernel,
        [Away(pltpu.HBM((2 * units, width), F32)), Away(pltpu.HBM((units, width), F32))],
        [*gates, *hiddens, *seconds, cot_all],
        scratch=[((2 * units, width), F32), ((units, width), F32)],
        copies=4,
        flops=6 * total_rows * width * units,
    )
    fars, in_grad, mlp_grad = lax.optimization_barrier((fars, in_grad, mlp_grad))
    second_gain_grad, branch_grad, middle_grad, message, qkv_grad = call(
        functools.partial(back_kernel, heads),
        [
            fast((1, width), F32),
            fast(tall, BF16),
            fast((rows, width), F32),
            fast((rows + 16, width), BF16),
            Away(pltpu.HBM((3 * local, width), F32)),
        ],
        [
            place,
            *middles,
            *means,
            *scales,
            *parts,
            *fars,
            cot_all,
            second_row,
            attn_weight,
            qkv,
            exact_a,
            exact_b,
            lse_a,
            lse_b,
            qkv_t,
            cosine,
            sine,
            first_input,
            first_gain[None, :],
        ],
        scratch=[
            ((3 * local, total_rows), BF16),
            ((local, total_rows), BF16),
            ((8, total_rows), F32),
            ((total_rows, HEAD), BF16),
            ((total_rows, HEAD), BF16),
            ((total_rows, HEAD), F32),
            ((total_rows, HEAD), F32),
            ((3 * local, width), F32),
        ],
        copies=4,
        flops=2 * total_rows * local * (4 * width + 20 * total_rows),
        cells=heads * total_rows * total_rows,
    )
    (mine,) = call(
        sum_kernel, [fast((rows + 16, width), BF16)], [message, swap(message, 1)], flops=rows * width
    )
    far = swap(mine, 2)
    out_far, att_b, _ = lax.optimization_barrier((out_far, att_b, mine))
    attn_grad, output = call(
        output_kernel,
        [Away(pltpu.HBM((local, width), F32)), jax.ShapeDtypeStruct((rows, width), BF16)],
        [att_a, att_b, branch_grad, own_middle, out_part, out_far],
        scratch=[((local, width), F32)],
        copies=2,
        flops=2 * total_rows * width * local,
    )
    tokens_grad, first_gain_grad = call(
        last_kernel,
        [jax.ShapeDtypeStruct((rows, width), BF16), jax.ShapeDtypeStruct((1, width), F32)],
        [mine, far, tokens, first_gain[None, :], middle_grad],
        flops=16 * rows * width,
    )
    return (
        output,
        tokens_grad,
        first_gain_grad[0],
        jnp.transpose(qkv_grad.reshape(3, local, width), (2, 0, 1)),
        attn_grad,
        second_gain_grad[0],
        jnp.transpose(in_grad.reshape(2, units, width), (2, 0, 1)),
        mlp_grad,
    )


def body(sizes, tokens, *rest):
    spots, lanes = sizes["ctx"], sizes["wt"]
    rows = tokens.shape[0]
    small = spots * rows <= REPLICATED_TOKENS and rows % 128 == 0 and (spots * rows) % 256 == 0
    if small and lanes == 4 and spots == 8:
        return replicated_body(spots, tokens, *rest)
    return split_body(tokens, *rest)


def solution(mesh):
    return jax.shard_map(
        functools.partial(body, dict(mesh.shape)),
        mesh=mesh,
        in_specs=(
            P("ctx", None),
            P(),
            P(None, None, "wt"),
            P("wt", None),
            P(),
            P(None, None, "wt"),
            P("wt", None),
            P("ctx", None),
        ),
        out_specs=(
            P("ctx", None),
            P("ctx", None),
            P(),
            P(None, None, "wt"),
            P("wt", None),
            P(),
            P(None, None, "wt"),
            P("wt", None),
        ),
        check_vma=False,
    )
```

```python
import functools

import jax
import jax.numpy as jnp
from jax import lax
from jax.experimental import pallas as pl
from jax.experimental.pallas import tpu as pltpu
from jax.sharding import PartitionSpec as P

HEAD = 64


rope_base = 160000.0
norm_epsilon = 1e-05


def layer_norm(values):
    center = values - jnp.mean(values, axis=-1, keepdims=True)
    return center * lax.rsqrt(jnp.mean(center * center, axis=-1, keepdims=True) + norm_epsilon)


def rotate(values, positions, direction):
    half_width = values.shape[-1] // 2
    frequency = rope_base ** (
        -(jnp.arange(half_width).astype(jnp.float32) * 2.0 / values.shape[-1])
    )
    angles = positions[:, None] * frequency[None, :]
    cosine_part = jnp.cos(angles)[:, None, :]
    sine_part = jnp.sin(angles)[:, None, :]
    lower_half = values[..., :half_width]
    upper_half = values[..., half_width:]
    return jnp.concatenate(
        [
            lower_half * cosine_part - direction * upper_half * sine_part,
            upper_half * cosine_part + direction * lower_half * sine_part,
        ],
        axis=-1,
    )


def block_size_for(shard_rows):
    candidate = shard_rows * max(1, 1024 // shard_rows)
    return candidate


def score_terms(
    query_block, grad_block, logsum_block, delta_block, key_block, value_block, score_scale
):
    scores = (
        jnp.einsum("thd,shd->ths", query_block, key_block, preferred_element_type=jnp.float32)
        * score_scale
    )
    chances = jnp.exp(scores - logsum_block[..., None])
    chance_grad = jnp.einsum(
        "thd,shd->ths", grad_block, value_block, preferred_element_type=jnp.float32
    )
    score_grad = (chances * (chance_grad - delta_block[..., None])).astype(jnp.bfloat16)
    return (chances.astype(jnp.bfloat16), score_grad)


def split_body(
    tokens, first_gain, qkv_weight, attn_weight, second_gain, in_weight, mlp_weight, cotangent
):
    row_count = tokens.shape[0]
    local_width = qkv_weight.shape[2]
    heads_here = local_width // HEAD
    score_scale = HEAD ** (-0.5)
    positions = (lax.axis_index("ctx") * row_count + jnp.arange(row_count, dtype=jnp.int32)).astype(
        jnp.float32
    )
    inputs = tokens.astype(jnp.float32)
    normed_first, first_pull = jax.vjp(layer_norm, inputs)
    first_input = (normed_first * first_gain).astype(jnp.bfloat16)
    projected = jnp.einsum(
        "td,dsh->tsh", first_input, qkv_weight, preferred_element_type=jnp.float32
    )
    shaped = projected.reshape(row_count, 3, heads_here, HEAD)
    query_rows = rotate(shaped[:, 0], positions, 1.0).astype(jnp.bfloat16)
    key_rows = rotate(shaped[:, 1], positions, 1.0).astype(jnp.bfloat16)
    value_rows = shaped[:, 2].astype(jnp.bfloat16)
    key_flat = key_rows.reshape(row_count, local_width)
    value_flat = value_rows.reshape(row_count, local_width)
    start_state = (
        jnp.full((row_count, heads_here), -1e30, jnp.float32),
        jnp.zeros((row_count, heads_here), jnp.float32),
        jnp.zeros((row_count, heads_here, HEAD), jnp.float32),
    )
    key_piece = lax.all_gather(key_flat, "ctx", axis=0, tiled=True)
    value_piece = lax.all_gather(value_flat, "ctx", axis=0, tiled=True)
    piece_rows = key_piece.shape[0]
    block_size = block_size_for(row_count)
    key_blocks = key_piece.reshape(piece_rows // block_size, block_size, heads_here, HEAD)
    value_blocks = value_piece.reshape(piece_rows // block_size, block_size, heads_here, HEAD)

    def forward_visit(state, block_item):
        running_max, running_sum, weighted = state
        key_block, value_block = block_item
        scores = (
            jnp.einsum("thd,shd->ths", query_rows, key_block, preferred_element_type=jnp.float32)
            * score_scale
        )
        new_max = jnp.maximum(running_max, jnp.max(scores, axis=-1))
        factor = jnp.exp(running_max - new_max)
        exponent = jnp.exp(scores - new_max[..., None])
        running_sum = running_sum * factor + jnp.sum(exponent, axis=-1)
        weighted = weighted * factor[..., None] + jnp.einsum(
            "ths,shd->thd",
            exponent.astype(jnp.bfloat16),
            value_block,
            preferred_element_type=jnp.float32,
        )
        return ((new_max, running_sum, weighted), None)

    result = lax.scan(forward_visit, start_state, (key_blocks, value_blocks))
    running_max, running_sum, weighted = result[0]
    attended_exact = weighted / running_sum[..., None]
    logsum = running_max + jnp.log(running_sum)
    attended = attended_exact.astype(jnp.bfloat16).reshape(row_count, local_width)
    branch = lax.psum(
        jnp.dot(attended, attn_weight, preferred_element_type=jnp.float32).astype(jnp.bfloat16),
        "wt",
    ).astype(jnp.float32)
    middle = inputs + branch
    normed_second, second_pull = jax.vjp(layer_norm, middle)
    second_input = (normed_second * second_gain).astype(jnp.bfloat16)
    gate_up = jnp.einsum("td,dsf->tsf", second_input, in_weight, preferred_element_type=jnp.float32)

    def activate(pair):
        return jax.nn.gelu(pair[:, 0], approximate=False) * pair[:, 1]

    hidden_exact, activate_back = jax.vjp(activate, gate_up)
    hidden = hidden_exact.astype(jnp.bfloat16)
    mlp_branch = lax.psum(
        jnp.dot(hidden, mlp_weight, preferred_element_type=jnp.float32).astype(jnp.bfloat16), "wt"
    ).astype(jnp.float32)
    output = (middle + mlp_branch).astype(jnp.bfloat16)
    hidden_grad = jnp.einsum("td,fd->tf", cotangent, mlp_weight, preferred_element_type=jnp.float32)
    mlp_weight_grad = jnp.einsum("tf,td->fd", hidden, cotangent, preferred_element_type=jnp.float32)
    gate_up_grad = activate_back(hidden_grad)[0].astype(jnp.bfloat16)
    second_part = jnp.einsum(
        "tsf,dsf->td", gate_up_grad, in_weight, preferred_element_type=jnp.float32
    )
    in_weight_grad = jnp.einsum(
        "td,tsf->dsf", second_input, gate_up_grad, preferred_element_type=jnp.float32
    )
    second_grad = lax.psum(second_part.astype(jnp.bfloat16), "wt").astype(jnp.float32)
    second_gain_grad = jnp.sum(second_grad * normed_second, axis=0)
    middle_grad = cotangent.astype(jnp.float32) + second_pull(second_grad * second_gain)[0]
    branch_grad = middle_grad.astype(jnp.bfloat16)
    attended_grad = jnp.einsum(
        "td,hd->th", branch_grad, attn_weight, preferred_element_type=jnp.float32
    )
    attn_weight_grad = jnp.einsum(
        "th,td->hd", attended, branch_grad, preferred_element_type=jnp.float32
    )
    grad_rows = attended_grad.astype(jnp.bfloat16).reshape(row_count, heads_here, HEAD)
    row_delta = jnp.sum(grad_rows.astype(jnp.float32) * attended_exact, axis=-1)
    zero_rows = jnp.zeros((row_count, heads_here, HEAD), jnp.float32)
    query_acc = zero_rows
    key_piece = lax.all_gather(key_flat, "ctx", axis=0, tiled=True)
    value_piece = lax.all_gather(value_flat, "ctx", axis=0, tiled=True)
    piece_rows = key_piece.shape[0]
    block_size = block_size_for(row_count)
    key_blocks = key_piece.reshape(piece_rows // block_size, block_size, heads_here, HEAD)
    value_blocks = value_piece.reshape(piece_rows // block_size, block_size, heads_here, HEAD)

    def backward_visit(partial_value, block_item):
        key_block, value_block = block_item
        chance_low, score_grad = score_terms(
            query_rows, grad_rows, logsum, row_delta, key_block, value_block, score_scale
        )
        partial_value = (
            partial_value
            + jnp.einsum("ths,shd->thd", score_grad, key_block, preferred_element_type=jnp.float32)
            * score_scale
        )
        key_term = (
            jnp.einsum("ths,thd->shd", score_grad, query_rows, preferred_element_type=jnp.float32)
            * score_scale
        )
        value_term = jnp.einsum(
            "ths,thd->shd", chance_low, grad_rows, preferred_element_type=jnp.float32
        )
        return (partial_value, (key_term, value_term))

    query_acc, terms = lax.scan(backward_visit, query_acc, (key_blocks, value_blocks))
    key_total = terms[0].reshape(piece_rows, local_width)
    value_total = terms[1].reshape(piece_rows, local_width)
    key_sum, value_sum = (
        lax.psum_scatter(key_total, "ctx", scatter_dimension=0, tiled=True),
        lax.psum_scatter(value_total, "ctx", scatter_dimension=0, tiled=True),
    )
    key_grad = key_sum.reshape(row_count, heads_here, HEAD)
    value_grad = value_sum.reshape(row_count, heads_here, HEAD)
    query_back = rotate(query_acc, positions, -1.0)
    key_back = rotate(key_grad, positions, -1.0)
    projected_grad = (
        jnp.stack([query_back, key_back, value_grad], axis=1)
        .reshape(row_count, 3, local_width)
        .astype(jnp.bfloat16)
    )
    first_part = jnp.einsum(
        "tsh,dsh->td", projected_grad, qkv_weight, preferred_element_type=jnp.float32
    )
    qkv_weight_grad = jnp.einsum(
        "td,tsh->dsh", first_input, projected_grad, preferred_element_type=jnp.float32
    )
    first_grad = lax.psum(first_part.astype(jnp.bfloat16), "wt").astype(jnp.float32)
    first_gain_grad = jnp.sum(first_grad * normed_first, axis=0)
    tokens_grad = (middle_grad + first_pull(first_grad * first_gain)[0]).astype(jnp.bfloat16)
    summed = lax.psum(
        (
            first_gain_grad,
            qkv_weight_grad,
            attn_weight_grad,
            second_gain_grad,
            in_weight_grad,
            mlp_weight_grad,
        ),
        "ctx",
    )
    return (output, tokens_grad, summed[0], summed[1], summed[2], summed[3], summed[4], summed[5])


F32 = jnp.float32
BF16 = jnp.bfloat16
NT = (((1,), (1,)), ((), ()))
TN = (((0,), (0,)), ((), ()))
REPLICATED_TOKENS = 2048


def mm(a, b, dims=(((1,), (0,)), ((), ()))):
    return lax.dot_general(a, b, dims, preferred_element_type=F32)


def norm_parts(values):
    return norm_stats(values)[:2]


def norm_stats(values):
    mean = jnp.mean(values, axis=-1, keepdims=True)
    center = values - mean
    scale = lax.rsqrt(jnp.mean(center * center, axis=-1, keepdims=True) + norm_epsilon)
    return center * scale, scale, mean


def norm_back(grad, normed, scale):
    mean_grad = jnp.mean(grad, axis=-1, keepdims=True)
    mean_both = jnp.mean(grad * normed, axis=-1, keepdims=True)
    return scale * (grad - mean_grad - normed * mean_both)


def fast(shape, dtype):
    return pltpu.VMEM(shape, dtype)


class Away:
    def __init__(self, value):
        self.value = value


def call(kernel, outs, args, scratch=(), copies=0, flops=0, cells=0, room=16):
    in_specs, values = [], []
    for arg in args:
        value = arg.value if isinstance(arg, Away) else arg
        if value.dtype == jnp.int32:
            in_specs.append(pl.BlockSpec(memory_space=pltpu.SMEM))
            values.append(value)
            continue
        space = pltpu.HBM if isinstance(arg, Away) else pltpu.VMEM
        in_specs.append(pl.BlockSpec(memory_space=space))
        values.append(pltpu.with_memory_space_constraint(value, space))
    out_specs = [
        pl.BlockSpec(memory_space=pltpu.HBM if isinstance(o, Away) else pltpu.VMEM) for o in outs
    ]
    moved = sum(a.size * a.dtype.itemsize for a in values)
    return pl.pallas_call(
        kernel,
        out_shape=[o.value if isinstance(o, Away) else o for o in outs],
        in_specs=in_specs,
        out_specs=out_specs,
        scratch_shapes=[pltpu.VMEM(shape, dtype) for shape, dtype in scratch]
        + ([pltpu.SemaphoreType.DMA((copies,))] if copies else []),
        compiler_params=pltpu.CompilerParams(vmem_limit_bytes=room * 1024 * 1024),
        cost_estimate=pl.CostEstimate(
            flops=flops, bytes_accessed=moved if flops else 0, transcendentals=cells
        ),
    )(*values)


class Mover:
    def __init__(self, sems):
        self.sems, self.count, self.results = sems, 0, []

    def load(self, source, target):
        copy = pltpu.make_async_copy(source, target, self.sems.at[self.count])
        self.count += 1
        copy.start()
        return copy

    def store(self, source, target):
        self.results.append(self.load(source, target))

    def finish(self):
        for copy in self.results:
            copy.wait()


def wait_all(copies):
    for copy in copies:
        copy.wait()


def load_pieces(move, place, target, own, near, far, ids):
    here, core = place[0], place[1]
    rows = own.shape[0]
    half = rows // 2
    copies = [move.load(own, target.at[pl.ds(pl.multiple_of(here * rows, rows), rows), :])]
    for pieces, side in ((near, core), (far, 1 - core)):
        for ref, steps in zip(pieces, ids):
            for i, step in enumerate(steps):
                if step:
                    spot = jnp.bitwise_xor(here, step) * rows + side * half
                    copies.append(
                        move.load(ref.at[i], target.at[pl.ds(pl.multiple_of(spot, half), half), :])
                    )
    return copies


def loop(count, step, unroll=1):
    def some(i, carry):
        for j in range(unroll):
            step(i * unroll + j)
        return carry

    if unroll == count:
        some(0, 0)
    else:
        lax.fori_loop(0, count // unroll, some, 0)


def part_of(i, size):
    if isinstance(i, int):
        return slice(i * size, (i + 1) * size)
    return pl.ds(pl.multiple_of(i * size, size), size)


def attend(heads, first, qkv, att, exact, lse, keys, chunk=256):
    def one_head(head):
        keys[...] = qkv[part_of(heads + head, HEAD), :].T
        rows = part_of(head, HEAD)

        def one_chunk(i):
            at = part_of(i, chunk)
            scores = mm(keys[...], qkv[rows, part_of(i + first // chunk, chunk)])
            top = jnp.max(scores, axis=0, keepdims=True)
            exponent = jnp.exp(scores - top)
            total = jnp.sum(exponent, axis=0, keepdims=True)
            weighted = mm(qkv[part_of(2 * heads + head, HEAD), :], exponent.astype(BF16))
            weighted = weighted / total
            exact[rows, at] = weighted
            att[rows, at] = weighted.astype(BF16)
            lse[pl.ds(head, 1), at] = top + jnp.log(total)

        loop(att.shape[1] // chunk, one_chunk, att.shape[1] // chunk)

    lse[...] = jnp.zeros_like(lse)
    loop(heads, one_head, heads)


def project_kernel(heads, ids, place, own, *refs):
    count = len(ids)
    near, far, refs = refs[:count], refs[count : 2 * count], refs[2 * count :]
    gain, weight_in, cosine, sine, tok_out, first, qkv, att, exact, lse, tok, weight, keys, sems = refs
    move = Mover(sems)
    local = heads * HEAD
    tokens = tok.shape[0]
    pieces = load_pieces(move, place, tok, own, near, far, ids)
    weight_load = move.load(weight_in, weight)
    wait_all(pieces)
    move.store(tok, tok_out)
    weight_load.wait()
    chunk = 256

    def one_chunk(i):
        at = part_of(i, chunk)
        normed, _ = norm_parts(tok[at, :].astype(F32))
        rounded = (normed * gain[...]).astype(BF16)
        first[at, :] = rounded
        raw = mm(weight[...], rounded, NT)
        cos, sin = cosine[:, at], sine[:, at]
        for part in range(2):
            for head in range(heads):
                base = part * local + head * HEAD
                lower = raw[base : base + HEAD // 2]
                upper = raw[base + HEAD // 2 : base + HEAD]
                turned = jnp.concatenate(
                    [lower * cos - upper * sin, upper * cos + lower * sin], axis=0
                ).astype(BF16)
                if part == 0:
                    turned = turned * jnp.asarray(HEAD ** (-0.5), BF16)
                qkv[base : base + HEAD, at] = turned
        qkv[2 * local :, at] = raw[2 * local :].astype(BF16)

    loop(tokens // chunk, one_chunk, 2)
    attend(heads, 0, qkv, att, exact, lse, keys)
    move.finish()


def queries_kernel(heads, qkv, att, exact, lse, keys):
    attend(heads, qkv.shape[1] - att.shape[1], qkv, att, exact, lse, keys)


def cdf_terms(gate):
    half = 0.5 * (1.0 + lax.erf(gate * (0.5**0.5)))
    slope = half + gate * (jnp.exp(-0.5 * gate * gate) * 0.3989422804014327)
    return half, slope


def mlp_kernel(turn, ids, place, tok_in, *refs):
    count = len(ids)
    if turn == 0:
        cot_own, near, far = refs[0], refs[1 : 1 + count], refs[1 + count : 1 + 2 * count]
        refs = refs[1 + 2 * count :]
        atts, attns, (in_own, in_side, in_rest, mlp_own, rest_far) = refs[:4], refs[4:7], refs[7:12]
        units_here = mlp_own.shape[0]
        attns = [*attns[:2], rest_far.at[units_here:, :], attns[2].at[units_here:, :]]
        gain, cot, attn, w_in, w_mlp, tok_next = refs[12:18]
        refs = refs[18:]
    else:
        cot, atts, (gain, attn, w_in, w_mlp), refs = refs[0], refs[1:5], refs[5:9], refs[9:]
        (mid_before, out_before), refs = refs[:2], refs[2:]
    middle_ref, second_ref, hidden_ref, gate_ref, part_ref, mean_ref, scale_ref = refs[:7]
    mid_ref, out_ref, refs = refs[7], refs[8], refs[9:]
    tokens = middle_ref.shape[0]
    sems = refs[-1]
    move = Mover(sems)
    here, quarter, side = place[0], place[2], place[3]
    local = atts[0].shape[0]
    units = hidden_ref.shape[0]
    begin = turn * tokens
    first_loads = []
    if turn == 0:
        tok, refs = refs[0], refs[1:]
        first_loads.append(move.load(tok_in.at[:tokens, :], tok))
    else:
        tok = tok_in
    att, hidden_v, gate_v = refs[:3]
    for p in range(4):
        spot = pl.ds(pl.multiple_of(jnp.bitwise_xor(quarter, p) * local, local), local)
        first_loads.append(move.load(atts[p], att.at[spot, :]))
        if turn == 0:
            first_loads.append(move.load(attns[p], attn.at[spot, :]))
    in_loads, mlp_loads = [], []
    if turn == 0:
        row = here % 2
        for part in range(2):
            spot = pl.ds(pl.multiple_of((side + 2 * part) * units, units), units)
            rows = in_own.at[part * units : (part + 1) * units, :]
            in_loads.append(move.load(rows, w_in.at[spot, :]))
        for part, source in ((row, in_side), (1 - row, in_rest)):
            spot = pl.ds(pl.multiple_of((1 - side + 2 * part) * units, units), units)
            in_loads.append(move.load(source, w_in.at[spot, :]))
        for source, r in ((mlp_own, side), (rest_far, 1 - side)):
            spot = pl.ds(pl.multiple_of(r * units, units), units)
            mlp_loads.append(move.load(source.at[:units, :], w_mlp.at[spot, :]))
        mlp_loads += load_pieces(move, place, cot, cot_own, near, far, ids)
        mlp_loads.append(move.load(tok_in.at[tokens:, :], tok_next))
    wait_all(first_loads)
    chunk = 512

    def one_chunk(i):
        at = part_of(i, chunk)
        middle = tok[at, :].astype(F32) + mm(att[:, at].T, attn[...])
        middle_ref[at, :] = middle
        normed, scale_ref[at, :], mean_ref[at, :] = norm_stats(middle)
        second = (normed * gain[...]).astype(BF16)
        second_ref[at, :] = second

        if i == 0:
            wait_all(in_loads)

        gate_up = mm(w_in[...], second, NT)
        gate, up = gate_up[: 2 * units], gate_up[2 * units :]
        half, slope = cdf_terms(gate)
        active = gate * half
        hidden_v[:, at] = (active * up).astype(BF16)

        if i == 0:
            wait_all(mlp_loads)

        back = mm(w_mlp[...], cot[part_of(i + begin // chunk, chunk), :], NT)
        grads = jnp.concatenate([slope * up * back, active * back], axis=0).astype(BF16)
        gate_v[:, at] = grads
        part_ref[at, :] = mm(grads.T, w_in[...]).astype(BF16)

    loop(tokens // chunk, one_chunk, tokens // chunk)
    mine = pl.ds(pl.multiple_of(side * units, units), units)
    mine_up = pl.ds(pl.multiple_of(side * units + 2 * units, units), units)
    hidden_ref[...] = hidden_v[mine, :]
    gate_ref[:units, :] = gate_v[mine, :]
    gate_ref[units:, :] = gate_v[mine_up, :]
    rows = out_ref.shape[0]
    spots = tokens // rows
    mid_ref[...] = mid_before[...] if turn else jnp.zeros_like(mid_ref)
    out_ref[...] = out_before[...] if turn else jnp.zeros_like(out_ref)

    @pl.when(here // spots == turn)
    def _():
        own = pl.ds(pl.multiple_of((here - turn * spots) * rows, rows), rows)
        mid_ref[...] = middle_ref[own, :]
        out_ref[...] = mm(hidden_v[:, own].T, w_mlp[...]).astype(BF16)


def two_rows(row):
    high = row.astype(BF16).astype(F32)
    spots = lax.broadcasted_iota(jnp.int32, (16, row.shape[1]), 0)
    rows = jnp.where(spots == 0, high, jnp.where(spots == 1, row - high, 0.0))
    return rows.astype(BF16)


def sum_rows(rows):
    return jnp.sum(rows.astype(F32), axis=0, keepdims=True)


def back_kernel(heads, place, *refs):
    middles, means, scales, refs = refs[:2], refs[2:4], refs[4:6], refs[6:]
    parts, fars, refs = refs[:2], refs[2:4], refs[4:]
    cot, gain, attn, qkv, refs = refs[0], refs[1], refs[2], refs[3], refs[4:]
    exacts, lses, refs = refs[:2], refs[2:4], refs[4:]
    weight, cosine, sine, refs = refs[0], refs[1], refs[2], refs[3:]
    first_in, first_gain, gain_v, branch, own_v, message, qkv_out, refs = *refs[:7], refs[7:]
    grad_v, back_rows, lse, keys, values, key_grad, value_grad, qkv_grad, sems = refs
    move = Mover(sems)
    here = place[0]
    turns = middles[0].shape[0]
    tokens = 2 * turns
    rows = own_v.shape[0]
    local = heads * HEAD
    spots = turns // rows
    gain_v[...] = jnp.zeros_like(gain_v)

    def norm_block(turn, b):
        here_at = pl.ds(pl.multiple_of(b * rows, rows), rows)
        at = pl.ds(pl.multiple_of((b + turn * spots) * rows, rows), rows)
        second = parts[turn][here_at, :].astype(F32) + fars[turn][here_at, :].astype(F32)
        scale = scales[turn][here_at, :]
        normed = (middles[turn][here_at, :] - means[turn][here_at, :]) * scale
        gain_v[...] += jnp.sum(second * normed, axis=0, keepdims=True)
        grad = cot[at, :].astype(F32) + norm_back(second * gain[...], normed, scale)
        branch[at, :] = grad.astype(BF16)

        @pl.when(b + turn * spots == here)
        def _():
            own_v[...] = grad

    for turn in range(2):
        loop(spots, functools.partial(norm_block, turn), 2)
    chunk = 256

    def grad_chunk(i):
        at = part_of(i, chunk)
        back_rows[:, at] = mm(attn[...], branch[at, :], NT).astype(BF16)

    loop(tokens // chunk, grad_chunk, 2)
    for turn in range(2):
        lse[:, turn * turns : (turn + 1) * turns] = lses[turn][...]
    scale = HEAD ** (-0.5)

    def turn_back(grad, cos, sin):
        lower, upper = grad[: HEAD // 2], grad[HEAD // 2 :]
        return jnp.concatenate(
            [lower * cos + upper * sin, upper * cos - lower * sin], axis=0
        ).astype(BF16)

    def one_head(head):
        rows_q, rows_k, rows_v = [part_of(p * heads + head, HEAD) for p in range(3)]
        keys[...] = qkv[rows_k, :].T
        values[...] = qkv[rows_v, :].T
        key_grad[...] = jnp.zeros_like(key_grad)
        value_grad[...] = jnp.zeros_like(value_grad)

        def one_chunk(i):
            at = part_of(i, chunk)
            query = qkv[rows_q, at]
            out_grad = back_rows[rows_q, at]
            chances = jnp.exp(mm(keys[...], query) - lse[pl.ds(head, 1), at])
            chance_grad = mm(values[...], out_grad)
            exact = exacts[i * chunk // turns][rows_q, part_of(i % (turns // chunk), chunk)]
            delta = jnp.sum(out_grad.astype(F32) * exact, axis=0, keepdims=True)
            score_grad = (chances * (chance_grad - delta)).astype(BF16)
            query_grad = mm(qkv[rows_k, :], score_grad) * scale
            key_grad[...] += mm(query, score_grad, NT)
            value_grad[...] += mm(out_grad, chances.astype(BF16), NT)
            grad_v[rows_q, at] = turn_back(query_grad, cosine[:, at], sine[:, at])

        loop(tokens // chunk, one_chunk, tokens // chunk)
        grad_v[rows_k, :] = turn_back(key_grad[...], cosine[...], sine[...])
        grad_v[rows_v, :] = value_grad[...].astype(BF16)

    loop(heads, one_head, heads)
    own = pl.ds(pl.multiple_of(here * rows, rows), rows)
    message[:rows, :] = mm(grad_v[:, own].T, weight[...]).astype(BF16)
    gain_row = jnp.zeros_like(gain_v)
    for part in range(3):
        at = part_of(part, local)
        product = mm(grad_v[at, :], first_in[...])
        qkv_grad[at, :] = product
        move.store(qkv_grad.at[at, :], qkv_out.at[at, :])
        gain_row += jnp.sum(weight[at, :].astype(F32) * product, axis=0, keepdims=True)
    message[rows:, :] = two_rows(gain_row / first_gain[...])
    move.finish()


def sum_kernel(message, far, out):
    rows = out.shape[0] - 16
    out[:rows, :] = (message[:rows, :].astype(F32) + far[:rows, :].astype(F32)).astype(BF16)
    out[rows:, :] = two_rows(sum_rows(message[rows:, :]) + sum_rows(far[rows:, :]))


def last_kernel(mine, far, tokens, gain, middle_grad, tokens_grad, gain_grad):
    rows = tokens.shape[0]
    gain_grad[...] = (sum_rows(mine[rows:, :]) + sum_rows(far[rows:, :]))[0]
    first_grad = mine[:rows, :].astype(F32) + far[:rows, :].astype(F32)
    normed, scale = norm_parts(tokens[...].astype(F32))
    back = norm_back(first_grad * gain[...], normed, scale)
    tokens_grad[...] = (middle_grad[...] + back).astype(BF16)


def products_kernel(gate_a, gate_b, hidden_a, hidden_b, second_a, second_b, cot, *refs):
    in_out, mlp_out, in_grad, mlp_grad, sems = refs
    move = Mover(sems)
    tokens = second_a.shape[0]
    units = hidden_a.shape[0]
    for part in range(2):
        at = part_of(part, units)
        in_grad[at, :] = mm(gate_a[at, :], second_a[...]) + mm(gate_b[at, :], second_b[...])
        move.store(in_grad.at[at, :], in_out.at[at, :])
    mlp_grad[...] = mm(hidden_a[...], cot[:tokens, :]) + mm(hidden_b[...], cot[tokens:, :])
    move.store(mlp_grad, mlp_out)
    move.finish()


def output_kernel(att_a, att_b, branch, middle, part, far, attn_out, output, attn_grad, sems):
    move = Mover(sems)
    tokens = att_a.shape[1]
    attn_grad[...] = mm(att_a[...], branch[:tokens, :]) + mm(att_b[...], branch[tokens:, :])
    move.store(attn_grad, attn_out)
    branch_sum = part[...].astype(F32) + far[...].astype(F32)
    output[...] = (middle[...] + branch_sum).astype(BF16)
    move.finish()


def over_ctx(value, step, spots):
    return lax.ppermute(value, "ctx", [(spot, spot ^ step) for spot in range(spots)])


def swap(value, mask):
    return lax.ppermute(value, "wt", [(spot, spot ^ mask) for spot in range(4)])


def half_of(block, core):
    half = block.shape[0] // 2
    return lax.dynamic_slice_in_dim(block, core * half, half, axis=0)


def gather_tokens(block, core, spots):
    half = half_of(block, core)
    steps = [over_ctx(half, step, spots) for step in range(2, spots, 2)]
    first = jnp.stack([half, steps[0]])
    rest = jnp.stack(steps[1:])
    first_y = over_ctx(first, 1, spots)
    rest_y = over_ctx(rest, 1, spots)
    near = [first, first_y, rest, rest_y]
    later = list(range(4, spots, 2))
    ids = ((0, 2), (1, 3), tuple(later), tuple(step + 1 for step in later))
    return near, [swap(piece, 1) for piece in near], ids, steps


def gather_cotangent(block, core, spots, after, gate):
    near = half_of(block, core)[None]
    ids, step = (0,), 1
    while step < spots:
        if step == 2:
            near, _ = lax.optimization_barrier((near, after))
        near = jnp.concatenate([near, over_ctx(near, step, spots)], axis=0)
        ids += tuple(i + step for i in ids)
        step *= 2
    near, _ = lax.optimization_barrier((near, gate))
    return [near], [swap(near, 1)], (ids,)


def replicated_body(
    spots,
    tokens,
    first_gain,
    qkv_weight,
    attn_weight,
    second_gain,
    in_weight,
    mlp_weight,
    cotangent,
):
    rows, width = tokens.shape
    total_rows = rows * spots
    local = qkv_weight.shape[2]
    heads = local // HEAD
    units = mlp_weight.shape[0]
    here, quarter = lax.axis_index("ctx"), lax.axis_index("wt")
    core, side = quarter % 2, quarter // 2
    place = jnp.stack([here, core, quarter, side]).astype(jnp.int32)
    frequency = rope_base ** (-(jnp.arange(HEAD // 2).astype(F32) * 2.0 / HEAD))
    angles = frequency[:, None] * jnp.arange(total_rows).astype(F32)[None, :]
    cosine, sine = jnp.cos(angles), jnp.sin(angles)
    qkv_t = jnp.transpose(qkv_weight, (1, 2, 0)).reshape(3 * local, width)
    in_t = jnp.transpose(in_weight, (1, 2, 0)).reshape(2 * units, width)

    near, far, ids, steps = gather_tokens(tokens, core, spots)
    attn_core = swap(attn_weight, 1)
    in_part = lax.dynamic_index_in_dim(in_t.reshape(2, units, width), here % 2, 0, keepdims=False)
    in_side = swap(in_part, 2)
    in_rest = over_ctx(in_side, 1, spots)
    rest = jnp.concatenate([mlp_weight, attn_weight], axis=0)
    rest_side = swap(rest, 2)
    rest_both = swap(rest_side, 1)
    half_rows = total_rows // 2
    tall, wide = (total_rows, width), (half_rows, width)
    cells = heads * total_rows * half_rows
    tok_all, first_input, qkv, att_a, exact_a, lse_a = call(
        functools.partial(project_kernel, heads, ids),
        [
            Away(pltpu.HBM(tall, BF16)),
            fast(tall, BF16),
            fast((3 * local, total_rows), BF16),
            fast((local, half_rows), BF16),
            fast((local, half_rows), F32),
            fast((8, half_rows), F32),
        ],
        [
            place,
            Away(tokens),
            *map(Away, near),
            *map(Away, far),
            first_gain[None, :],
            Away(qkv_t),
            cosine,
            sine,
        ],
        scratch=[(tall, BF16), ((3 * local, width), BF16), ((total_rows, HEAD), BF16)],
        copies=20,
    )
    side_a = swap(att_a, 2)
    att_b, exact_b, lse_b = call(
        functools.partial(queries_kernel, heads),
        [
            fast((local, half_rows), BF16),
            fast((local, half_rows), F32),
            fast((8, half_rows), F32),
        ],
        [qkv],
        scratch=[((total_rows, HEAD), BF16)],
    )
    cot_near, cot_far, cot_ids = gather_cotangent(cotangent, core, spots, steps[-1], att_a)
    side_a, _ = lax.optimization_barrier((side_a, att_b))
    atts_a = [att_a, swap(att_a, 1), side_a, swap(side_a, 1)]
    halves = [
        fast(wide, F32),
        fast(wide, BF16),
        fast((units, half_rows), BF16),
        fast((2 * units, half_rows), BF16),
        fast(wide, BF16),
        fast((half_rows, 1), F32),
        fast((half_rows, 1), F32),
        fast((rows, width), F32),
        fast((rows, width), BF16),
    ]
    room = [
        ((4 * local, half_rows), BF16),
        ((2 * units, half_rows), BF16),
        ((4 * units, half_rows), BF16),
    ]
    second_row = second_gain[None, :]
    cot_all, attn_all, in_all, mlp_all, tok_b, *results_a = call(
        functools.partial(mlp_kernel, 0, cot_ids),
        [
            fast(tall, BF16),
            fast((4 * local, width), BF16),
            fast((4 * units, width), BF16),
            fast((2 * units, width), BF16),
            fast(wide, BF16),
            *halves,
        ],
        [
            place,
            *map(Away, [tok_all, cotangent, *cot_near, *cot_far]),
            att_a,
            *map(Away, atts_a[1:]),
            *map(Away, [attn_weight, attn_core, rest_both]),
            *map(Away, [in_t, in_side, in_rest, mlp_weight, rest_side]),
            second_row,
        ],
        scratch=[(wide, BF16), *room],
        copies=32,
        flops=2 * half_rows * width * (4 * local + 10 * units),
        cells=4 * units * half_rows,
        room=20,
    )
    att_core_b = swap(att_b, 1)
    side_b, _ = lax.optimization_barrier((swap(att_b, 2), cot_all))
    atts_b = [att_b, att_core_b, side_b, swap(side_b, 1)]
    results_b = call(
        functools.partial(mlp_kernel, 1, ()),
        halves,
        [
            place,
            tok_b,
            cot_all,
            att_b,
            *map(Away, atts_b[1:]),
            second_row,
            attn_all,
            in_all,
            mlp_all,
            *results_a[7:],
        ],
        scratch=room,
        copies=8,
        flops=2 * half_rows * width * (4 * local + 10 * units),
        cells=4 * units * half_rows,
        room=20,
    )
    middles, seconds, hiddens, gates, parts, means, scales = zip(results_a[:7], results_b[:7])
    own_middle, out_part = results_b[7:]
    fars = [swap(part, 1) for part in parts]
    out_far = swap(out_part, 1)
    in_grad, mlp_grad = call(
        products_kernel,
        [Away(pltpu.HBM((2 * units, width), F32)), Away(pltpu.HBM((units, width), F32))],
        [*gates, *hiddens, *seconds, cot_all],
        scratch=[((2 * units, width), F32), ((units, width), F32)],
        copies=4,
        flops=6 * total_rows * width * units,
    )
    fars, in_grad, mlp_grad = lax.optimization_barrier((fars, in_grad, mlp_grad))
    second_gain_grad, branch_grad, middle_grad, message, qkv_grad = call(
        functools.partial(back_kernel, heads),
        [
            fast((1, width), F32),
            fast(tall, BF16),
            fast((rows, width), F32),
            fast((rows + 16, width), BF16),
            Away(pltpu.HBM((3 * local, width), F32)),
        ],
        [
            place,
            *middles,
            *means,
            *scales,
            *parts,
            *fars,
            cot_all,
            second_row,
            attn_weight,
            qkv,
            exact_a,
            exact_b,
            lse_a,
            lse_b,
            qkv_t,
            cosine,
            sine,
            first_input,
            first_gain[None, :],
        ],
        scratch=[
            ((3 * local, total_rows), BF16),
            ((local, total_rows), BF16),
            ((8, total_rows), F32),
            ((total_rows, HEAD), BF16),
            ((total_rows, HEAD), BF16),
            ((HEAD, total_rows), F32),
            ((HEAD, total_rows), F32),
            ((3 * local, width), F32),
        ],
        copies=4,
        flops=2 * total_rows * local * (4 * width + 20 * total_rows),
        cells=heads * total_rows * total_rows,
    )
    (mine,) = call(
        sum_kernel, [fast((rows + 16, width), BF16)], [message, swap(message, 1)], flops=rows * width
    )
    far = swap(mine, 2)
    out_far, att_b, _ = lax.optimization_barrier((out_far, att_b, mine))
    attn_grad, output = call(
        output_kernel,
        [Away(pltpu.HBM((local, width), F32)), jax.ShapeDtypeStruct((rows, width), BF16)],
        [att_a, att_b, branch_grad, own_middle, out_part, out_far],
        scratch=[((local, width), F32)],
        copies=2,
        flops=2 * total_rows * width * local,
    )
    tokens_grad, first_gain_grad = call(
        last_kernel,
        [jax.ShapeDtypeStruct((rows, width), BF16), jax.ShapeDtypeStruct((width,), F32)],
        [mine, far, tokens, first_gain[None, :], middle_grad],
        flops=16 * rows * width,
    )
    return (
        output,
        tokens_grad,
        first_gain_grad,
        jnp.transpose(qkv_grad.reshape(3, local, width), (2, 0, 1)),
        attn_grad,
        second_gain_grad[0],
        jnp.transpose(in_grad.reshape(2, units, width), (2, 0, 1)),
        mlp_grad,
    )


def body(sizes, tokens, *rest):
    spots, lanes = sizes["ctx"], sizes["wt"]
    rows = tokens.shape[0]
    small = spots * rows <= REPLICATED_TOKENS and rows % 128 == 0 and (spots * rows) % 256 == 0
    if small and lanes == 4 and spots == 8:
        return replicated_body(spots, tokens, *rest)
    return split_body(tokens, *rest)


def solution(mesh):
    return jax.shard_map(
        functools.partial(body, dict(mesh.shape)),
        mesh=mesh,
        in_specs=(
            P("ctx", None),
            P(),
            P(None, None, "wt"),
            P("wt", None),
            P(),
            P(None, None, "wt"),
            P("wt", None),
            P("ctx", None),
        ),
        out_specs=(
            P("ctx", None),
            P("ctx", None),
            P(),
            P(None, None, "wt"),
            P("wt", None),
            P(),
            P(None, None, "wt"),
            P("wt", None),
        ),
        check_vma=False,
    )
```

```python
import functools

import jax
import jax.numpy as jnp
from jax import lax
from jax.experimental import pallas as pl
from jax.experimental.pallas import tpu as pltpu
from jax.sharding import PartitionSpec as P

HEAD = 64


rope_base = 160000.0
norm_epsilon = 1e-05


def layer_norm(values):
    center = values - jnp.mean(values, axis=-1, keepdims=True)
    return center * lax.rsqrt(jnp.mean(center * center, axis=-1, keepdims=True) + norm_epsilon)


def rotate(values, positions, direction):
    half_width = values.shape[-1] // 2
    frequency = rope_base ** (
        -(jnp.arange(half_width).astype(jnp.float32) * 2.0 / values.shape[-1])
    )
    angles = positions[:, None] * frequency[None, :]
    cosine_part = jnp.cos(angles)[:, None, :]
    sine_part = jnp.sin(angles)[:, None, :]
    lower_half = values[..., :half_width]
    upper_half = values[..., half_width:]
    return jnp.concatenate(
        [
            lower_half * cosine_part - direction * upper_half * sine_part,
            upper_half * cosine_part + direction * lower_half * sine_part,
        ],
        axis=-1,
    )


def block_size_for(shard_rows):
    candidate = shard_rows * max(1, 1024 // shard_rows)
    return candidate


def score_terms(
    query_block, grad_block, logsum_block, delta_block, key_block, value_block, score_scale
):
    scores = (
        jnp.einsum("thd,shd->ths", query_block, key_block, preferred_element_type=jnp.float32)
        * score_scale
    )
    chances = jnp.exp(scores - logsum_block[..., None])
    chance_grad = jnp.einsum(
        "thd,shd->ths", grad_block, value_block, preferred_element_type=jnp.float32
    )
    score_grad = (chances * (chance_grad - delta_block[..., None])).astype(jnp.bfloat16)
    return (chances.astype(jnp.bfloat16), score_grad)


def split_body(
    tokens, first_gain, qkv_weight, attn_weight, second_gain, in_weight, mlp_weight, cotangent
):
    row_count = tokens.shape[0]
    local_width = qkv_weight.shape[2]
    heads_here = local_width // HEAD
    score_scale = HEAD ** (-0.5)
    positions = (lax.axis_index("ctx") * row_count + jnp.arange(row_count, dtype=jnp.int32)).astype(
        jnp.float32
    )
    inputs = tokens.astype(jnp.float32)
    normed_first, first_pull = jax.vjp(layer_norm, inputs)
    first_input = (normed_first * first_gain).astype(jnp.bfloat16)
    projected = jnp.einsum(
        "td,dsh->tsh", first_input, qkv_weight, preferred_element_type=jnp.float32
    )
    shaped = projected.reshape(row_count, 3, heads_here, HEAD)
    query_rows = rotate(shaped[:, 0], positions, 1.0).astype(jnp.bfloat16)
    key_rows = rotate(shaped[:, 1], positions, 1.0).astype(jnp.bfloat16)
    value_rows = shaped[:, 2].astype(jnp.bfloat16)
    key_flat = key_rows.reshape(row_count, local_width)
    value_flat = value_rows.reshape(row_count, local_width)
    start_state = (
        jnp.full((row_count, heads_here), -1e30, jnp.float32),
        jnp.zeros((row_count, heads_here), jnp.float32),
        jnp.zeros((row_count, heads_here, HEAD), jnp.float32),
    )
    key_piece = lax.all_gather(key_flat, "ctx", axis=0, tiled=True)
    value_piece = lax.all_gather(value_flat, "ctx", axis=0, tiled=True)
    piece_rows = key_piece.shape[0]
    block_size = block_size_for(row_count)
    key_blocks = key_piece.reshape(piece_rows // block_size, block_size, heads_here, HEAD)
    value_blocks = value_piece.reshape(piece_rows // block_size, block_size, heads_here, HEAD)

    def forward_visit(state, block_item):
        running_max, running_sum, weighted = state
        key_block, value_block = block_item
        scores = (
            jnp.einsum("thd,shd->ths", query_rows, key_block, preferred_element_type=jnp.float32)
            * score_scale
        )
        new_max = jnp.maximum(running_max, jnp.max(scores, axis=-1))
        factor = jnp.exp(running_max - new_max)
        exponent = jnp.exp(scores - new_max[..., None])
        running_sum = running_sum * factor + jnp.sum(exponent, axis=-1)
        weighted = weighted * factor[..., None] + jnp.einsum(
            "ths,shd->thd",
            exponent.astype(jnp.bfloat16),
            value_block,
            preferred_element_type=jnp.float32,
        )
        return ((new_max, running_sum, weighted), None)

    result = lax.scan(forward_visit, start_state, (key_blocks, value_blocks))
    running_max, running_sum, weighted = result[0]
    attended_exact = weighted / running_sum[..., None]
    logsum = running_max + jnp.log(running_sum)
    attended = attended_exact.astype(jnp.bfloat16).reshape(row_count, local_width)
    branch = lax.psum(
        jnp.dot(attended, attn_weight, preferred_element_type=jnp.float32).astype(jnp.bfloat16),
        "wt",
    ).astype(jnp.float32)
    middle = inputs + branch
    normed_second, second_pull = jax.vjp(layer_norm, middle)
    second_input = (normed_second * second_gain).astype(jnp.bfloat16)
    gate_up = jnp.einsum("td,dsf->tsf", second_input, in_weight, preferred_element_type=jnp.float32)

    def activate(pair):
        return jax.nn.gelu(pair[:, 0], approximate=False) * pair[:, 1]

    hidden_exact, activate_back = jax.vjp(activate, gate_up)
    hidden = hidden_exact.astype(jnp.bfloat16)
    mlp_branch = lax.psum(
        jnp.dot(hidden, mlp_weight, preferred_element_type=jnp.float32).astype(jnp.bfloat16), "wt"
    ).astype(jnp.float32)
    output = (middle + mlp_branch).astype(jnp.bfloat16)
    hidden_grad = jnp.einsum("td,fd->tf", cotangent, mlp_weight, preferred_element_type=jnp.float32)
    mlp_weight_grad = jnp.einsum("tf,td->fd", hidden, cotangent, preferred_element_type=jnp.float32)
    gate_up_grad = activate_back(hidden_grad)[0].astype(jnp.bfloat16)
    second_part = jnp.einsum(
        "tsf,dsf->td", gate_up_grad, in_weight, preferred_element_type=jnp.float32
    )
    in_weight_grad = jnp.einsum(
        "td,tsf->dsf", second_input, gate_up_grad, preferred_element_type=jnp.float32
    )
    second_grad = lax.psum(second_part.astype(jnp.bfloat16), "wt").astype(jnp.float32)
    second_gain_grad = jnp.sum(second_grad * normed_second, axis=0)
    middle_grad = cotangent.astype(jnp.float32) + second_pull(second_grad * second_gain)[0]
    branch_grad = middle_grad.astype(jnp.bfloat16)
    attended_grad = jnp.einsum(
        "td,hd->th", branch_grad, attn_weight, preferred_element_type=jnp.float32
    )
    attn_weight_grad = jnp.einsum(
        "th,td->hd", attended, branch_grad, preferred_element_type=jnp.float32
    )
    grad_rows = attended_grad.astype(jnp.bfloat16).reshape(row_count, heads_here, HEAD)
    row_delta = jnp.sum(grad_rows.astype(jnp.float32) * attended_exact, axis=-1)
    zero_rows = jnp.zeros((row_count, heads_here, HEAD), jnp.float32)
    query_acc = zero_rows
    key_piece = lax.all_gather(key_flat, "ctx", axis=0, tiled=True)
    value_piece = lax.all_gather(value_flat, "ctx", axis=0, tiled=True)
    piece_rows = key_piece.shape[0]
    block_size = block_size_for(row_count)
    key_blocks = key_piece.reshape(piece_rows // block_size, block_size, heads_here, HEAD)
    value_blocks = value_piece.reshape(piece_rows // block_size, block_size, heads_here, HEAD)

    def backward_visit(partial_value, block_item):
        key_block, value_block = block_item
        chance_low, score_grad = score_terms(
            query_rows, grad_rows, logsum, row_delta, key_block, value_block, score_scale
        )
        partial_value = (
            partial_value
            + jnp.einsum("ths,shd->thd", score_grad, key_block, preferred_element_type=jnp.float32)
            * score_scale
        )
        key_term = (
            jnp.einsum("ths,thd->shd", score_grad, query_rows, preferred_element_type=jnp.float32)
            * score_scale
        )
        value_term = jnp.einsum(
            "ths,thd->shd", chance_low, grad_rows, preferred_element_type=jnp.float32
        )
        return (partial_value, (key_term, value_term))

    query_acc, terms = lax.scan(backward_visit, query_acc, (key_blocks, value_blocks))
    key_total = terms[0].reshape(piece_rows, local_width)
    value_total = terms[1].reshape(piece_rows, local_width)
    key_sum, value_sum = (
        lax.psum_scatter(key_total, "ctx", scatter_dimension=0, tiled=True),
        lax.psum_scatter(value_total, "ctx", scatter_dimension=0, tiled=True),
    )
    key_grad = key_sum.reshape(row_count, heads_here, HEAD)
    value_grad = value_sum.reshape(row_count, heads_here, HEAD)
    query_back = rotate(query_acc, positions, -1.0)
    key_back = rotate(key_grad, positions, -1.0)
    projected_grad = (
        jnp.stack([query_back, key_back, value_grad], axis=1)
        .reshape(row_count, 3, local_width)
        .astype(jnp.bfloat16)
    )
    first_part = jnp.einsum(
        "tsh,dsh->td", projected_grad, qkv_weight, preferred_element_type=jnp.float32
    )
    qkv_weight_grad = jnp.einsum(
        "td,tsh->dsh", first_input, projected_grad, preferred_element_type=jnp.float32
    )
    first_grad = lax.psum(first_part.astype(jnp.bfloat16), "wt").astype(jnp.float32)
    first_gain_grad = jnp.sum(first_grad * normed_first, axis=0)
    tokens_grad = (middle_grad + first_pull(first_grad * first_gain)[0]).astype(jnp.bfloat16)
    summed = lax.psum(
        (
            first_gain_grad,
            qkv_weight_grad,
            attn_weight_grad,
            second_gain_grad,
            in_weight_grad,
            mlp_weight_grad,
        ),
        "ctx",
    )
    return (output, tokens_grad, summed[0], summed[1], summed[2], summed[3], summed[4], summed[5])


F32 = jnp.float32
BF16 = jnp.bfloat16
NT = (((1,), (1,)), ((), ()))
TN = (((0,), (0,)), ((), ()))
REPLICATED_TOKENS = 2048


def mm(a, b, dims=(((1,), (0,)), ((), ()))):
    return lax.dot_general(a, b, dims, preferred_element_type=F32)


def norm_parts(values):
    return norm_stats(values)[:2]


def norm_stats(values):
    mean = jnp.mean(values, axis=-1, keepdims=True)
    center = values - mean
    scale = lax.rsqrt(jnp.mean(center * center, axis=-1, keepdims=True) + norm_epsilon)
    return center * scale, scale, mean


def norm_back(grad, normed, scale):
    mean_grad = jnp.mean(grad, axis=-1, keepdims=True)
    mean_both = jnp.mean(grad * normed, axis=-1, keepdims=True)
    return scale * (grad - mean_grad - normed * mean_both)


def fast(shape, dtype):
    return pltpu.VMEM(shape, dtype)


class Away:
    def __init__(self, value, anywhere=False):
        self.value, self.anywhere = value, anywhere


def loose(value):
    return Away(value, True)


def call(kernel, outs, args, scratch=(), copies=0, flops=0, cells=0, room=16):
    in_specs, values = [], []
    for arg in args:
        value = arg.value if isinstance(arg, Away) else arg
        if value.dtype == jnp.int32:
            in_specs.append(pl.BlockSpec(memory_space=pltpu.SMEM))
            values.append(value)
            continue
        space = pltpu.HBM if isinstance(arg, Away) else pltpu.VMEM
        if isinstance(arg, Away) and arg.anywhere:
            space = pl.ANY
        in_specs.append(pl.BlockSpec(memory_space=space))
        values.append(pltpu.with_memory_space_constraint(value, space))
    out_specs = [
        pl.BlockSpec(memory_space=pltpu.HBM if isinstance(o, Away) else pltpu.VMEM) for o in outs
    ]
    moved = sum(a.size * a.dtype.itemsize for a in values)
    return pl.pallas_call(
        kernel,
        out_shape=[o.value if isinstance(o, Away) else o for o in outs],
        in_specs=in_specs,
        out_specs=out_specs,
        scratch_shapes=[pltpu.VMEM(shape, dtype) for shape, dtype in scratch]
        + ([pltpu.SemaphoreType.DMA((copies,))] if copies else []),
        compiler_params=pltpu.CompilerParams(vmem_limit_bytes=room * 1024 * 1024),
        cost_estimate=pl.CostEstimate(
            flops=flops, bytes_accessed=moved if flops else 0, transcendentals=cells
        ),
    )(*values)


class Mover:
    def __init__(self, sems):
        self.sems, self.count, self.results = sems, 0, []

    def load(self, source, target):
        copy = pltpu.make_async_copy(source, target, self.sems.at[self.count])
        self.count += 1
        copy.start()
        return copy

    def store(self, source, target):
        self.results.append(self.load(source, target))

    def finish(self):
        for copy in self.results:
            copy.wait()


def wait_all(copies):
    for copy in copies:
        copy.wait()


def load_pieces(move, place, target, own, near, far, ids):
    here, core = place[0], place[1]
    rows = own.shape[0]
    half = rows // 2
    copies = [move.load(own, target.at[pl.ds(pl.multiple_of(here * rows, rows), rows), :])]
    for pieces, side in ((near, core), (far, 1 - core)):
        for ref, steps in zip(pieces, ids):
            for i, step in enumerate(steps):
                if step:
                    spot = jnp.bitwise_xor(here, step) * rows + side * half
                    copies.append(
                        move.load(ref.at[i], target.at[pl.ds(pl.multiple_of(spot, half), half), :])
                    )
    return copies


def loop(count, step, unroll=1):
    def some(i, carry):
        for j in range(unroll):
            step(i * unroll + j)
        return carry

    if unroll == count:
        some(0, 0)
    else:
        lax.fori_loop(0, count // unroll, some, 0)


def part_of(i, size):
    if isinstance(i, int):
        return slice(i * size, (i + 1) * size)
    return pl.ds(pl.multiple_of(i * size, size), size)


def attend(heads, first, qkv, att, exact, lse, keys, chunk=256):
    def one_head(head):
        keys[...] = qkv[part_of(heads + head, HEAD), :].T
        rows = part_of(head, HEAD)

        def one_chunk(i):
            at = part_of(i, chunk)
            scores = mm(keys[...], qkv[rows, part_of(i + first // chunk, chunk)])
            top = jnp.max(scores, axis=0, keepdims=True)
            exponent = jnp.exp(scores - top)
            total = jnp.sum(exponent, axis=0, keepdims=True)
            weighted = mm(qkv[part_of(2 * heads + head, HEAD), :], exponent.astype(BF16))
            weighted = weighted / total
            exact[rows, at] = weighted
            att[rows, at] = weighted.astype(BF16)
            lse[pl.ds(head, 1), at] = top + jnp.log(total)

        loop(att.shape[1] // chunk, one_chunk, att.shape[1] // chunk)

    lse[...] = jnp.zeros_like(lse)
    loop(heads, one_head, heads)


def project_kernel(heads, ids, place, own, *refs):
    count = len(ids)
    near, far, refs = refs[:count], refs[count : 2 * count], refs[2 * count :]
    gain, weight_in, cosine, sine, tok_out, first, qkv, att, exact, lse, tok, weight, keys, sems = refs
    move = Mover(sems)
    local = heads * HEAD
    tokens = tok.shape[0]
    pieces = load_pieces(move, place, tok, own, near, far, ids)
    weight_load = move.load(weight_in, weight)
    wait_all(pieces)
    move.store(tok, tok_out)
    weight_load.wait()
    chunk = 256

    def one_chunk(i):
        at = part_of(i, chunk)
        normed, _ = norm_parts(tok[at, :].astype(F32))
        rounded = (normed * gain[...]).astype(BF16)
        first[at, :] = rounded
        raw = mm(weight[...], rounded, NT)
        cos, sin = cosine[:, at], sine[:, at]
        for part in range(2):
            for head in range(heads):
                base = part * local + head * HEAD
                lower = raw[base : base + HEAD // 2]
                upper = raw[base + HEAD // 2 : base + HEAD]
                turned = jnp.concatenate(
                    [lower * cos - upper * sin, upper * cos + lower * sin], axis=0
                ).astype(BF16)
                if part == 0:
                    turned = turned * jnp.asarray(HEAD ** (-0.5), BF16)
                qkv[base : base + HEAD, at] = turned
        qkv[2 * local :, at] = raw[2 * local :].astype(BF16)

    loop(tokens // chunk, one_chunk, 2)
    attend(heads, 0, qkv, att, exact, lse, keys)
    move.finish()


def queries_kernel(heads, qkv, att, exact, lse, keys):
    attend(heads, qkv.shape[1] - att.shape[1], qkv, att, exact, lse, keys)


def cdf_terms(gate):
    half = 0.5 * (1.0 + lax.erf(gate * (0.5**0.5)))
    slope = half + gate * (jnp.exp(-0.5 * gate * gate) * 0.3989422804014327)
    return half, slope


def mlp_kernel(turn, ids, place, tok_in, *refs):
    count = len(ids)
    if turn == 0:
        cot_own, near, far = refs[0], refs[1 : 1 + count], refs[1 + count : 1 + 2 * count]
        refs = refs[1 + 2 * count :]
        atts, attns, (in_own, in_side, in_rest, mlp_own, rest_far) = refs[:4], refs[4:7], refs[7:12]
        units_here = mlp_own.shape[0]
        attns = [*attns[:2], rest_far.at[units_here:, :], attns[2].at[units_here:, :]]
        gain, cot, attn, w_in, w_mlp, tok_next = refs[12:18]
        refs = refs[18:]
    else:
        cot, atts, (gain, attn, w_in, w_mlp), refs = refs[0], refs[1:5], refs[5:9], refs[9:]
        (mid_before, out_before), refs = refs[:2], refs[2:]
    middle_ref, second_ref, hidden_ref, gate_ref, part_ref, mean_ref, scale_ref = refs[:7]
    mid_ref, out_ref, refs = refs[7], refs[8], refs[9:]
    tokens = middle_ref.shape[0]
    sems = refs[-1]
    move = Mover(sems)
    here, quarter, side = place[0], place[2], place[3]
    local = atts[0].shape[0]
    units = hidden_ref.shape[0]
    begin = turn * tokens
    first_loads = []
    if turn == 0:
        tok, refs = refs[0], refs[1:]
        first_loads.append(move.load(tok_in.at[:tokens, :], tok))
    else:
        tok = tok_in
    att, hidden_v, gate_v = refs[:3]
    for p in range(4):
        spot = pl.ds(pl.multiple_of(jnp.bitwise_xor(quarter, p) * local, local), local)
        first_loads.append(move.load(atts[p], att.at[spot, :]))
        if turn == 0:
            first_loads.append(move.load(attns[p], attn.at[spot, :]))
    in_loads, mlp_loads = [], []
    if turn == 0:
        row = here % 2
        for part in range(2):
            spot = pl.ds(pl.multiple_of((side + 2 * part) * units, units), units)
            rows = in_own.at[part * units : (part + 1) * units, :]
            in_loads.append(move.load(rows, w_in.at[spot, :]))
        for part, source in ((row, in_side), (1 - row, in_rest)):
            spot = pl.ds(pl.multiple_of((1 - side + 2 * part) * units, units), units)
            in_loads.append(move.load(source, w_in.at[spot, :]))
        for source, r in ((mlp_own, side), (rest_far, 1 - side)):
            spot = pl.ds(pl.multiple_of(r * units, units), units)
            mlp_loads.append(move.load(source.at[:units, :], w_mlp.at[spot, :]))
        mlp_loads += load_pieces(move, place, cot, cot_own, near, far, ids)
        mlp_loads.append(move.load(tok_in.at[tokens:, :], tok_next))
    wait_all(first_loads)
    chunk = 512

    def one_chunk(i):
        at = part_of(i, chunk)
        middle = tok[at, :].astype(F32) + mm(att[:, at].T, attn[...])
        middle_ref[at, :] = middle
        normed, scale_ref[at, :], mean_ref[at, :] = norm_stats(middle)
        second = (normed * gain[...]).astype(BF16)
        second_ref[at, :] = second

        if i == 0:
            wait_all(in_loads)

        gate_up = mm(w_in[...], second, NT)
        gate, up = gate_up[: 2 * units], gate_up[2 * units :]
        half, slope = cdf_terms(gate)
        active = gate * half
        hidden_v[:, at] = (active * up).astype(BF16)

        if i == 0:
            wait_all(mlp_loads)

        back = mm(w_mlp[...], cot[part_of(i + begin // chunk, chunk), :], NT)
        grads = jnp.concatenate([slope * up * back, active * back], axis=0).astype(BF16)
        gate_v[:, at] = grads
        part_ref[at, :] = mm(grads.T, w_in[...]).astype(BF16)

    loop(tokens // chunk, one_chunk, tokens // chunk)
    mine = pl.ds(pl.multiple_of(side * units, units), units)
    mine_up = pl.ds(pl.multiple_of(side * units + 2 * units, units), units)
    hidden_ref[...] = hidden_v[mine, :]
    gate_ref[:units, :] = gate_v[mine, :]
    gate_ref[units:, :] = gate_v[mine_up, :]
    rows = out_ref.shape[0]
    spots = tokens // rows
    mid_ref[...] = mid_before[...] if turn else jnp.zeros_like(mid_ref)
    out_ref[...] = out_before[...] if turn else jnp.zeros_like(out_ref)

    @pl.when(here // spots == turn)
    def _():
        own = pl.ds(pl.multiple_of((here - turn * spots) * rows, rows), rows)
        mid_ref[...] = middle_ref[own, :]
        out_ref[...] = mm(hidden_v[:, own].T, w_mlp[...]).astype(BF16)


def two_rows(row):
    high = row.astype(BF16).astype(F32)
    spots = lax.broadcasted_iota(jnp.int32, (16, row.shape[1]), 0)
    rows = jnp.where(spots == 0, high, jnp.where(spots == 1, row - high, 0.0))
    return rows.astype(BF16)


def sum_rows(rows):
    return jnp.sum(rows.astype(F32), axis=0, keepdims=True)


def back_kernel(heads, place, *refs):
    middles, means, scales, refs = refs[:2], refs[2:4], refs[4:6], refs[6:]
    parts, fars, refs = refs[:2], refs[2:4], refs[4:]
    cot, gain, attn, qkv, refs = refs[0], refs[1], refs[2], refs[3], refs[4:]
    exacts, lses, refs = refs[:2], refs[2:4], refs[4:]
    weight, cosine, sine, refs = refs[0], refs[1], refs[2], refs[3:]
    first_in, first_gain, gain_v, branch, own_v, message, qkv_out, refs = *refs[:7], refs[7:]
    grad_v, back_rows, lse, keys, values, key_grad, value_grad, qkv_grad, sems = refs
    move = Mover(sems)
    here = place[0]
    turns = middles[0].shape[0]
    tokens = 2 * turns
    rows = own_v.shape[0]
    local = heads * HEAD
    spots = turns // rows
    gain_v[...] = jnp.zeros_like(gain_v)

    def norm_block(turn, b):
        here_at = pl.ds(pl.multiple_of(b * rows, rows), rows)
        at = pl.ds(pl.multiple_of((b + turn * spots) * rows, rows), rows)
        second = parts[turn][here_at, :].astype(F32) + fars[turn][here_at, :].astype(F32)
        scale = scales[turn][here_at, :]
        normed = (middles[turn][here_at, :] - means[turn][here_at, :]) * scale
        gain_v[...] += jnp.sum(second * normed, axis=0, keepdims=True)
        grad = cot[at, :].astype(F32) + norm_back(second * gain[...], normed, scale)
        branch[at, :] = grad.astype(BF16)

        @pl.when(b + turn * spots == here)
        def _():
            own_v[...] = grad

    for turn in range(2):
        loop(spots, functools.partial(norm_block, turn), 2)
    chunk = 256

    def grad_chunk(i):
        at = part_of(i, chunk)
        back_rows[:, at] = mm(attn[...], branch[at, :], NT).astype(BF16)

    loop(tokens // chunk, grad_chunk, 2)
    for turn in range(2):
        lse[:, turn * turns : (turn + 1) * turns] = lses[turn][...]
    scale = HEAD ** (-0.5)

    def turn_back(grad, cos, sin):
        lower, upper = grad[: HEAD // 2], grad[HEAD // 2 :]
        return jnp.concatenate(
            [lower * cos + upper * sin, upper * cos - lower * sin], axis=0
        ).astype(BF16)

    def one_head(head):
        rows_q, rows_k, rows_v = [part_of(p * heads + head, HEAD) for p in range(3)]
        keys[...] = qkv[rows_k, :].T
        values[...] = qkv[rows_v, :].T
        key_grad[...] = jnp.zeros_like(key_grad)
        value_grad[...] = jnp.zeros_like(value_grad)

        def one_chunk(i):
            at = part_of(i, chunk)
            query = qkv[rows_q, at]
            out_grad = back_rows[rows_q, at]
            chances = jnp.exp(mm(keys[...], query) - lse[pl.ds(head, 1), at])
            chance_grad = mm(values[...], out_grad)
            exact = exacts[i * chunk // turns][rows_q, part_of(i % (turns // chunk), chunk)]
            delta = jnp.sum(out_grad.astype(F32) * exact, axis=0, keepdims=True)
            score_grad = (chances * (chance_grad - delta)).astype(BF16)
            query_grad = mm(qkv[rows_k, :], score_grad) * scale
            key_grad[...] += mm(query, score_grad, NT)
            value_grad[...] += mm(out_grad, chances.astype(BF16), NT)
            grad_v[rows_q, at] = turn_back(query_grad, cosine[:, at], sine[:, at])

        loop(tokens // chunk, one_chunk, tokens // chunk)
        grad_v[rows_k, :] = turn_back(key_grad[...], cosine[...], sine[...])
        grad_v[rows_v, :] = value_grad[...].astype(BF16)

    loop(heads, one_head, heads)
    own = pl.ds(pl.multiple_of(here * rows, rows), rows)
    message[:rows, :] = mm(grad_v[:, own].T, weight[...]).astype(BF16)
    gain_row = jnp.zeros_like(gain_v)
    for part in range(3):
        at = part_of(part, local)
        product = mm(grad_v[at, :], first_in[...])
        qkv_grad[at, :] = product
        move.store(qkv_grad.at[at, :], qkv_out.at[at, :])
        gain_row += jnp.sum(weight[at, :].astype(F32) * product, axis=0, keepdims=True)
    message[rows:, :] = two_rows(gain_row / first_gain[...])
    move.finish()


def sum_kernel(message, far, out):
    rows = out.shape[0] - 16
    out[:rows, :] = (message[:rows, :].astype(F32) + far[:rows, :].astype(F32)).astype(BF16)
    out[rows:, :] = two_rows(sum_rows(message[rows:, :]) + sum_rows(far[rows:, :]))


def last_kernel(mine, far, tokens, gain, middle_grad, tokens_grad, gain_grad):
    rows = tokens.shape[0]
    gain_grad[...] = (sum_rows(mine[rows:, :]) + sum_rows(far[rows:, :]))[0]
    first_grad = mine[:rows, :].astype(F32) + far[:rows, :].astype(F32)
    normed, scale = norm_parts(tokens[...].astype(F32))
    back = norm_back(first_grad * gain[...], normed, scale)
    tokens_grad[...] = (middle_grad[...] + back).astype(BF16)


def products_kernel(gate_a, gate_b, hidden_a, hidden_b, second_a, second_b, cot, *refs):
    in_out, mlp_out, in_grad, mlp_grad, sems = refs
    move = Mover(sems)
    tokens = second_a.shape[0]
    units = hidden_a.shape[0]
    for part in range(2):
        at = part_of(part, units)
        in_grad[at, :] = mm(gate_a[at, :], second_a[...]) + mm(gate_b[at, :], second_b[...])
        move.store(in_grad.at[at, :], in_out.at[at, :])
    mlp_grad[...] = mm(hidden_a[...], cot[:tokens, :]) + mm(hidden_b[...], cot[tokens:, :])
    move.store(mlp_grad, mlp_out)
    move.finish()


def output_kernel(att_a, att_b, branch, middle, part, far, attn_out, output, attn_grad, sems):
    move = Mover(sems)
    tokens = att_a.shape[1]
    attn_grad[...] = mm(att_a[...], branch[:tokens, :]) + mm(att_b[...], branch[tokens:, :])
    move.store(attn_grad, attn_out)
    branch_sum = part[...].astype(F32) + far[...].astype(F32)
    output[...] = (middle[...] + branch_sum).astype(BF16)
    move.finish()


def over_ctx(value, step, spots):
    return lax.ppermute(value, "ctx", [(spot, spot ^ step) for spot in range(spots)])


def swap(value, mask):
    return lax.ppermute(value, "wt", [(spot, spot ^ mask) for spot in range(4)])


def half_of(block, core):
    half = block.shape[0] // 2
    return lax.dynamic_slice_in_dim(block, core * half, half, axis=0)


def gather_tokens(block, core, spots):
    half = half_of(block, core)
    steps = [over_ctx(half, step, spots) for step in range(2, spots, 2)]
    first = jnp.stack([half, steps[0]])
    rest = jnp.stack(steps[1:])
    first_y = over_ctx(first, 1, spots)
    rest_y = over_ctx(rest, 1, spots)
    near = [first, first_y, rest, rest_y]
    later = list(range(4, spots, 2))
    ids = ((0, 2), (1, 3), tuple(later), tuple(step + 1 for step in later))
    return near, [swap(piece, 1) for piece in near], ids, steps


def gather_cotangent(block, core, spots, after, gate):
    near = half_of(block, core)[None]
    ids, step = (0,), 1
    while step < spots:
        if step == 2:
            near, _ = lax.optimization_barrier((near, after))
        near = jnp.concatenate([near, over_ctx(near, step, spots)], axis=0)
        ids += tuple(i + step for i in ids)
        step *= 2
    near, _ = lax.optimization_barrier((near, gate))
    return [near], [swap(near, 1)], (ids,)


def replicated_body(
    spots,
    tokens,
    first_gain,
    qkv_weight,
    attn_weight,
    second_gain,
    in_weight,
    mlp_weight,
    cotangent,
):
    rows, width = tokens.shape
    total_rows = rows * spots
    local = qkv_weight.shape[2]
    heads = local // HEAD
    units = mlp_weight.shape[0]
    here, quarter = lax.axis_index("ctx"), lax.axis_index("wt")
    core, side = quarter % 2, quarter // 2
    place = jnp.stack([here, core, quarter, side]).astype(jnp.int32)
    frequency = rope_base ** (-(jnp.arange(HEAD // 2).astype(F32) * 2.0 / HEAD))
    angles = frequency[:, None] * jnp.arange(total_rows).astype(F32)[None, :]
    cosine, sine = jnp.cos(angles), jnp.sin(angles)
    qkv_t = jnp.transpose(qkv_weight, (1, 2, 0)).reshape(3 * local, width)
    in_t = jnp.transpose(in_weight, (1, 2, 0)).reshape(2 * units, width)

    near, far, ids, steps = gather_tokens(tokens, core, spots)
    attn_core = swap(attn_weight, 1)
    in_part = lax.dynamic_index_in_dim(in_t.reshape(2, units, width), here % 2, 0, keepdims=False)
    in_side = swap(in_part, 2)
    in_rest = over_ctx(in_side, 1, spots)
    rest = jnp.concatenate([mlp_weight, attn_weight], axis=0)
    rest_side = swap(rest, 2)
    rest_both = swap(rest_side, 1)
    half_rows = total_rows // 2
    tall, wide = (total_rows, width), (half_rows, width)
    cells = heads * total_rows * half_rows
    tok_all, first_input, qkv, att_a, exact_a, lse_a = call(
        functools.partial(project_kernel, heads, ids),
        [
            Away(pltpu.HBM(tall, BF16)),
            fast(tall, BF16),
            fast((3 * local, total_rows), BF16),
            fast((local, half_rows), BF16),
            fast((local, half_rows), F32),
            fast((8, half_rows), F32),
        ],
        [
            place,
            Away(tokens),
            *map(Away, near),
            *map(loose, far),
            first_gain[None, :],
            Away(qkv_t),
            cosine,
            sine,
        ],
        scratch=[(tall, BF16), ((3 * local, width), BF16), ((total_rows, HEAD), BF16)],
        copies=20,
    )
    side_a = swap(att_a, 2)
    att_b, exact_b, lse_b = call(
        functools.partial(queries_kernel, heads),
        [
            fast((local, half_rows), BF16),
            fast((local, half_rows), F32),
            fast((8, half_rows), F32),
        ],
        [qkv],
        scratch=[((total_rows, HEAD), BF16)],
    )
    cot_near, cot_far, cot_ids = gather_cotangent(cotangent, core, spots, steps[-1], att_a)
    side_a, _ = lax.optimization_barrier((side_a, att_b))
    atts_a = [att_a, swap(att_a, 1), side_a, swap(side_a, 1)]
    halves = [
        fast(wide, F32),
        fast(wide, BF16),
        fast((units, half_rows), BF16),
        fast((2 * units, half_rows), BF16),
        fast(wide, BF16),
        fast((half_rows, 1), F32),
        fast((half_rows, 1), F32),
        fast((rows, width), F32),
        fast((rows, width), BF16),
    ]
    room = [
        ((4 * local, half_rows), BF16),
        ((2 * units, half_rows), BF16),
        ((4 * units, half_rows), BF16),
    ]
    second_row = second_gain[None, :]
    cot_all, attn_all, in_all, mlp_all, tok_b, *results_a = call(
        functools.partial(mlp_kernel, 0, cot_ids),
        [
            fast(tall, BF16),
            fast((4 * local, width), BF16),
            fast((4 * units, width), BF16),
            fast((2 * units, width), BF16),
            fast(wide, BF16),
            *halves,
        ],
        [
            place,
            *map(Away, [tok_all, cotangent, *cot_near]),
            *map(loose, cot_far),
            att_a,
            loose(atts_a[1]),
            Away(atts_a[2]),
            loose(atts_a[3]),
            *map(Away, [attn_weight, attn_core]),
            loose(rest_both),
            *map(Away, [in_t, in_side]),
            loose(in_rest),
            *map(Away, [mlp_weight, rest_side]),
            second_row,
        ],
        scratch=[(wide, BF16), *room],
        copies=32,
        flops=2 * half_rows * width * (4 * local + 10 * units),
        cells=4 * units * half_rows,
        room=20,
    )
    att_core_b = swap(att_b, 1)
    side_b, _ = lax.optimization_barrier((swap(att_b, 2), cot_all))
    atts_b = [att_b, att_core_b, side_b, swap(side_b, 1)]
    results_b = call(
        functools.partial(mlp_kernel, 1, ()),
        halves,
        [
            place,
            tok_b,
            cot_all,
            att_b,
            *map(loose, atts_b[1:]),
            second_row,
            attn_all,
            in_all,
            mlp_all,
            *results_a[7:],
        ],
        scratch=room,
        copies=8,
        flops=2 * half_rows * width * (4 * local + 10 * units),
        cells=4 * units * half_rows,
        room=20,
    )
    middles, seconds, hiddens, gates, parts, means, scales = zip(results_a[:7], results_b[:7])
    own_middle, out_part = results_b[7:]
    fars = [swap(part, 1) for part in parts]
    out_far = swap(out_part, 1)
    in_grad, mlp_grad = call(
        products_kernel,
        [Away(pltpu.HBM((2 * units, width), F32)), Away(pltpu.HBM((units, width), F32))],
        [*gates, *hiddens, *seconds, cot_all],
        scratch=[((2 * units, width), F32), ((units, width), F32)],
        copies=4,
        flops=6 * total_rows * width * units,
    )
    fars, in_grad, mlp_grad = lax.optimization_barrier((fars, in_grad, mlp_grad))
    second_gain_grad, branch_grad, middle_grad, message, qkv_grad = call(
        functools.partial(back_kernel, heads),
        [
            fast((1, width), F32),
            fast(tall, BF16),
            fast((rows, width), F32),
            fast((rows + 16, width), BF16),
            Away(pltpu.HBM((3 * local, width), F32)),
        ],
        [
            place,
            *middles,
            *means,
            *scales,
            *parts,
            *fars,
            cot_all,
            second_row,
            attn_weight,
            qkv,
            exact_a,
            exact_b,
            lse_a,
            lse_b,
            qkv_t,
            cosine,
            sine,
            first_input,
            first_gain[None, :],
        ],
        scratch=[
            ((3 * local, total_rows), BF16),
            ((local, total_rows), BF16),
            ((8, total_rows), F32),
            ((total_rows, HEAD), BF16),
            ((total_rows, HEAD), BF16),
            ((HEAD, total_rows), F32),
            ((HEAD, total_rows), F32),
            ((3 * local, width), F32),
        ],
        copies=4,
        flops=2 * total_rows * local * (4 * width + 20 * total_rows),
        cells=heads * total_rows * total_rows,
    )
    (mine,) = call(
        sum_kernel, [fast((rows + 16, width), BF16)], [message, swap(message, 1)], flops=rows * width
    )
    far = swap(mine, 2)
    out_far, att_b, _ = lax.optimization_barrier((out_far, att_b, mine))
    attn_grad, output = call(
        output_kernel,
        [Away(pltpu.HBM((local, width), F32)), jax.ShapeDtypeStruct((rows, width), BF16)],
        [att_a, att_b, branch_grad, own_middle, out_part, out_far],
        scratch=[((local, width), F32)],
        copies=2,
        flops=2 * total_rows * width * local,
    )
    tokens_grad, first_gain_grad = call(
        last_kernel,
        [jax.ShapeDtypeStruct((rows, width), BF16), jax.ShapeDtypeStruct((width,), F32)],
        [mine, far, tokens, first_gain[None, :], middle_grad],
        flops=16 * rows * width,
    )
    return (
        output,
        tokens_grad,
        first_gain_grad,
        jnp.transpose(qkv_grad.reshape(3, local, width), (2, 0, 1)),
        attn_grad,
        second_gain_grad[0],
        jnp.transpose(in_grad.reshape(2, units, width), (2, 0, 1)),
        mlp_grad,
    )


def body(sizes, tokens, *rest):
    spots, lanes = sizes["ctx"], sizes["wt"]
    rows = tokens.shape[0]
    small = spots * rows <= REPLICATED_TOKENS and rows % 128 == 0 and (spots * rows) % 256 == 0
    if small and lanes == 4 and spots == 8:
        return replicated_body(spots, tokens, *rest)
    return split_body(tokens, *rest)


def solution(mesh):
    return jax.shard_map(
        functools.partial(body, dict(mesh.shape)),
        mesh=mesh,
        in_specs=(
            P("ctx", None),
            P(),
            P(None, None, "wt"),
            P("wt", None),
            P(),
            P(None, None, "wt"),
            P("wt", None),
            P("ctx", None),
        ),
        out_specs=(
            P("ctx", None),
            P("ctx", None),
            P(),
            P(None, None, "wt"),
            P("wt", None),
            P(),
            P(None, None, "wt"),
            P("wt", None),
        ),
        check_vma=False,
    )
```

```python
import functools

import jax
import jax.numpy as jnp
from jax import lax
from jax.experimental import pallas as pl
from jax.experimental.pallas import tpu as pltpu
from jax.sharding import PartitionSpec as P

HEAD = 64


rope_base = 160000.0
norm_epsilon = 1e-05


def layer_norm(values):
    center = values - jnp.mean(values, axis=-1, keepdims=True)
    return center * lax.rsqrt(jnp.mean(center * center, axis=-1, keepdims=True) + norm_epsilon)


def rotate(values, positions, direction):
    half_width = values.shape[-1] // 2
    frequency = rope_base ** (
        -(jnp.arange(half_width).astype(jnp.float32) * 2.0 / values.shape[-1])
    )
    angles = positions[:, None] * frequency[None, :]
    cosine_part = jnp.cos(angles)[:, None, :]
    sine_part = jnp.sin(angles)[:, None, :]
    lower_half = values[..., :half_width]
    upper_half = values[..., half_width:]
    return jnp.concatenate(
        [
            lower_half * cosine_part - direction * upper_half * sine_part,
            upper_half * cosine_part + direction * lower_half * sine_part,
        ],
        axis=-1,
    )


def block_size_for(shard_rows):
    candidate = shard_rows * max(1, 1024 // shard_rows)
    return candidate


def score_terms(
    query_block, grad_block, logsum_block, delta_block, key_block, value_block, score_scale
):
    scores = (
        jnp.einsum("thd,shd->ths", query_block, key_block, preferred_element_type=jnp.float32)
        * score_scale
    )
    chances = jnp.exp(scores - logsum_block[..., None])
    chance_grad = jnp.einsum(
        "thd,shd->ths", grad_block, value_block, preferred_element_type=jnp.float32
    )
    score_grad = (chances * (chance_grad - delta_block[..., None])).astype(jnp.bfloat16)
    return (chances.astype(jnp.bfloat16), score_grad)


def split_body(
    tokens, first_gain, qkv_weight, attn_weight, second_gain, in_weight, mlp_weight, cotangent
):
    row_count = tokens.shape[0]
    local_width = qkv_weight.shape[2]
    heads_here = local_width // HEAD
    score_scale = HEAD ** (-0.5)
    positions = (lax.axis_index("ctx") * row_count + jnp.arange(row_count, dtype=jnp.int32)).astype(
        jnp.float32
    )
    inputs = tokens.astype(jnp.float32)
    normed_first, first_pull = jax.vjp(layer_norm, inputs)
    first_input = (normed_first * first_gain).astype(jnp.bfloat16)
    projected = jnp.einsum(
        "td,dsh->tsh", first_input, qkv_weight, preferred_element_type=jnp.float32
    )
    shaped = projected.reshape(row_count, 3, heads_here, HEAD)
    query_rows = rotate(shaped[:, 0], positions, 1.0).astype(jnp.bfloat16)
    key_rows = rotate(shaped[:, 1], positions, 1.0).astype(jnp.bfloat16)
    value_rows = shaped[:, 2].astype(jnp.bfloat16)
    key_flat = key_rows.reshape(row_count, local_width)
    value_flat = value_rows.reshape(row_count, local_width)
    start_state = (
        jnp.full((row_count, heads_here), -1e30, jnp.float32),
        jnp.zeros((row_count, heads_here), jnp.float32),
        jnp.zeros((row_count, heads_here, HEAD), jnp.float32),
    )
    key_piece = lax.all_gather(key_flat, "ctx", axis=0, tiled=True)
    value_piece = lax.all_gather(value_flat, "ctx", axis=0, tiled=True)
    piece_rows = key_piece.shape[0]
    block_size = block_size_for(row_count)
    key_blocks = key_piece.reshape(piece_rows // block_size, block_size, heads_here, HEAD)
    value_blocks = value_piece.reshape(piece_rows // block_size, block_size, heads_here, HEAD)

    def forward_visit(state, block_item):
        running_max, running_sum, weighted = state
        key_block, value_block = block_item
        scores = (
            jnp.einsum("thd,shd->ths", query_rows, key_block, preferred_element_type=jnp.float32)
            * score_scale
        )
        new_max = jnp.maximum(running_max, jnp.max(scores, axis=-1))
        factor = jnp.exp(running_max - new_max)
        exponent = jnp.exp(scores - new_max[..., None])
        running_sum = running_sum * factor + jnp.sum(exponent, axis=-1)
        weighted = weighted * factor[..., None] + jnp.einsum(
            "ths,shd->thd",
            exponent.astype(jnp.bfloat16),
            value_block,
            preferred_element_type=jnp.float32,
        )
        return ((new_max, running_sum, weighted), None)

    result = lax.scan(forward_visit, start_state, (key_blocks, value_blocks))
    running_max, running_sum, weighted = result[0]
    attended_exact = weighted / running_sum[..., None]
    logsum = running_max + jnp.log(running_sum)
    attended = attended_exact.astype(jnp.bfloat16).reshape(row_count, local_width)
    branch = lax.psum(
        jnp.dot(attended, attn_weight, preferred_element_type=jnp.float32).astype(jnp.bfloat16),
        "wt",
    ).astype(jnp.float32)
    middle = inputs + branch
    normed_second, second_pull = jax.vjp(layer_norm, middle)
    second_input = (normed_second * second_gain).astype(jnp.bfloat16)
    gate_up = jnp.einsum("td,dsf->tsf", second_input, in_weight, preferred_element_type=jnp.float32)

    def activate(pair):
        return jax.nn.gelu(pair[:, 0], approximate=False) * pair[:, 1]

    hidden_exact, activate_back = jax.vjp(activate, gate_up)
    hidden = hidden_exact.astype(jnp.bfloat16)
    mlp_branch = lax.psum(
        jnp.dot(hidden, mlp_weight, preferred_element_type=jnp.float32).astype(jnp.bfloat16), "wt"
    ).astype(jnp.float32)
    output = (middle + mlp_branch).astype(jnp.bfloat16)
    hidden_grad = jnp.einsum("td,fd->tf", cotangent, mlp_weight, preferred_element_type=jnp.float32)
    mlp_weight_grad = jnp.einsum("tf,td->fd", hidden, cotangent, preferred_element_type=jnp.float32)
    gate_up_grad = activate_back(hidden_grad)[0].astype(jnp.bfloat16)
    second_part = jnp.einsum(
        "tsf,dsf->td", gate_up_grad, in_weight, preferred_element_type=jnp.float32
    )
    in_weight_grad = jnp.einsum(
        "td,tsf->dsf", second_input, gate_up_grad, preferred_element_type=jnp.float32
    )
    second_grad = lax.psum(second_part.astype(jnp.bfloat16), "wt").astype(jnp.float32)
    second_gain_grad = jnp.sum(second_grad * normed_second, axis=0)
    middle_grad = cotangent.astype(jnp.float32) + second_pull(second_grad * second_gain)[0]
    branch_grad = middle_grad.astype(jnp.bfloat16)
    attended_grad = jnp.einsum(
        "td,hd->th", branch_grad, attn_weight, preferred_element_type=jnp.float32
    )
    attn_weight_grad = jnp.einsum(
        "th,td->hd", attended, branch_grad, preferred_element_type=jnp.float32
    )
    grad_rows = attended_grad.astype(jnp.bfloat16).reshape(row_count, heads_here, HEAD)
    row_delta = jnp.sum(grad_rows.astype(jnp.float32) * attended_exact, axis=-1)
    zero_rows = jnp.zeros((row_count, heads_here, HEAD), jnp.float32)
    query_acc = zero_rows
    key_piece = lax.all_gather(key_flat, "ctx", axis=0, tiled=True)
    value_piece = lax.all_gather(value_flat, "ctx", axis=0, tiled=True)
    piece_rows = key_piece.shape[0]
    block_size = block_size_for(row_count)
    key_blocks = key_piece.reshape(piece_rows // block_size, block_size, heads_here, HEAD)
    value_blocks = value_piece.reshape(piece_rows // block_size, block_size, heads_here, HEAD)

    def backward_visit(partial_value, block_item):
        key_block, value_block = block_item
        chance_low, score_grad = score_terms(
            query_rows, grad_rows, logsum, row_delta, key_block, value_block, score_scale
        )
        partial_value = (
            partial_value
            + jnp.einsum("ths,shd->thd", score_grad, key_block, preferred_element_type=jnp.float32)
            * score_scale
        )
        key_term = (
            jnp.einsum("ths,thd->shd", score_grad, query_rows, preferred_element_type=jnp.float32)
            * score_scale
        )
        value_term = jnp.einsum(
            "ths,thd->shd", chance_low, grad_rows, preferred_element_type=jnp.float32
        )
        return (partial_value, (key_term, value_term))

    query_acc, terms = lax.scan(backward_visit, query_acc, (key_blocks, value_blocks))
    key_total = terms[0].reshape(piece_rows, local_width)
    value_total = terms[1].reshape(piece_rows, local_width)
    key_sum, value_sum = (
        lax.psum_scatter(key_total, "ctx", scatter_dimension=0, tiled=True),
        lax.psum_scatter(value_total, "ctx", scatter_dimension=0, tiled=True),
    )
    key_grad = key_sum.reshape(row_count, heads_here, HEAD)
    value_grad = value_sum.reshape(row_count, heads_here, HEAD)
    query_back = rotate(query_acc, positions, -1.0)
    key_back = rotate(key_grad, positions, -1.0)
    projected_grad = (
        jnp.stack([query_back, key_back, value_grad], axis=1)
        .reshape(row_count, 3, local_width)
        .astype(jnp.bfloat16)
    )
    first_part = jnp.einsum(
        "tsh,dsh->td", projected_grad, qkv_weight, preferred_element_type=jnp.float32
    )
    qkv_weight_grad = jnp.einsum(
        "td,tsh->dsh", first_input, projected_grad, preferred_element_type=jnp.float32
    )
    first_grad = lax.psum(first_part.astype(jnp.bfloat16), "wt").astype(jnp.float32)
    first_gain_grad = jnp.sum(first_grad * normed_first, axis=0)
    tokens_grad = (middle_grad + first_pull(first_grad * first_gain)[0]).astype(jnp.bfloat16)
    summed = lax.psum(
        (
            first_gain_grad,
            qkv_weight_grad,
            attn_weight_grad,
            second_gain_grad,
            in_weight_grad,
            mlp_weight_grad,
        ),
        "ctx",
    )
    return (output, tokens_grad, summed[0], summed[1], summed[2], summed[3], summed[4], summed[5])


F32 = jnp.float32
BF16 = jnp.bfloat16
NT = (((1,), (1,)), ((), ()))
TN = (((0,), (0,)), ((), ()))
REPLICATED_TOKENS = 2048


def mm(a, b, dims=(((1,), (0,)), ((), ()))):
    return lax.dot_general(a, b, dims, preferred_element_type=F32)


def norm_parts(values):
    return norm_stats(values)[:2]


def norm_stats(values):
    mean = jnp.mean(values, axis=-1, keepdims=True)
    center = values - mean
    scale = lax.rsqrt(jnp.mean(center * center, axis=-1, keepdims=True) + norm_epsilon)
    return center * scale, scale, mean


def norm_back(grad, normed, scale):
    mean_grad = jnp.mean(grad, axis=-1, keepdims=True)
    mean_both = jnp.mean(grad * normed, axis=-1, keepdims=True)
    return scale * (grad - mean_grad - normed * mean_both)


def fast(shape, dtype):
    return pltpu.VMEM(shape, dtype)


class Away:
    def __init__(self, value, anywhere=False):
        self.value, self.anywhere = value, anywhere


def loose(value):
    return Away(value, True)


def call(kernel, outs, args, scratch=(), copies=0, flops=0, cells=0, room=16):
    in_specs, values = [], []
    for arg in args:
        value = arg.value if isinstance(arg, Away) else arg
        if value.dtype == jnp.int32:
            in_specs.append(pl.BlockSpec(memory_space=pltpu.SMEM))
            values.append(value)
            continue
        space = pltpu.HBM if isinstance(arg, Away) else pltpu.VMEM
        if isinstance(arg, Away) and arg.anywhere:
            space = pl.ANY
        in_specs.append(pl.BlockSpec(memory_space=space))
        values.append(pltpu.with_memory_space_constraint(value, space))
    out_specs = [
        pl.BlockSpec(memory_space=pltpu.HBM if isinstance(o, Away) else pltpu.VMEM) for o in outs
    ]
    moved = sum(a.size * a.dtype.itemsize for a in values)
    return pl.pallas_call(
        kernel,
        out_shape=[o.value if isinstance(o, Away) else o for o in outs],
        in_specs=in_specs,
        out_specs=out_specs,
        scratch_shapes=[pltpu.VMEM(shape, dtype) for shape, dtype in scratch]
        + ([pltpu.SemaphoreType.DMA((copies,))] if copies else []),
        compiler_params=pltpu.CompilerParams(vmem_limit_bytes=room * 1024 * 1024),
        cost_estimate=pl.CostEstimate(
            flops=flops, bytes_accessed=moved if flops else 0, transcendentals=cells
        ),
    )(*values)


class Mover:
    def __init__(self, sems):
        self.sems, self.count, self.results = sems, 0, []

    def load(self, source, target):
        copy = pltpu.make_async_copy(source, target, self.sems.at[self.count])
        self.count += 1
        copy.start()
        return copy

    def store(self, source, target):
        self.results.append(self.load(source, target))

    def finish(self):
        for copy in self.results:
            copy.wait()


def wait_all(copies):
    for copy in copies:
        copy.wait()


def load_pieces(move, place, target, own, near, far, ids):
    here, core = place[0], place[1]
    rows = own.shape[0]
    half = rows // 2
    copies = [move.load(own, target.at[pl.ds(pl.multiple_of(here * rows, rows), rows), :])]
    for pieces, side in ((near, core), (far, 1 - core)):
        for ref, steps in zip(pieces, ids):
            for i, step in enumerate(steps):
                if step:
                    spot = jnp.bitwise_xor(here, step) * rows + side * half
                    copies.append(
                        move.load(ref.at[i], target.at[pl.ds(pl.multiple_of(spot, half), half), :])
                    )
    return copies


def loop(count, step, unroll=1):
    def some(i, carry):
        for j in range(unroll):
            step(i * unroll + j)
        return carry

    if unroll == count:
        some(0, 0)
    else:
        lax.fori_loop(0, count // unroll, some, 0)


def part_of(i, size):
    if isinstance(i, int):
        return slice(i * size, (i + 1) * size)
    return pl.ds(pl.multiple_of(i * size, size), size)


def attend(heads, first, qkv, att, exact, lse, keys, chunk=256):
    def one_head(head):
        keys[...] = qkv[part_of(heads + head, HEAD), :].T
        rows = part_of(head, HEAD)

        def one_chunk(i):
            at = part_of(i, chunk)
            scores = mm(keys[...], qkv[rows, part_of(i + first // chunk, chunk)])
            top = jnp.max(scores, axis=0, keepdims=True)
            exponent = jnp.exp(scores - top)
            total = jnp.sum(exponent, axis=0, keepdims=True)
            weighted = mm(qkv[part_of(2 * heads + head, HEAD), :], exponent.astype(BF16))
            weighted = weighted / total
            exact[rows, at] = weighted
            att[rows, at] = weighted.astype(BF16)
            lse[pl.ds(head, 1), at] = top + jnp.log(total)

        loop(att.shape[1] // chunk, one_chunk, att.shape[1] // chunk)

    lse[...] = jnp.zeros_like(lse)
    loop(heads, one_head, heads)


def project_kernel(heads, ids, place, own, *refs):
    count = len(ids)
    near, far, refs = refs[:count], refs[count : 2 * count], refs[2 * count :]
    gain, weight_in, cosine, sine, tok_out, first, qkv, att, exact, lse, tok, weight, keys, sems = refs
    move = Mover(sems)
    local = heads * HEAD
    tokens = tok.shape[0]
    pieces = load_pieces(move, place, tok, own, near, far, ids)
    weight_load = move.load(weight_in, weight)
    wait_all(pieces)
    move.store(tok, tok_out)
    weight_load.wait()
    chunk = 256

    def one_chunk(i):
        at = part_of(i, chunk)
        normed, _ = norm_parts(tok[at, :].astype(F32))
        rounded = (normed * gain[...]).astype(BF16)
        first[at, :] = rounded
        raw = mm(weight[...], rounded, NT)
        cos, sin = cosine[:, at], sine[:, at]
        for part in range(2):
            for head in range(heads):
                base = part * local + head * HEAD
                lower = raw[base : base + HEAD // 2]
                upper = raw[base + HEAD // 2 : base + HEAD]
                turned = jnp.concatenate(
                    [lower * cos - upper * sin, upper * cos + lower * sin], axis=0
                ).astype(BF16)
                if part == 0:
                    turned = turned * jnp.asarray(HEAD ** (-0.5), BF16)
                qkv[base : base + HEAD, at] = turned
        qkv[2 * local :, at] = raw[2 * local :].astype(BF16)

    loop(tokens // chunk, one_chunk, tokens // chunk)
    attend(heads, 0, qkv, att, exact, lse, keys)
    move.finish()


def queries_kernel(heads, qkv, att, exact, lse, keys):
    attend(heads, qkv.shape[1] - att.shape[1], qkv, att, exact, lse, keys)


def cdf_terms(gate):
    half = 0.5 * (1.0 + lax.erf(gate * (0.5**0.5)))
    slope = half + gate * (jnp.exp(-0.5 * gate * gate) * 0.3989422804014327)
    return half, slope


def mlp_kernel(turn, ids, place, tok_in, *refs):
    count = len(ids)
    if turn == 0:
        cot_own, near, far = refs[0], refs[1 : 1 + count], refs[1 + count : 1 + 2 * count]
        refs = refs[1 + 2 * count :]
        atts, attns, (in_own, in_side, in_rest, mlp_own, rest_far) = refs[:4], refs[4:7], refs[7:12]
        units_here = mlp_own.shape[0]
        attns = [*attns[:2], rest_far.at[units_here:, :], attns[2].at[units_here:, :]]
        gain, cot, attn, w_in, w_mlp, tok_next = refs[12:18]
        refs = refs[18:]
    else:
        cot, atts, (gain, attn, w_in, w_mlp), refs = refs[0], refs[1:5], refs[5:9], refs[9:]
        (mid_before, out_before), refs = refs[:2], refs[2:]
    middle_ref, second_ref, hidden_ref, gate_ref, part_ref, mean_ref, scale_ref = refs[:7]
    mid_ref, out_ref, refs = refs[7], refs[8], refs[9:]
    tokens = middle_ref.shape[0]
    sems = refs[-1]
    move = Mover(sems)
    here, quarter, side = place[0], place[2], place[3]
    local = atts[0].shape[0]
    units = hidden_ref.shape[0]
    begin = turn * tokens
    first_loads = []
    if turn == 0:
        tok, refs = refs[0], refs[1:]
        first_loads.append(move.load(tok_in.at[:tokens, :], tok))
    else:
        tok = tok_in
    att, hidden_v, gate_v = refs[:3]
    for p in range(4):
        spot = pl.ds(pl.multiple_of(jnp.bitwise_xor(quarter, p) * local, local), local)
        first_loads.append(move.load(atts[p], att.at[spot, :]))
        if turn == 0:
            first_loads.append(move.load(attns[p], attn.at[spot, :]))
    in_loads, mlp_loads = [], []
    if turn == 0:
        row = here % 2
        for part in range(2):
            spot = pl.ds(pl.multiple_of((side + 2 * part) * units, units), units)
            rows = in_own.at[part * units : (part + 1) * units, :]
            in_loads.append(move.load(rows, w_in.at[spot, :]))
        for part, source in ((row, in_side), (1 - row, in_rest)):
            spot = pl.ds(pl.multiple_of((1 - side + 2 * part) * units, units), units)
            in_loads.append(move.load(source, w_in.at[spot, :]))
        for source, r in ((mlp_own, side), (rest_far, 1 - side)):
            spot = pl.ds(pl.multiple_of(r * units, units), units)
            mlp_loads.append(move.load(source.at[:units, :], w_mlp.at[spot, :]))
        mlp_loads += load_pieces(move, place, cot, cot_own, near, far, ids)
        mlp_loads.append(move.load(tok_in.at[tokens:, :], tok_next))
    wait_all(first_loads)
    chunk = 512

    def one_chunk(i):
        at = part_of(i, chunk)
        middle = tok[at, :].astype(F32) + mm(att[:, at].T, attn[...])
        middle_ref[at, :] = middle
        normed, scale_ref[at, :], mean_ref[at, :] = norm_stats(middle)
        second = (normed * gain[...]).astype(BF16)
        second_ref[at, :] = second

        if i == 0:
            wait_all(in_loads)

        gate_up = mm(w_in[...], second, NT)
        gate, up = gate_up[: 2 * units], gate_up[2 * units :]
        half, slope = cdf_terms(gate)
        active = gate * half
        hidden_v[:, at] = (active * up).astype(BF16)

        if i == 0:
            wait_all(mlp_loads)

        back = mm(w_mlp[...], cot[part_of(i + begin // chunk, chunk), :], NT)
        grads = jnp.concatenate([slope * up * back, active * back], axis=0).astype(BF16)
        gate_v[:, at] = grads
        part_ref[at, :] = mm(grads.T, w_in[...]).astype(BF16)

    loop(tokens // chunk, one_chunk, tokens // chunk)
    mine = pl.ds(pl.multiple_of(side * units, units), units)
    mine_up = pl.ds(pl.multiple_of(side * units + 2 * units, units), units)
    hidden_ref[...] = hidden_v[mine, :]
    gate_ref[:units, :] = gate_v[mine, :]
    gate_ref[units:, :] = gate_v[mine_up, :]
    rows = out_ref.shape[0]
    spots = tokens // rows
    mid_ref[...] = mid_before[...] if turn else jnp.zeros_like(mid_ref)
    out_ref[...] = out_before[...] if turn else jnp.zeros_like(out_ref)

    @pl.when(here // spots == turn)
    def _():
        own = pl.ds(pl.multiple_of((here - turn * spots) * rows, rows), rows)
        mid_ref[...] = middle_ref[own, :]
        out_ref[...] = mm(hidden_v[:, own].T, w_mlp[...]).astype(BF16)


def two_rows(row):
    high = row.astype(BF16).astype(F32)
    spots = lax.broadcasted_iota(jnp.int32, (16, row.shape[1]), 0)
    rows = jnp.where(spots == 0, high, jnp.where(spots == 1, row - high, 0.0))
    return rows.astype(BF16)


def sum_rows(rows):
    return jnp.sum(rows.astype(F32), axis=0, keepdims=True)


def back_kernel(heads, place, *refs):
    middles, means, scales, refs = refs[:2], refs[2:4], refs[4:6], refs[6:]
    parts, fars, refs = refs[:2], refs[2:4], refs[4:]
    cot, gain, attn, qkv, refs = refs[0], refs[1], refs[2], refs[3], refs[4:]
    exacts, lses, refs = refs[:2], refs[2:4], refs[4:]
    weight, cosine, sine, refs = refs[0], refs[1], refs[2], refs[3:]
    first_in, first_gain, gain_v, branch, own_v, message, qkv_out, refs = *refs[:7], refs[7:]
    grad_v, back_rows, lse, keys, values, key_grad, value_grad, qkv_grad, sems = refs
    move = Mover(sems)
    here = place[0]
    turns = middles[0].shape[0]
    tokens = 2 * turns
    rows = own_v.shape[0]
    local = heads * HEAD
    spots = turns // rows
    gain_v[...] = jnp.zeros_like(gain_v)

    def norm_block(turn, b):
        here_at = pl.ds(pl.multiple_of(b * rows, rows), rows)
        at = pl.ds(pl.multiple_of((b + turn * spots) * rows, rows), rows)
        second = parts[turn][here_at, :].astype(F32) + fars[turn][here_at, :].astype(F32)
        scale = scales[turn][here_at, :]
        normed = (middles[turn][here_at, :] - means[turn][here_at, :]) * scale
        gain_v[...] += jnp.sum(second * normed, axis=0, keepdims=True)
        grad = cot[at, :].astype(F32) + norm_back(second * gain[...], normed, scale)
        branch[at, :] = grad.astype(BF16)

        @pl.when(b + turn * spots == here)
        def _():
            own_v[...] = grad

    for turn in range(2):
        loop(spots, functools.partial(norm_block, turn), spots)
    chunk = 256

    def grad_chunk(i):
        at = part_of(i, chunk)
        back_rows[:, at] = mm(attn[...], branch[at, :], NT).astype(BF16)

    loop(tokens // chunk, grad_chunk, tokens // chunk)
    for turn in range(2):
        lse[:, turn * turns : (turn + 1) * turns] = lses[turn][...]
    scale = HEAD ** (-0.5)

    def turn_back(grad, cos, sin):
        lower, upper = grad[: HEAD // 2], grad[HEAD // 2 :]
        return jnp.concatenate(
            [lower * cos + upper * sin, upper * cos - lower * sin], axis=0
        ).astype(BF16)

    def one_head(head):
        rows_q, rows_k, rows_v = [part_of(p * heads + head, HEAD) for p in range(3)]
        keys[...] = qkv[rows_k, :].T
        values[...] = qkv[rows_v, :].T
        key_grad[...] = jnp.zeros_like(key_grad)
        value_grad[...] = jnp.zeros_like(value_grad)

        def one_chunk(i):
            at = part_of(i, chunk)
            query = qkv[rows_q, at]
            out_grad = back_rows[rows_q, at]
            chances = jnp.exp(mm(keys[...], query) - lse[pl.ds(head, 1), at])
            chance_grad = mm(values[...], out_grad)
            exact = exacts[i * chunk // turns][rows_q, part_of(i % (turns // chunk), chunk)]
            delta = jnp.sum(out_grad.astype(F32) * exact, axis=0, keepdims=True)
            score_grad = (chances * (chance_grad - delta)).astype(BF16)
            query_grad = mm(qkv[rows_k, :], score_grad) * scale
            key_grad[...] += mm(query, score_grad, NT)
            value_grad[...] += mm(out_grad, chances.astype(BF16), NT)
            grad_v[rows_q, at] = turn_back(query_grad, cosine[:, at], sine[:, at])

        loop(tokens // chunk, one_chunk, tokens // chunk)
        grad_v[rows_k, :] = turn_back(key_grad[...], cosine[...], sine[...])
        grad_v[rows_v, :] = value_grad[...].astype(BF16)

    loop(heads, one_head, heads)
    own = pl.ds(pl.multiple_of(here * rows, rows), rows)
    message[:rows, :] = mm(grad_v[:, own].T, weight[...]).astype(BF16)
    gain_row = jnp.zeros_like(gain_v)
    for part in range(3):
        at = part_of(part, local)
        product = mm(grad_v[at, :], first_in[...])
        qkv_grad[at, :] = product
        move.store(qkv_grad.at[at, :], qkv_out.at[at, :])
        gain_row += jnp.sum(weight[at, :].astype(F32) * product, axis=0, keepdims=True)
    message[rows:, :] = two_rows(gain_row / first_gain[...])
    move.finish()


def sum_kernel(message, far, out):
    rows = out.shape[0] - 16
    out[:rows, :] = (message[:rows, :].astype(F32) + far[:rows, :].astype(F32)).astype(BF16)
    out[rows:, :] = two_rows(sum_rows(message[rows:, :]) + sum_rows(far[rows:, :]))


def last_kernel(mine, far, tokens, gain, middle_grad, tokens_grad, gain_grad):
    rows = tokens.shape[0]
    gain_grad[...] = (sum_rows(mine[rows:, :]) + sum_rows(far[rows:, :]))[0]
    first_grad = mine[:rows, :].astype(F32) + far[:rows, :].astype(F32)
    normed, scale = norm_parts(tokens[...].astype(F32))
    back = norm_back(first_grad * gain[...], normed, scale)
    tokens_grad[...] = (middle_grad[...] + back).astype(BF16)


def products_kernel(gate_a, gate_b, hidden_a, hidden_b, second_a, second_b, cot, *refs):
    in_out, mlp_out, in_grad, mlp_grad, sems = refs
    move = Mover(sems)
    tokens = second_a.shape[0]
    units = hidden_a.shape[0]
    for part in range(2):
        at = part_of(part, units)
        in_grad[at, :] = mm(gate_a[at, :], second_a[...]) + mm(gate_b[at, :], second_b[...])
        move.store(in_grad.at[at, :], in_out.at[at, :])
    mlp_grad[...] = mm(hidden_a[...], cot[:tokens, :]) + mm(hidden_b[...], cot[tokens:, :])
    move.store(mlp_grad, mlp_out)
    move.finish()


def output_kernel(att_a, att_b, branch, middle, part, far, attn_out, output, attn_grad, sems):
    move = Mover(sems)
    tokens = att_a.shape[1]
    attn_grad[...] = mm(att_a[...], branch[:tokens, :]) + mm(att_b[...], branch[tokens:, :])
    move.store(attn_grad, attn_out)
    branch_sum = part[...].astype(F32) + far[...].astype(F32)
    output[...] = (middle[...] + branch_sum).astype(BF16)
    move.finish()


def over_ctx(value, step, spots):
    return lax.ppermute(value, "ctx", [(spot, spot ^ step) for spot in range(spots)])


def swap(value, mask):
    return lax.ppermute(value, "wt", [(spot, spot ^ mask) for spot in range(4)])


def half_of(block, core):
    half = block.shape[0] // 2
    return lax.dynamic_slice_in_dim(block, core * half, half, axis=0)


def gather_tokens(block, core, spots):
    half = half_of(block, core)
    steps = [over_ctx(half, step, spots) for step in range(2, spots, 2)]
    first = jnp.stack([half, steps[0]])
    rest = jnp.stack(steps[1:])
    first_y = over_ctx(first, 1, spots)
    rest_y = over_ctx(rest, 1, spots)
    near = [first, first_y, rest, rest_y]
    later = list(range(4, spots, 2))
    ids = ((0, 2), (1, 3), tuple(later), tuple(step + 1 for step in later))
    return near, [swap(piece, 1) for piece in near], ids, steps


def gather_cotangent(block, core, spots, after, gate):
    near = half_of(block, core)[None]
    ids, step = (0,), 1
    while 2 * step < spots:
        if step == 2:
            near, _ = lax.optimization_barrier((near, after))
        near = jnp.concatenate([near, over_ctx(near, step, spots)], axis=0)
        ids += tuple(i + step for i in ids)
        step *= 2
    last, _ = lax.optimization_barrier((over_ctx(near, step, spots), gate))
    return [near, last], [swap(near, 1), swap(last, 1)], (ids, tuple(i + step for i in ids))


def replicated_body(
    spots,
    tokens,
    first_gain,
    qkv_weight,
    attn_weight,
    second_gain,
    in_weight,
    mlp_weight,
    cotangent,
):
    rows, width = tokens.shape
    total_rows = rows * spots
    local = qkv_weight.shape[2]
    heads = local // HEAD
    units = mlp_weight.shape[0]
    here, quarter = lax.axis_index("ctx"), lax.axis_index("wt")
    core, side = quarter % 2, quarter // 2
    place = jnp.stack([here, core, quarter, side]).astype(jnp.int32)
    frequency = rope_base ** (-(jnp.arange(HEAD // 2).astype(F32) * 2.0 / HEAD))
    angles = frequency[:, None] * jnp.arange(total_rows).astype(F32)[None, :]
    cosine, sine = jnp.cos(angles), jnp.sin(angles)
    qkv_t = jnp.transpose(qkv_weight, (1, 2, 0)).reshape(3 * local, width)
    in_t = jnp.transpose(in_weight, (1, 2, 0)).reshape(2 * units, width)

    near, far, ids, steps = gather_tokens(tokens, core, spots)
    attn_core = swap(attn_weight, 1)
    in_part = lax.dynamic_index_in_dim(in_t.reshape(2, units, width), here % 2, 0, keepdims=False)
    in_side = swap(in_part, 2)
    in_rest = over_ctx(in_side, 1, spots)
    rest = jnp.concatenate([mlp_weight, attn_weight], axis=0)
    rest_side = swap(rest, 2)
    rest_both = swap(rest_side, 1)
    half_rows = total_rows // 2
    tall, wide = (total_rows, width), (half_rows, width)
    cells = heads * total_rows * half_rows
    tok_all, first_input, qkv, att_a, exact_a, lse_a = call(
        functools.partial(project_kernel, heads, ids),
        [
            Away(pltpu.HBM(tall, BF16)),
            fast(tall, BF16),
            fast((3 * local, total_rows), BF16),
            fast((local, half_rows), BF16),
            fast((local, half_rows), F32),
            fast((8, half_rows), F32),
        ],
        [
            place,
            Away(tokens),
            *map(Away, near),
            *map(loose, far),
            first_gain[None, :],
            Away(qkv_t),
            cosine,
            sine,
        ],
        scratch=[(tall, BF16), ((3 * local, width), BF16), ((total_rows, HEAD), BF16)],
        copies=20,
    )
    side_a = swap(att_a, 2)
    att_b, exact_b, lse_b = call(
        functools.partial(queries_kernel, heads),
        [
            fast((local, half_rows), BF16),
            fast((local, half_rows), F32),
            fast((8, half_rows), F32),
        ],
        [qkv],
        scratch=[((total_rows, HEAD), BF16)],
    )
    cot_near, cot_far, cot_ids = gather_cotangent(cotangent, core, spots, steps[-1], att_a)
    side_a, _ = lax.optimization_barrier((side_a, att_b))
    atts_a = [att_a, swap(att_a, 1), side_a, swap(side_a, 1)]
    halves = [
        fast(wide, F32),
        fast(wide, BF16),
        fast((units, half_rows), BF16),
        fast((2 * units, half_rows), BF16),
        fast(wide, BF16),
        fast((half_rows, 1), F32),
        fast((half_rows, 1), F32),
        fast((rows, width), F32),
        fast((rows, width), BF16),
    ]
    room = [
        ((4 * local, half_rows), BF16),
        ((2 * units, half_rows), BF16),
        ((4 * units, half_rows), BF16),
    ]
    second_row = second_gain[None, :]
    cot_all, attn_all, in_all, mlp_all, tok_b, *results_a = call(
        functools.partial(mlp_kernel, 0, cot_ids),
        [
            fast(tall, BF16),
            fast((4 * local, width), BF16),
            fast((4 * units, width), BF16),
            fast((2 * units, width), BF16),
            fast(wide, BF16),
            *halves,
        ],
        [
            place,
            *map(Away, [tok_all, cotangent, *cot_near]),
            *map(loose, cot_far),
            att_a,
            loose(atts_a[1]),
            Away(atts_a[2]),
            loose(atts_a[3]),
            *map(Away, [attn_weight, attn_core]),
            loose(rest_both),
            *map(Away, [in_t, in_side]),
            loose(in_rest),
            *map(Away, [mlp_weight, rest_side]),
            second_row,
        ],
        scratch=[(wide, BF16), *room],
        copies=32,
        flops=2 * half_rows * width * (4 * local + 10 * units),
        cells=4 * units * half_rows,
        room=20,
    )
    att_core_b = swap(att_b, 1)
    side_b, _ = lax.optimization_barrier((swap(att_b, 2), cot_all))
    atts_b = [att_b, att_core_b, side_b, swap(side_b, 1)]
    results_b = call(
        functools.partial(mlp_kernel, 1, ()),
        halves,
        [
            place,
            tok_b,
            cot_all,
            att_b,
            *map(loose, atts_b[1:]),
            second_row,
            attn_all,
            in_all,
            mlp_all,
            *results_a[7:],
        ],
        scratch=room,
        copies=8,
        flops=2 * half_rows * width * (4 * local + 10 * units),
        cells=4 * units * half_rows,
        room=20,
    )
    middles, seconds, hiddens, gates, parts, means, scales = zip(results_a[:7], results_b[:7])
    own_middle, out_part = results_b[7:]
    fars = [swap(part, 1) for part in parts]
    out_far = swap(out_part, 1)
    in_grad, mlp_grad = call(
        products_kernel,
        [Away(pltpu.HBM((2 * units, width), F32)), Away(pltpu.HBM((units, width), F32))],
        [*gates, *hiddens, *seconds, cot_all],
        scratch=[((2 * units, width), F32), ((units, width), F32)],
        copies=4,
        flops=6 * total_rows * width * units,
    )
    fars, in_grad, mlp_grad = lax.optimization_barrier((fars, in_grad, mlp_grad))
    second_gain_grad, branch_grad, middle_grad, message, qkv_grad = call(
        functools.partial(back_kernel, heads),
        [
            fast((1, width), F32),
            fast(tall, BF16),
            fast((rows, width), F32),
            fast((rows + 16, width), BF16),
            Away(pltpu.HBM((3 * local, width), F32)),
        ],
        [
            place,
            *middles,
            *means,
            *scales,
            *parts,
            *fars,
            cot_all,
            second_row,
            attn_weight,
            qkv,
            exact_a,
            exact_b,
            lse_a,
            lse_b,
            qkv_t,
            cosine,
            sine,
            first_input,
            first_gain[None, :],
        ],
        scratch=[
            ((3 * local, total_rows), BF16),
            ((local, total_rows), BF16),
            ((8, total_rows), F32),
            ((total_rows, HEAD), BF16),
            ((total_rows, HEAD), BF16),
            ((HEAD, total_rows), F32),
            ((HEAD, total_rows), F32),
            ((3 * local, width), F32),
        ],
        copies=4,
        flops=2 * total_rows * local * (4 * width + 20 * total_rows),
        cells=heads * total_rows * total_rows,
    )
    (mine,) = call(
        sum_kernel, [fast((rows + 16, width), BF16)], [message, swap(message, 1)], flops=rows * width
    )
    far = swap(mine, 2)
    out_far, att_b, _ = lax.optimization_barrier((out_far, att_b, mine))
    attn_grad, output = call(
        output_kernel,
        [Away(pltpu.HBM((local, width), F32)), jax.ShapeDtypeStruct((rows, width), BF16)],
        [att_a, att_b, branch_grad, own_middle, out_part, out_far],
        scratch=[((local, width), F32)],
        copies=2,
        flops=2 * total_rows * width * local,
    )
    tokens_grad, first_gain_grad = call(
        last_kernel,
        [jax.ShapeDtypeStruct((rows, width), BF16), jax.ShapeDtypeStruct((width,), F32)],
        [mine, far, tokens, first_gain[None, :], middle_grad],
        flops=16 * rows * width,
    )
    return (
        output,
        tokens_grad,
        first_gain_grad,
        jnp.transpose(qkv_grad.reshape(3, local, width), (2, 0, 1)),
        attn_grad,
        second_gain_grad[0],
        jnp.transpose(in_grad.reshape(2, units, width), (2, 0, 1)),
        mlp_grad,
    )


def body(sizes, tokens, *rest):
    spots, lanes = sizes["ctx"], sizes["wt"]
    rows = tokens.shape[0]
    small = spots * rows <= REPLICATED_TOKENS and rows % 128 == 0 and (spots * rows) % 256 == 0
    if small and lanes == 4 and spots == 8:
        return replicated_body(spots, tokens, *rest)
    return split_body(tokens, *rest)


def solution(mesh):
    return jax.shard_map(
        functools.partial(body, dict(mesh.shape)),
        mesh=mesh,
        in_specs=(
            P("ctx", None),
            P(),
            P(None, None, "wt"),
            P("wt", None),
            P(),
            P(None, None, "wt"),
            P("wt", None),
            P("ctx", None),
        ),
        out_specs=(
            P("ctx", None),
            P("ctx", None),
            P(),
            P(None, None, "wt"),
            P("wt", None),
            P(),
            P(None, None, "wt"),
            P("wt", None),
        ),
        check_vma=False,
    )
```
